32 devices in a mesh: dp: 16 (over z, y, core), fsdp: 2 (over x).
Axes of the slice: x: 2, y: 2, z: 4, core: 2. Of those that a mesh axis runs over, the one named last changes fastest.
Arguments:
- tokens: bfloat16 [32, 2048, 1024], P('dp', 'fsdp'), may hold values from -6 to 6
- lengths: int32 [32], P('dp'), may hold values from 256 to 2048, as said below
- w_query: bfloat16 [1024, 1024], P(('dp', 'fsdp')), may hold values from -0.1875 to 0.1875
- w_key: bfloat16 [1024, 1024], P(('dp', 'fsdp')), may hold values from -0.1875 to 0.1875
- w_value: bfloat16 [1024, 1024], P(('dp', 'fsdp')), may hold values from -0.1875 to 0.1875
- w_gate: bfloat16 [1024, 1024], P(('dp', 'fsdp')), may hold values from -0.1875 to 0.1875
- out_gain: bfloat16 [1024], P(('dp', 'fsdp')), may hold values from 0.5 to 1.5
- w_out: bfloat16 [1024, 1024], P(('dp', 'fsdp')), may hold values from -0.1875 to 0.1875
- w_one: bfloat16 [1024, 2816], P(('dp', 'fsdp')), may hold values from -0.1875 to 0.1875
- w_two: bfloat16 [1024, 2816], P(('dp', 'fsdp')), may hold values from -0.1875 to 0.1875
- w_three: bfloat16 [2816, 1024], P(('dp', 'fsdp')), may hold values from -0.109375 to 0.109375
- cotangent: bfloat16 [32, 2048, 1024], P('dp', 'fsdp'), may hold values from -6 to 6
Outputs:
- layer_out: bfloat16 [32, 2048, 1024], P('dp', 'fsdp')
- input_grad: float32 [32, 2048, 1024], P('dp', 'fsdp')
- grad_query: float32 [1024, 1024], P(('dp', 'fsdp'))
- grad_key: float32 [1024, 1024], P(('dp', 'fsdp'))
- grad_value: float32 [1024, 1024], P(('dp', 'fsdp'))
- grad_gate: float32 [1024, 1024], P(('dp', 'fsdp'))
- grad_gain: float32 [1024], P(('dp', 'fsdp'))
- grad_out: float32 [1024, 1024], P(('dp', 'fsdp'))
- grad_one: float32 [1024, 2816], P(('dp', 'fsdp'))
- grad_two: float32 [1024, 2816], P(('dp', 'fsdp'))
- grad_three: float32 [2816, 1024], P(('dp', 'fsdp'))
The draws below stay inside these ranges and needn't reach their ends.
Inputs may be any that keep to these rules, and one draw needn't show every extreme that they name: `lengths`: the 2 sequences on one index of dp include at least one whose length is the full 2048.
All inputs are finite; a program needn't handle non-finite values.
Results may differ from the reference program's by a relative error of at most 0.014.
Values may be sent and summed in bfloat16 or wider, within the bound.
A program may use at most 232 MiB of HBM per device.

```python
import jax
import jax.numpy as jnp
from jax import lax

D = 1024
FF = 2816
HD = 64
H = 16
BLOCK = 256
LEN = 2048
SEQS = 2
SEQ_TOTAL = 32


def draw_lengths(key, part):
    key = jax.random.fold_in(key, 11)
    pick_key, length_key = jax.random.split(key)
    groups = SEQ_TOTAL // SEQS
    drawn_rows = jax.random.randint(length_key, (groups, SEQS), LEN // 8, LEN + 1, dtype=jnp.int32)
    chosen = jax.random.randint(pick_key, (groups, 1), 0, SEQS, dtype=jnp.int32)
    slot_ids = jnp.arange(SEQS, dtype=jnp.int32)[None, :]
    return jnp.where(slot_ids == chosen, LEN, drawn_rows).astype(jnp.int32).reshape(SEQ_TOTAL)


def steps_of(own_key, extent, shards, low, largest):
    def one(axis_at, blocks):
        draws = jax.random.uniform(jax.random.fold_in(jax.random.fold_in(own_key, 6), axis_at), (blocks,), jnp.float32, low / len(shards), largest / len(shards))
        return jnp.repeat(jnp.exp(draws), extent[axis_at] // blocks).reshape((-1,) + (1,) * (len(extent) - axis_at - 1))

    level = one(*shards[0])
    for cut in shards[1:]:
        level = level * one(*cut)
    return level


def scatter_about(rng, shape, spread, reach, shards=(), kind=jnp.bfloat16):
    array = jax.random.normal(rng, shape, jnp.float32) * spread
    if len(shards) > 0:
        array = steps_of(rng, shape, shards, -0.22, 0.18) * array
    return jnp.clip(array, min=-reach, max=reach).astype(kind)


def setup_inputs(seed: int = 0) -> dict:
    key_list = jax.random.split(jax.random.key(seed), 13)
    tokens = scatter_about(key_list[0], (SEQ_TOTAL, LEN, D), 1.0, 6.0, ((0, 16), (1, 2)))
    lengths = draw_lengths(jax.random.fold_in(key_list[12], 71), 0)
    w_query = scatter_about(key_list[2], (D, D), D ** -0.5, 0.1875, ((0, 32),))
    w_key = scatter_about(key_list[3], (D, D), D ** -0.5, 0.1875, ((0, 32),))
    w_value = scatter_about(key_list[4], (D, D), D ** -0.5, 0.1875, ((0, 32),))
    w_gate = scatter_about(key_list[5], (D, D), D ** -0.5, 0.1875, ((0, 32),))
    out_gain = jnp.clip(1.0 + 0.1 * jax.random.normal(key_list[6], (D,), jnp.float32), 0.5, 1.5).astype(jnp.bfloat16)
    w_out = scatter_about(key_list[7], (D, D), D ** -0.5, 0.1875, ((0, 32),))
    w_one = scatter_about(key_list[8], (D, FF), D ** -0.5, 0.1875, ((0, 32),))
    w_two = scatter_about(key_list[9], (D, FF), D ** -0.5, 0.1875, ((0, 32),))
    w_three = scatter_about(key_list[10], (FF, D), FF ** -0.5, 0.109375, ((0, 32),))
    cotangent = scatter_about(key_list[11], (SEQ_TOTAL, LEN, D), 1.0, 6.0, ((0, 16), (1, 2)))
    return dict(tokens=tokens, lengths=lengths, w_query=w_query, w_key=w_key, w_value=w_value, w_gate=w_gate, out_gain=out_gain, w_out=w_out, w_one=w_one, w_two=w_two, w_three=w_three, cotangent=cotangent)


norm_epsilon = 1e-06
highest = lax.Precision.HIGHEST

@jax.custom_vjp
def low(v):
    return lax.optimization_barrier(v.astype(jnp.bfloat16)).astype(jnp.float32)

@jax.custom_vjp
def low_back(v):
    return v

def low_keep(v):
    return (low(v), None)

def low_pass(kept, grad):
    return (grad,)

def back_keep(v):
    return (v, None)

def back_low(kept, grad):
    return (low(grad),)
low.defvjp(low_keep, low_pass)
low_back.defvjp(back_keep, back_low)

def simple_norm(values):
    return values * lax.rsqrt(lax.optimization_barrier(jnp.mean(values * values, axis=-1, keepdims=True)) + norm_epsilon)

def product(left_side, right_side):
    return jnp.dot(left_side, right_side, precision=highest)

def causal_linear(query_rows, key_rows, value_rows):
    blocks = LEN // BLOCK
    query_tiles = query_rows.reshape(blocks, BLOCK, H, HD)
    key_tiles = key_rows.reshape(blocks, BLOCK, H, HD)
    value_tiles = value_rows.reshape(blocks, BLOCK, H, HD)
    causal_mask = (jnp.arange(BLOCK)[:, None] >= jnp.arange(BLOCK)[None, :]).astype(jnp.float32)
    scores = jnp.einsum('nihd,njhd->nhij', query_tiles, key_tiles, precision=highest) * causal_mask
    scores = low(low_back(scores))
    within = jnp.einsum('nhij,njhe->nihe', scores, value_tiles, precision=highest)
    block_states = low_back(jnp.einsum('njhd,njhe->nhde', key_tiles, value_tiles, precision=highest))
    leading = jnp.zeros_like(block_states[:1])
    prefix = low(jnp.concatenate([leading, jnp.cumsum(block_states[:-1], axis=0)], axis=0))
    carried = jnp.einsum('nihd,nhde->nihe', query_tiles, prefix, precision=highest)
    return (within + carried).reshape(LEN, D)

def block_forward(inputs, valid_rows, w_query, w_key, w_value, w_gate, out_gain, w_out, w_one, w_two, w_three):
    normed_one = low(simple_norm(inputs))
    query_rows = low(jax.nn.silu(low_back(product(normed_one, w_query))))
    key_rows = low(jax.nn.silu(low_back(product(normed_one, w_key))))
    value_rows = low(low_back(product(normed_one, w_value)))
    gate_rows = jax.nn.sigmoid(low_back(product(normed_one, w_gate)))
    attended = low_back(causal_linear(query_rows, key_rows, value_rows))
    mixed = low(simple_norm(attended) * out_gain * gate_rows)
    residual = inputs + low_back(product(mixed, w_out))
    normed_two = low(simple_norm(residual))
    up_one = low_back(product(normed_two, w_one))
    up_two = low_back(product(normed_two, w_two))
    glu_rows = low(up_one * up_two)
    return valid_rows * (residual + product(glu_rows, w_three))

def reference(tokens, lengths, w_query, w_key, w_value, w_gate, out_gain, w_out, w_one, w_two, w_three, cotangent):
    weights = tuple((weight.astype(jnp.float32) for weight in (w_query, w_key, w_value, w_gate, out_gain, w_out, w_one, w_two, w_three)))
    positions = jnp.arange(LEN, dtype=jnp.int32)

    def one_sequence(totals, element):
        sequence, length, upstream = element
        valid_rows = (positions < length).astype(jnp.float32)[:, None]

        def forward(inputs, *params):
            return block_forward(inputs, valid_rows, *params)
        result, pullback = jax.vjp(forward, sequence.astype(jnp.float32), *weights)
        gradients = pullback(upstream.astype(jnp.float32))
        totals = tuple((total + gradient for total, gradient in zip(totals, gradients[1:])))
        return (totals, (result.astype(jnp.bfloat16), gradients[0]))
    zero_sums = tuple((jnp.zeros_like(weight) for weight in weights))
    totals, (layer_out, input_grad) = lax.scan(one_sequence, zero_sums, (tokens, lengths, cotangent))
    return (layer_out, input_grad, totals[0], totals[1], totals[2], totals[3], totals[4], totals[5], totals[6], totals[7], totals[8])
```

```python
import jax
import jax.numpy as jnp
from jax import lax
from jax.experimental import pallas as pl
from jax.experimental.pallas import tpu as pltpu
from jax.sharding import PartitionSpec as P

HD = 64
H = 16
BLOCK = 256


GROUP = 256
HEADS = GROUP // HD
LOW = jnp.bfloat16
WIDE = jnp.float32

norm_epsilon = 1e-06


def bit_steps():
    steps = []
    for axis in ("dp", "fsdp"):
        size = lax.axis_size(axis)
        bit = 0
        while (1 << bit) < size:
            steps.append((axis, bit, [(i, i ^ (1 << bit)) for i in range(size)]))
            bit += 1
    return steps


def stream_orders():
    steps = bit_steps()
    dp = [s for s in steps if s[0] == "dp"]
    fs = [s for s in steps if s[0] == "fsdp"]
    core, rest = dp[0], fs[:1] + dp[1:3]
    tail = dp[3:] + fs[1:]
    return [[core] + rest[k:] + rest[:k] + tail for k in range(3)]


def own_bit(step):
    axis, bit, _ = step
    return lax.rem(lax.div(lax.axis_index(axis), 1 << bit), 2)


def bit_dims():
    steps = bit_steps()
    dp = sorted([s for s in steps if s[0] == "dp"], key=lambda s: -s[1])
    fs = sorted([s for s in steps if s[0] == "fsdp"], key=lambda s: -s[1])
    return [(s[0], s[1]) for s in dp + fs]


def gather_rows(shard, order):
    dims = bit_dims()
    held = []
    data = shard
    for step in reversed(order):
        axis, bit, perm = step
        other = lax.ppermute(data, axis, perm)
        mine = own_bit(step) == 0
        place = sum(1 for d in held if dims.index(d) < dims.index((axis, bit)))
        held.append((axis, bit))
        data = jnp.stack(
            [jnp.where(mine, data, other), jnp.where(mine, other, data)], axis=place
        )
    return data.reshape((-1,) + shard.shape[1:])


def scatter_rows(full, order):
    dims = bit_dims()
    rows = full.shape[0] >> len(dims)
    data = full.astype(jnp.bfloat16).reshape((2,) * len(dims) + (rows,) + full.shape[1:])
    left = list(dims)
    for at, step in enumerate(order):
        axis, bit, perm = step
        place = left.index((axis, bit))
        left.pop(place)
        own = own_bit(step)
        send = lax.dynamic_index_in_dim(data, 1 - own, place, keepdims=False)
        keep = lax.dynamic_index_in_dim(data, own, place, keepdims=False)
        come = lax.ppermute(send, axis, perm)
        data = keep.astype(jnp.float32) + come.astype(jnp.float32)
        if at < len(order) - 1:
            data = data.astype(jnp.bfloat16)
    return data


def shift_sum(x, axis, reverse):
    size = lax.axis_size(axis)
    total = jnp.zeros_like(x)
    low = x.astype(jnp.bfloat16)
    for s in range(1, size):
        pairs = [(i + s, i) if reverse else (i, i + s) for i in range(size - s)]
        total = total + lax.ppermute(low, axis, pairs).astype(x.dtype)
    return total


def dot_nn(a, b):
    return jnp.dot(a, b, preferred_element_type=WIDE)


def dot_nt(a, b):
    return lax.dot_general(a, b, (((1,), (1,)), ((), ())), preferred_element_type=WIDE)


def dot_tn(a, b):
    return lax.dot_general(a, b, (((0,), (0,)), ((), ())), preferred_element_type=WIDE)


def rms_scale(values):
    return lax.rsqrt(jnp.mean(values * values, axis=-1, keepdims=True) + norm_epsilon)


def norm_back(values, scale, upstream):
    inner_mean = jnp.mean(upstream * values, axis=-1, keepdims=True)
    return scale * (upstream - values * (scale * scale) * inner_mean)


def silu_slope(pre_rows):
    logistic = jax.nn.sigmoid(pre_rows)
    return logistic * (1.0 + pre_rows * (1.0 - logistic))


def head_square():
    row = lax.broadcasted_iota(jnp.int32, (GROUP, GROUP), 0) // HD
    col = lax.broadcasted_iota(jnp.int32, (GROUP, GROUP), 1) // HD
    return (row == col).astype(WIDE)


def head_rows():
    lane = lax.broadcasted_iota(jnp.int32, (1, GROUP), 1) // HD
    return [(lane == h).astype(WIDE).astype(LOW) for h in range(HEADS)]


def split_heads(rows, marks):
    return jnp.concatenate([rows * mark for mark in marks], axis=0)


def pack_state(square, same):
    return jnp.sum((square * same).reshape(HEADS, HD, GROUP), axis=0)


def open_state(packed, same):
    return (jnp.concatenate([packed] * HEADS, axis=0) * same).astype(LOW)


def causal_masks():
    i = lax.broadcasted_iota(jnp.int32, (BLOCK, HEADS * BLOCK), 0)
    j = lax.broadcasted_iota(jnp.int32, (BLOCK, HEADS * BLOCK), 1) % BLOCK
    return (i >= j).astype(WIDE), (j >= i).astype(WIDE)


def groups(width):
    return [slice(g * GROUP, (g + 1) * GROUP) for g in range(width // GROUP)]


def key_value_kernel(per_seq, tok, w_key, w_value, normed, pre_key, keys, values, totals):
    x = tok[...].astype(WIDE)
    rows = (x * rms_scale(x)).astype(LOW)
    normed[...] = rows
    pre = dot_nn(rows, w_key[...])
    pre_key[...] = pre.astype(LOW)
    k = jax.nn.silu(pre).astype(LOW)
    keys[...] = k
    v = dot_nn(rows, w_value[...]).astype(LOW)
    values[...] = v

    @pl.when(pl.program_id(0) % per_seq == 0)
    def _():
        totals[...] = jnp.zeros_like(totals)

    same = head_square()
    for g in groups(k.shape[1]):
        totals[0, :, g] += pack_state(dot_tn(k[:, g], v[:, g]), same)


def query_gate_kernel(normed, w_query, w_gate, pre_query, queries, pre_gate):
    rows = normed[...]
    pre = dot_nn(rows, w_query[...])
    pre_query[...] = pre.astype(LOW)
    queries[...] = jax.nn.silu(pre).astype(LOW)
    pre_gate[...] = dot_nn(rows, w_gate[...]).astype(LOW)


def attend_kernel(
    per_seq, queries, keys, values, pre_gate, tok, incoming, gain, w_out,
    attended, mixed, residual, prefix, carry,
):
    @pl.when(pl.program_id(0) % per_seq == 0)
    def _():
        carry[...] = incoming[0]

    same, marks = head_square(), head_rows()
    causal, _ = causal_masks()
    prefix[0] = carry[...].astype(LOW)
    for g in groups(queries.shape[1]):
        q, k, v = queries[:, g], keys[:, g], values[:, g]
        scores = (dot_nt(q, split_heads(k, marks)) * causal).astype(LOW)
        out = dot_nn(scores, split_heads(v, marks))
        out += dot_nn(q, open_state(carry[:, g], same))
        attended[:, g] = out.astype(LOW)
        carry[:, g] += pack_state(dot_tn(k, v), same)
    rows = attended[...].astype(WIDE)
    gate = jax.nn.sigmoid(pre_gate[...].astype(WIDE))
    rows = (rows * rms_scale(rows) * gain[...] * gate).astype(LOW)
    mixed[...] = rows
    residual[...] = tok[...].astype(WIDE) + dot_nn(rows, w_out[...])


def feed_kernel(
    per_seq, limits, residual, cotangent, w_one, w_two, w_three, w_out, gain, pre_gate,
    attended, queries,
    layer_out, normed, glu, grad_one, grad_two, upstream_low, grad_residual, grad_low,
    grad_gate, grad_attended, totals, grad_gain,
):
    step = pl.program_id(0)
    row_count = residual.shape[0]
    spot = lax.broadcasted_iota(jnp.int32, (row_count, 1), 0) + (step % per_seq) * row_count
    valid = (spot < limits[step // per_seq]).astype(WIDE)
    res = residual[...]
    scale = rms_scale(res)
    rows = (res * scale).astype(LOW)
    normed[...] = rows
    upstream = cotangent[...].astype(WIDE) * valid
    up_low = upstream.astype(LOW)
    upstream_low[...] = up_low
    for c in groups(w_one.shape[1]):
        one = dot_nn(rows, w_one[:, c])
        two = dot_nn(rows, w_two[:, c])
        back = dot_nt(up_low, w_three[c, :])
        glu[:, c] = (one * two).astype(LOW)
        grad_one[:, c] = (back * two).astype(LOW)
        grad_two[:, c] = (back * one).astype(LOW)
    layer_out[...] = (valid * (res + dot_nn(glu[...], w_three[...]))).astype(LOW)
    back = dot_nt(grad_one[...], w_one[...]) + dot_nt(grad_two[...], w_two[...])
    grad = upstream + norm_back(res, scale, back)
    grad_residual[...] = grad
    grad = grad.astype(LOW)
    grad_low[...] = grad
    grad = dot_nt(grad, w_out[...])
    gate = jax.nn.sigmoid(pre_gate[...].astype(WIDE))
    att = attended[...].astype(WIDE)
    scale = rms_scale(att)
    hat = att * scale
    gated = grad * gate

    @pl.when(step == 0)
    def _():
        grad_gain[...] = jnp.zeros_like(grad_gain)

    grad_gain[...] += jnp.sum(gated * hat, axis=0, keepdims=True)
    gated = gated * gain[...]
    grad_gate[...] = (gated * hat * (1.0 - gate)).astype(LOW)
    grad_att = norm_back(att, scale, gated).astype(LOW)
    grad_attended[...] = grad_att

    @pl.when(step % per_seq == 0)
    def _():
        totals[...] = jnp.zeros_like(totals)

    same = head_square()
    for g in groups(grad_att.shape[1]):
        totals[0, :, g] += pack_state(dot_tn(queries[:, g], grad_att[:, g]), same)


def attend_back_kernel(
    per_seq, queries, keys, values, grad_attended, pre_query, pre_key, prefix, incoming,
    grad_query, grad_key, grad_value, carry,
):
    @pl.when(pl.program_id(0) % per_seq == 0)
    def _():
        carry[...] = incoming[0]

    same, marks = head_square(), head_rows()
    causal, causal_t = causal_masks()
    for g in groups(queries.shape[1]):
        q, k, v, ga = queries[:, g], keys[:, g], values[:, g], grad_attended[:, g]
        qs, ks, vs, gs = (split_heads(rows, marks) for rows in (q, k, v, ga))
        state = open_state(prefix[0, :, g].astype(WIDE), same)
        grad_state = open_state(carry[:, g], same)
        grad_scores = (dot_nt(ga, vs) * causal).astype(LOW)
        gq = dot_nn(grad_scores, ks) + dot_nt(ga, state)
        grad_scores = (dot_nt(v, gs) * causal_t).astype(LOW)
        gk = dot_nn(grad_scores, qs) + dot_nt(v, grad_state)
        scores = (dot_nt(k, qs) * causal_t).astype(LOW)
        gv = dot_nn(scores, gs) + dot_nn(k, grad_state)
        grad_query[:, g] = (gq * silu_slope(pre_query[:, g].astype(WIDE))).astype(LOW)
        grad_key[:, g] = (gk * silu_slope(pre_key[:, g].astype(WIDE))).astype(LOW)
        grad_value[:, g] = gv.astype(LOW)
        carry[:, g] += pack_state(dot_tn(q, ga), same)


def input_kernel(
    grad_query, grad_key, grad_value, grad_gate, w_query, w_key, w_value, w_gate, tok,
    grad_residual, input_grad,
):
    grad = dot_nt(grad_query[...], w_query[...]) + dot_nt(grad_key[...], w_key[...])
    grad += dot_nt(grad_value[...], w_value[...]) + dot_nt(grad_gate[...], w_gate[...])
    x = tok[...].astype(WIDE)
    input_grad[...] = grad_residual[...] + norm_back(x, rms_scale(x), grad)


def rows_spec(width, block=BLOCK, order=lambda i: i):
    return pl.BlockSpec((block, width), lambda i: (order(i), 0))


def whole_spec(array):
    rank = array.ndim
    return pl.BlockSpec(array.shape, lambda i: (0,) * rank, pipeline_mode=pl.Buffered(1))


def call(kernel, steps, operands, results, scratch=(), flops=0, limit=56):
    moved = sum(a.size * a.dtype.itemsize for a, _ in operands)
    return pl.pallas_call(
        kernel,
        grid=(steps,),
        in_specs=[spec for _, spec in operands],
        out_specs=[spec for _, _, spec in results],
        out_shape=[jax.ShapeDtypeStruct(shape, dtype) for shape, dtype, _ in results],
        scratch_shapes=list(scratch),
        compiler_params=pltpu.CompilerParams(
            dimension_semantics=("arbitrary",), vmem_limit_bytes=limit << 20
        ),
        cost_estimate=pl.CostEstimate(flops=flops, bytes_accessed=moved, transcendentals=0),
    )(*[a for a, _ in operands])


def shards(
    tokens,
    lengths,
    w_query,
    w_key,
    w_value,
    w_gate,
    out_gain,
    w_out,
    w_one,
    w_two,
    w_three,
    cotangent,
):
    seq_count, local_length, width = tokens.shape
    row_count = seq_count * local_length
    hidden = w_one.shape[1]
    steps = row_count // BLOCK
    per_seq = local_length // BLOCK
    orders = stream_orders()
    tok = tokens.reshape(row_count, width)
    cot = cotangent.reshape(row_count, width)
    limits = lengths - lax.axis_index("fsdp") * local_length
    full_key = gather_rows(w_key, orders[0])
    full_value = gather_rows(w_value, orders[1])
    full_query = gather_rows(w_query, orders[2])
    full_gate = gather_rows(w_gate, orders[0])
    gain_columns = jnp.broadcast_to(out_gain[:, None], (out_gain.shape[0], 128))
    full_out = gather_rows(jnp.concatenate([w_out, gain_columns], axis=1), orders[1])
    full_one = gather_rows(w_one, orders[2])
    full_two = gather_rows(w_two, orders[0])
    full_three = gather_rows(w_three, orders[1])
    gain = full_out[:, width].astype(WIDE)[None, :]
    full_out = full_out[:, :width]

    rows = rows_spec(width)
    narrow = ((row_count, width), LOW, rows)
    wide = ((row_count, width), WIDE, rows)
    big = ((row_count, hidden), LOW, rows_spec(hidden))
    state_spec = pl.BlockSpec((1, HD, width), lambda i: (i // per_seq, 0, 0))
    state = ((seq_count, HD, width), WIDE, state_spec)
    square = 2 * row_count * width * width

    normed_low, pre_key, keys, values, totals = call(
        lambda *refs: key_value_kernel(per_seq, *refs),
        steps,
        [(tok, rows), (full_key, whole_spec(full_key)), (full_value, whole_spec(full_value))],
        [narrow, narrow, narrow, narrow, state],
        flops=2 * square,
    )
    incoming = shift_sum(totals, "fsdp", False)
    pre_query, queries, pre_gate = call(
        query_gate_kernel,
        steps,
        [(normed_low, rows), (full_query, whole_spec(full_query)), (full_gate, whole_spec(full_gate))],
        [narrow, narrow, narrow],
        flops=2 * square,
    )
    prefix_spec = pl.BlockSpec((1, HD, width), lambda i: (i, 0, 0))
    attended, mixed, residual, prefix = call(
        lambda *refs: attend_kernel(per_seq, *refs),
        steps,
        [(queries, rows), (keys, rows), (values, rows), (pre_gate, rows), (tok, rows),
         (incoming, state_spec), (gain, whole_spec(gain)), (full_out, whole_spec(full_out))],
        [narrow, narrow, wide, ((steps, HD, width), LOW, prefix_spec)],
        scratch=[pltpu.VMEM((HD, width), WIDE)],
        flops=3 * square,
    )
    (
        layer_out, normed_two, glu, grad_up_one, grad_up_two, upstream_low, grad_residual,
        grad_residual_low, grad_pre_gate, grad_attended, grad_totals, grad_gain_term,
    ) = call(
        lambda *refs: feed_kernel(per_seq, *refs),
        steps,
        [(limits, pl.BlockSpec(memory_space=pltpu.SMEM)), (residual, rows), (cot, rows),
         (full_one, whole_spec(full_one)), (full_two, whole_spec(full_two)),
         (full_three, whole_spec(full_three)), (full_out, whole_spec(full_out)),
         (gain, whole_spec(gain)), (pre_gate, rows), (attended, rows), (queries, rows)],
        [narrow, narrow, big, big, big, narrow, wide, narrow, narrow, narrow, state,
         ((1, width), WIDE, pl.BlockSpec((1, width), lambda i: (0, 0)))],
        flops=12 * row_count * width * hidden + square,
    )
    outgoing = shift_sum(grad_totals, "fsdp", True)
    grad_one = scatter_rows(dot_tn(normed_two, grad_up_one), orders[1])
    grad_two = scatter_rows(dot_tn(normed_two, grad_up_two), orders[2])
    grad_three = scatter_rows(dot_tn(glu, upstream_low), orders[0])
    gain_term = jnp.broadcast_to(grad_gain_term.reshape(width, 1), (width, 128))
    grad_out = scatter_rows(
        jnp.concatenate([dot_tn(mixed, grad_residual_low), gain_term], axis=1), orders[1]
    )
    grad_gain = grad_out[:, width]
    grad_out = grad_out[:, :width]

    def back(i):
        return (i // per_seq) * per_seq + per_seq - 1 - i % per_seq

    back_rows = rows_spec(width, order=back)
    back_narrow = ((row_count, width), LOW, back_rows)
    grad_pre_query, grad_pre_key, grad_pre_value = call(
        lambda *refs: attend_back_kernel(per_seq, *refs),
        steps,
        [(queries, back_rows), (keys, back_rows), (values, back_rows),
         (grad_attended, back_rows), (pre_query, back_rows), (pre_key, back_rows),
         (prefix, pl.BlockSpec((1, HD, width), lambda i: (back(i), 0, 0))),
         (outgoing, state_spec)],
        [back_narrow, back_narrow, back_narrow],
        scratch=[pltpu.VMEM((HD, width), WIDE)],
        flops=6 * square,
    )
    grad_query = scatter_rows(dot_tn(normed_low, grad_pre_query), orders[0])
    grad_key = scatter_rows(dot_tn(normed_low, grad_pre_key), orders[1])
    grad_value = scatter_rows(dot_tn(normed_low, grad_pre_value), orders[2])
    grad_gate = scatter_rows(dot_tn(normed_low, grad_pre_gate), orders[0])
    (input_grad,) = call(
        input_kernel,
        steps,
        [(grad_pre_query, rows), (grad_pre_key, rows), (grad_pre_value, rows),
         (grad_pre_gate, rows), (full_query, whole_spec(full_query)),
         (full_key, whole_spec(full_key)), (full_value, whole_spec(full_value)),
         (full_gate, whole_spec(full_gate)), (tok, rows), (grad_residual, rows)],
        [wide],
        flops=4 * square,
    )
    return (
        layer_out.reshape(tokens.shape),
        input_grad.reshape(tokens.shape),
        grad_query,
        grad_key,
        grad_value,
        grad_gate,
        grad_gain,
        grad_out,
        grad_one,
        grad_two,
        grad_three,
    )


def solution(mesh):
    in_specs = (
        P("dp", "fsdp", None),
        P("dp"),
        P(("dp", "fsdp"), None),
        P(("dp", "fsdp"), None),
        P(("dp", "fsdp"), None),
        P(("dp", "fsdp"), None),
        P(("dp", "fsdp")),
        P(("dp", "fsdp"), None),
        P(("dp", "fsdp"), None),
        P(("dp", "fsdp"), None),
        P(("dp", "fsdp"), None),
        P("dp", "fsdp", None),
    )
    out_specs = (
        P("dp", "fsdp", None),
        P("dp", "fsdp", None),
        P(("dp", "fsdp"), None),
        P(("dp", "fsdp"), None),
        P(("dp", "fsdp"), None),
        P(("dp", "fsdp"), None),
        P(("dp", "fsdp")),
        P(("dp", "fsdp"), None),
        P(("dp", "fsdp"), None),
        P(("dp", "fsdp"), None),
        P(("dp", "fsdp"), None),
    )
    return jax.shard_map(shards, mesh=mesh, in_specs=in_specs, out_specs=out_specs, check_vma=False)
```

```python
import functools

import jax
import jax.numpy as jnp
from jax import lax
from jax.experimental import pallas as pl
from jax.experimental.pallas import tpu as pltpu
from jax.sharding import PartitionSpec as P

HD = 64
H = 16
BLOCK = 256


GROUP = 256
HEADS = GROUP // HD
LOW = jnp.bfloat16
WIDE = jnp.float32

norm_epsilon = 1e-06


def bit_steps():
    steps = []
    for axis in ("dp", "fsdp"):
        size = lax.axis_size(axis)
        bit = 0
        while (1 << bit) < size:
            steps.append((axis, bit, [(i, i ^ (1 << bit)) for i in range(size)]))
            bit += 1
    return steps


def stream_orders():
    steps = bit_steps()
    dp = [s for s in steps if s[0] == "dp"]
    fs = [s for s in steps if s[0] == "fsdp"]
    core, rest = dp[0], fs[:1] + dp[1:3]
    tail = dp[3:] + fs[1:]
    return [[core] + rest[k:] + rest[:k] + tail for k in range(3)]


def own_bit(step):
    axis, bit, _ = step
    return lax.rem(lax.div(lax.axis_index(axis), 1 << bit), 2)


def bit_dims():
    steps = bit_steps()
    dp = sorted([s for s in steps if s[0] == "dp"], key=lambda s: -s[1])
    fs = sorted([s for s in steps if s[0] == "fsdp"], key=lambda s: -s[1])
    return [(s[0], s[1]) for s in dp + fs]


def gather_rows(shard, order):
    dims = bit_dims()
    held = []
    data = shard
    for step in reversed(order):
        axis, bit, perm = step
        other = lax.ppermute(data, axis, perm)
        mine = own_bit(step) == 0
        place = sum(1 for d in held if dims.index(d) < dims.index((axis, bit)))
        held.append((axis, bit))
        data = jnp.stack(
            [jnp.where(mine, data, other), jnp.where(mine, other, data)], axis=place
        )
    return data.reshape((-1,) + shard.shape[1:])


def scatter_rows(full, order):
    dims = bit_dims()
    rows = full.shape[0] >> len(dims)
    data = full.astype(jnp.bfloat16).reshape((2,) * len(dims) + (rows,) + full.shape[1:])
    left = list(dims)
    for at, step in enumerate(order):
        axis, bit, perm = step
        place = left.index((axis, bit))
        left.pop(place)
        own = own_bit(step)
        send = lax.dynamic_index_in_dim(data, 1 - own, place, keepdims=False)
        keep = lax.dynamic_index_in_dim(data, own, place, keepdims=False)
        come = lax.ppermute(send, axis, perm)
        data = keep.astype(jnp.float32) + come.astype(jnp.float32)
        if at < len(order) - 1:
            data = data.astype(jnp.bfloat16)
    return data


def shift_sum(x, axis, reverse):
    size = lax.axis_size(axis)
    total = jnp.zeros_like(x)
    low = x.astype(jnp.bfloat16)
    for s in range(1, size):
        pairs = [(i + s, i) if reverse else (i, i + s) for i in range(size - s)]
        total = total + lax.ppermute(low, axis, pairs).astype(x.dtype)
    return total


def dot_nn(a, b):
    return jnp.dot(a, b, preferred_element_type=WIDE)


def dot_nt(a, b):
    return lax.dot_general(a, b, (((1,), (1,)), ((), ())), preferred_element_type=WIDE)


def dot_tn(a, b):
    return lax.dot_general(a, b, (((0,), (0,)), ((), ())), preferred_element_type=WIDE)


def rms_scale(values):
    return lax.rsqrt(jnp.mean(values * values, axis=-1, keepdims=True) + norm_epsilon)


def norm_back(values, scale, upstream):
    inner_mean = jnp.mean(upstream * values, axis=-1, keepdims=True)
    return scale * (upstream - values * (scale * scale) * inner_mean)


def silu_slope(pre_rows):
    logistic = jax.nn.sigmoid(pre_rows)
    return logistic * (1.0 + pre_rows * (1.0 - logistic))


def head_square():
    row = lax.broadcasted_iota(jnp.int32, (GROUP, GROUP), 0) // HD
    col = lax.broadcasted_iota(jnp.int32, (GROUP, GROUP), 1) // HD
    return (row == col).astype(WIDE)


def head_rows():
    lane = lax.broadcasted_iota(jnp.int32, (1, GROUP), 1) // HD
    return [(lane == h).astype(WIDE).astype(LOW) for h in range(HEADS)]


def split_heads(rows, marks):
    return jnp.concatenate([rows * mark for mark in marks], axis=0)


def pack_state(square, same):
    return jnp.sum((square * same).reshape(HEADS, HD, GROUP), axis=0)


def open_state(packed, same):
    return (jnp.concatenate([packed] * HEADS, axis=0) * same).astype(LOW)


def causal_masks():
    i = lax.broadcasted_iota(jnp.int32, (BLOCK, HEADS * BLOCK), 0)
    j = lax.broadcasted_iota(jnp.int32, (BLOCK, HEADS * BLOCK), 1) % BLOCK
    return (i >= j).astype(WIDE), (j >= i).astype(WIDE)


def groups(width):
    return [slice(g * GROUP, (g + 1) * GROUP) for g in range(width // GROUP)]


def key_value_kernel(per_seq, tok, w_key, w_value, normed, pre_key, keys, values, totals):
    x = tok[...].astype(WIDE)
    rows = (x * rms_scale(x)).astype(LOW)
    normed[...] = rows
    pre = dot_nn(rows, w_key[...])
    pre_key[...] = pre.astype(LOW)
    k = jax.nn.silu(pre).astype(LOW)
    keys[...] = k
    v = dot_nn(rows, w_value[...]).astype(LOW)
    values[...] = v

    @pl.when(pl.program_id(0) % per_seq == 0)
    def _():
        totals[...] = jnp.zeros_like(totals)

    same = head_square()
    for g in groups(k.shape[1]):
        totals[0, :, g] += pack_state(dot_tn(k[:, g], v[:, g]), same)


def query_gate_kernel(normed, w_query, w_gate, pre_query, queries, pre_gate):
    rows = normed[...]
    pre = dot_nn(rows, w_query[...])
    pre_query[...] = pre.astype(LOW)
    queries[...] = jax.nn.silu(pre).astype(LOW)
    pre_gate[...] = dot_nn(rows, w_gate[...]).astype(LOW)


def attend_kernel(
    per_seq, queries, keys, values, pre_gate, tok, incoming, gain, w_out,
    attended, mixed, residual, prefix, carry,
):
    @pl.when(pl.program_id(0) % per_seq == 0)
    def _():
        carry[...] = incoming[0]

    same, marks = head_square(), head_rows()
    causal, _ = causal_masks()
    prefix[0] = carry[...].astype(LOW)
    for g in groups(queries.shape[1]):
        q, k, v = queries[:, g], keys[:, g], values[:, g]
        scores = (dot_nt(q, split_heads(k, marks)) * causal).astype(LOW)
        out = dot_nn(scores, split_heads(v, marks))
        out += dot_nn(q, open_state(carry[:, g], same))
        attended[:, g] = out.astype(LOW)
        carry[:, g] += pack_state(dot_tn(k, v), same)
    rows = attended[...].astype(WIDE)
    gate = jax.nn.sigmoid(pre_gate[...].astype(WIDE))
    rows = (rows * rms_scale(rows) * gain[...] * gate).astype(LOW)
    mixed[...] = rows
    residual[...] = tok[...].astype(WIDE) + dot_nn(rows, w_out[...])


def feed_kernel(
    per_seq, limits, residual, cotangent, w_one, w_two, w_three, w_out, gain, pre_gate,
    attended, queries,
    layer_out, normed, glu, grad_one, grad_two, upstream_low, grad_residual, grad_low,
    grad_gate, grad_attended, totals, grad_gain,
):
    step = pl.program_id(0)
    row_count = residual.shape[0]
    spot = lax.broadcasted_iota(jnp.int32, (row_count, 1), 0) + (step % per_seq) * row_count
    valid = (spot < limits[step // per_seq]).astype(WIDE)
    res = residual[...]
    scale = rms_scale(res)
    rows = (res * scale).astype(LOW)
    normed[...] = rows
    upstream = cotangent[...].astype(WIDE) * valid
    up_low = upstream.astype(LOW)
    upstream_low[...] = up_low
    for c in groups(w_one.shape[1]):
        one = dot_nn(rows, w_one[:, c])
        two = dot_nn(rows, w_two[:, c])
        back = dot_nt(up_low, w_three[c, :])
        glu[:, c] = (one * two).astype(LOW)
        grad_one[:, c] = (back * two).astype(LOW)
        grad_two[:, c] = (back * one).astype(LOW)
    layer_out[...] = (valid * (res + dot_nn(glu[...], w_three[...]))).astype(LOW)
    back = dot_nt(grad_one[...], w_one[...]) + dot_nt(grad_two[...], w_two[...])
    grad = upstream + norm_back(res, scale, back)
    grad_residual[...] = grad
    grad = grad.astype(LOW)
    grad_low[...] = grad
    grad = dot_nt(grad, w_out[...])
    gate = jax.nn.sigmoid(pre_gate[...].astype(WIDE))
    att = attended[...].astype(WIDE)
    scale = rms_scale(att)
    hat = att * scale
    gated = grad * gate

    @pl.when(step == 0)
    def _():
        grad_gain[...] = jnp.zeros_like(grad_gain)

    grad_gain[...] += jnp.sum(gated * hat, axis=0, keepdims=True)
    gated = gated * gain[...]
    grad_gate[...] = (gated * hat * (1.0 - gate)).astype(LOW)
    grad_att = norm_back(att, scale, gated).astype(LOW)
    grad_attended[...] = grad_att

    @pl.when(step % per_seq == 0)
    def _():
        totals[...] = jnp.zeros_like(totals)

    same = head_square()
    for g in groups(grad_att.shape[1]):
        totals[0, :, g] += pack_state(dot_tn(queries[:, g], grad_att[:, g]), same)


def attend_back_kernel(
    per_seq, queries, keys, values, grad_attended, pre_query, pre_key, prefix, incoming,
    grad_query, grad_key, grad_value, carry,
):
    @pl.when(pl.program_id(0) % per_seq == 0)
    def _():
        carry[...] = incoming[0]

    same, marks = head_square(), head_rows()
    causal, causal_t = causal_masks()
    for g in groups(queries.shape[1]):
        q, k, v, ga = queries[:, g], keys[:, g], values[:, g], grad_attended[:, g]
        qs, ks, vs, gs = (split_heads(rows, marks) for rows in (q, k, v, ga))
        state = open_state(prefix[0, :, g].astype(WIDE), same)
        grad_state = open_state(carry[:, g], same)
        grad_scores = (dot_nt(ga, vs) * causal).astype(LOW)
        gq = dot_nn(grad_scores, ks) + dot_nt(ga, state)
        grad_scores = (dot_nt(v, gs) * causal_t).astype(LOW)
        gk = dot_nn(grad_scores, qs) + dot_nt(v, grad_state)
        scores = (dot_nt(k, qs) * causal_t).astype(LOW)
        gv = dot_nn(scores, gs) + dot_nn(k, grad_state)
        grad_query[:, g] = (gq * silu_slope(pre_query[:, g].astype(WIDE))).astype(LOW)
        grad_key[:, g] = (gk * silu_slope(pre_key[:, g].astype(WIDE))).astype(LOW)
        grad_value[:, g] = gv.astype(LOW)
        carry[:, g] += pack_state(dot_tn(q, ga), same)


def input_kernel(
    grad_query, grad_key, grad_value, grad_gate, w_query, w_key, w_value, w_gate, tok,
    grad_residual, input_grad,
):
    grad = dot_nt(grad_query[...], w_query[...]) + dot_nt(grad_key[...], w_key[...])
    grad += dot_nt(grad_value[...], w_value[...]) + dot_nt(grad_gate[...], w_gate[...])
    x = tok[...].astype(WIDE)
    input_grad[...] = grad_residual[...] + norm_back(x, rms_scale(x), grad)


def rows_spec(width, block=BLOCK, order=lambda i: i):
    return pl.BlockSpec((block, width), lambda i: (order(i), 0))


def whole_spec(array):
    rank = array.ndim
    return pl.BlockSpec(array.shape, lambda i: (0,) * rank, pipeline_mode=pl.Buffered(1))


def call(kernel, steps, operands, results, scratch=(), flops=0, limit=56):
    moved = sum(a.size * a.dtype.itemsize for a, _ in operands)
    return pl.pallas_call(
        kernel,
        grid=(steps,),
        in_specs=[spec for _, spec in operands],
        out_specs=[spec for _, _, spec in results],
        out_shape=[jax.ShapeDtypeStruct(shape, dtype) for shape, dtype, _ in results],
        scratch_shapes=list(scratch),
        compiler_params=pltpu.CompilerParams(
            dimension_semantics=("arbitrary",), vmem_limit_bytes=limit << 20
        ),
        cost_estimate=pl.CostEstimate(flops=flops, bytes_accessed=moved, transcendentals=0),
    )(*[a for a, _ in operands])


def index_bits():
    bits = []
    for axis in ("dp", "fsdp"):
        count = lax.axis_size(axis).bit_length() - 1
        bits += [(axis, bit) for bit in reversed(range(count))]
    return bits


def bit_value(bit):
    axis, at = bit
    return lax.rem(lax.div(lax.axis_index(axis), 1 << at), 2)


def flip_device(bit):
    axis, at = bit
    return {axis: lax.axis_index(axis) + (1 - 2 * bit_value(bit)) * (1 << at)}


def greet(bits):
    barrier = pltpu.get_barrier_semaphore()
    for bit in bits:
        pl.semaphore_signal(
            barrier, inc=1, device_id=flip_device(bit), device_id_type=pl.DeviceIdType.MESH
        )
    pl.semaphore_wait(barrier, len(bits))


class Sems:
    def __init__(self, send, recv):
        self.send, self.recv, self.used = send, recv, 0

    def copy(self, src, dst, bit):
        at = self.used
        self.used += 1
        return pltpu.make_async_remote_copy(
            src_ref=src,
            dst_ref=dst,
            send_sem=self.send.at[at],
            recv_sem=self.recv.at[at],
            device_id=flip_device(bit),
            device_id_type=pl.DeviceIdType.MESH,
        )


class Gather:
    def __init__(self, buf, bits, order, sems, columns=slice(None)):
        self.stages = []
        held = []

        def cube(flipped=None):
            index = []
            for bit in bits:
                if bit == flipped:
                    index.append(1 - bit_value(bit))
                else:
                    index.append(slice(None) if bit in held else bit_value(bit))
            return buf.at[tuple(index) + (slice(None), columns)]

        for bit in order[:-1]:
            ref = cube()
            copies = [sems.copy(ref, ref, bit)]
            if bit == order[-2]:
                copies.append(sems.copy(ref, ref, order[-1]))
                far = cube(flipped=bit)
            self.stages.append(copies)
            held.append(bit)
        self.stages.append([sems.copy(far, far, order[-1])])

    def start(self, stage):
        for copy in self.stages[stage]:
            copy.start()

    def arrive(self, stage):
        self.stages[stage][0].wait_recv()

    def advance(self, stage):
        self.arrive(stage - 1)
        self.start(stage)

    def finish(self):
        self.stages[-2][1].wait_recv()
        self.stages[-1][0].wait_recv()

    def drain(self):
        for copies in self.stages:
            for copy in copies:
                copy.wait_send()


FORWARD_COPIES = 80


def forward_kernel(
    steps, per_seq, bits, waves, feed_orders, three_order,
    tok, s_key, s_value, s_query, s_gate, s_out, s_gain, s_one, s_two, s_three,
    normed, pre_key, keys, values, pre_query, queries, pre_gate, attended, mixed, residual,
    prefix, gain_row, full_attn, full_one, full_two, full_three,
    held, all_keys, all_values, all_normed, totals, state_out, state_in, carry,
    three_in, three_slab, send, recv, local,
):
    step = pl.program_id(0)
    width = tok.shape[1]
    last = bits[-1]
    sems = Sems(send, recv)
    attn = [
        [Gather(held, bits, order, sems, columns) for order, columns in wave] for wave in waves
    ]
    feed = [
        Gather(buf, bits, order, sems)
        for buf, order in zip((full_one, full_two), feed_orders)
    ]
    three = Gather(full_three, bits[:-1], three_order, sems)
    swap_three = sems.copy(s_three, three_in, last)
    swap_state = sems.copy(state_out, state_in, last)
    own = tuple(bit_value(bit) for bit in bits)
    keep_attn = pltpu.make_async_copy(held, full_attn, local.at[3])

    def feed_advance(stage):
        for piece in feed:
            piece.advance(stage)
        if stage > 1:
            three.advance(stage - 1)

    @pl.when(step == 0)
    def _():
        place = [
            pltpu.make_async_copy(s_one, full_one.at[own], local.at[0]),
            pltpu.make_async_copy(s_two, full_two.at[own], local.at[1]),
        ]
        for copy in place:
            copy.start()
        for n, shard in enumerate((s_key, s_value, s_query, s_gate, s_out)):
            held[own + (slice(None), slice(n * width, (n + 1) * width))] = shard[...]
        held[own + (slice(None), slice(5 * width, 5 * width + 128))] = s_gain[...]
        greet(bits)
        for wave in attn:
            for piece in wave:
                piece.start(0)
        swap_three.start()
        for copy in place:
            copy.wait()
        for stage in range(1, len(bits)):
            for wave in attn:
                for piece in wave:
                    piece.advance(stage)
            if stage == 1:
                for piece in feed:
                    piece.start(0)
                swap_three.wait_recv()
                mine = (own[-1] == 0).astype(WIDE)
                low, high = s_three[...], three_in[...]
                three_slab[...] = jnp.concatenate(
                    [mine * low + (1 - mine) * high, mine * high + (1 - mine) * low], axis=0
                ).astype(LOW)
                lay = pltpu.make_async_copy(three_slab, full_three.at[own[:-1]], local.at[2])
                lay.start()
                lay.wait()
                three.start(0)
        for piece in attn[0]:
            piece.finish()
        feed_advance(1)

    @pl.when(step == 3)
    def _():
        feed_advance(2)

    @pl.when(step == steps)
    def _():
        for wave in attn[1:]:
            for piece in wave:
                piece.finish()
        keep_attn.start()
        column = held[..., 5 * width : 5 * width + 128].reshape(width, 128)
        gain_row[...] = column.astype(WIDE).T[:1]

    @pl.when(step == steps + 1)
    def _():
        feed_advance(3)

    def weight(n):
        return held[..., n * width : (n + 1) * width].reshape(width, width)

    same = head_square()

    @pl.when(step < steps)
    def _():
        x = tok[...].astype(WIDE)
        rows = (x * rms_scale(x)).astype(LOW)
        normed[...] = rows
        here = pl.ds(pl.multiple_of(step * BLOCK, BLOCK), BLOCK)
        all_normed[here, :] = rows
        pre = dot_nn(rows, weight(0))
        pre_key[...] = pre.astype(LOW)
        k = jax.nn.silu(pre).astype(LOW)
        keys[...] = k
        all_keys[here, :] = k
        v = dot_nn(rows, weight(1)).astype(LOW)
        values[...] = v
        all_values[here, :] = v
        seq = step // per_seq

        @pl.when(step % per_seq == 0)
        def _():
            totals[seq] = jnp.zeros((HD, width), WIDE)

        for g in groups(width):
            totals[seq, :, g] += pack_state(dot_tn(k[:, g], v[:, g]), same)

    @pl.when(step == steps - 1)
    def _():
        state_out[...] = totals[...].astype(LOW)
        swap_state.start()

    @pl.when(step >= steps)
    def _():
        at = step - steps
        here = pl.ds(pl.multiple_of(at * BLOCK, BLOCK), BLOCK)
        rows = all_normed[here, :]
        pre = dot_nn(rows, weight(2))
        pre_query[...] = pre.astype(LOW)
        queries[...] = jax.nn.silu(pre).astype(LOW)
        gate = dot_nn(rows, weight(3))
        pre_gate[...] = gate.astype(LOW)

        @pl.when(at == 0)
        def _():
            swap_state.wait_recv()

        @pl.when(at % per_seq == 0)
        def _():
            carry[...] = state_in[at // per_seq].astype(WIDE) * own[-1].astype(WIDE)

        marks = head_rows()
        causal, _ = causal_masks()
        prefix[0] = carry[...].astype(LOW)
        for g in groups(width):
            q, k, v = queries[:, g], all_keys[here, g], all_values[here, g]
            scores = (dot_nt(q, split_heads(k, marks)) * causal).astype(LOW)
            out = dot_nn(scores, split_heads(v, marks))
            out += dot_nn(q, open_state(carry[:, g], same))
            attended[:, g] = out.astype(LOW)
            carry[:, g] += pack_state(dot_tn(k, v), same)
        rows = attended[...].astype(WIDE)
        rows = rows * rms_scale(rows) * gain_row[...] * jax.nn.sigmoid(gate)
        rows = rows.astype(LOW)
        mixed[...] = rows
        residual[...] = tok[...].astype(WIDE) + dot_nn(rows, weight(4))

    @pl.when(step == 2 * steps - 1)
    def _():
        feed_advance(4)
        for piece in feed:
            piece.finish()
        three.finish()
        for piece in [p for wave in attn for p in wave] + feed + [three]:
            piece.drain()
        swap_three.wait_send()
        swap_state.wait_send()
        keep_attn.wait()


def tile_cuts(start, tiles):
    cuts = []
    for count in tiles:
        cuts.append(slice(start, start + 128 * count))
        start += 128 * count
    return cuts


def forward(tok, seq_count, shards_attn, gain_columns, s_one, s_two, s_three):
    row_count, width = tok.shape
    hidden = s_one.shape[1]
    steps = row_count // BLOCK
    per_seq = steps // seq_count
    bits = index_bits()
    orders = [[(s[0], s[1]) for s in reversed(order)] for order in stream_orders()]
    third = width // 128
    waves = [
        list(zip(orders, tile_cuts(0, (6, 5, 5)))),
        list(zip(orders, tile_cuts(2 * width, (5, 6, 5)))),
        list(zip(orders, tile_cuts(4 * width, (3, 3, 3)))),
    ]
    feed_orders = [orders[0], orders[2]]
    three_order = [bit for bit in orders[1] if bit != bits[-1]]
    lead = (2,) * len(bits)
    slab = s_one.shape[0]
    deep = s_three.shape[0]
    in_rows = pl.BlockSpec((BLOCK, width), lambda i: (i % steps, 0))
    first = pl.BlockSpec((BLOCK, width), lambda i: (jnp.minimum(i, steps - 1), 0))
    second = pl.BlockSpec((BLOCK, width), lambda i: (jnp.maximum(i - steps, 0), 0))
    any_spec = pl.BlockSpec(memory_space=pl.ANY)
    vmem = pl.BlockSpec(memory_space=pltpu.VMEM)
    rows_low = jax.ShapeDtypeStruct((row_count, width), LOW)

    def shape(*dims, dtype=LOW):
        return jax.ShapeDtypeStruct(dims, dtype)

    kernel = functools.partial(
        forward_kernel, steps, per_seq, bits, waves, feed_orders, three_order
    )
    out = pl.pallas_call(
        kernel,
        grid=(2 * steps,),
        in_specs=[in_rows] + [vmem] * 6 + [any_spec] * 2 + [vmem],
        out_specs=[first] * 4 + [second] * 6
        + [
            pl.BlockSpec((1, HD, width), lambda i: (jnp.maximum(i - steps, 0), 0, 0)),
            pl.BlockSpec((1, width), lambda i: (0, 0)),
        ]
        + [any_spec] * 4,
        out_shape=[rows_low] * 9
        + [
            shape(row_count, width, dtype=WIDE),
            shape(steps, HD, width),
            shape(1, width, dtype=WIDE),
            shape(*lead, slab, 5 * width + 128),
            shape(*lead, slab, hidden),
            shape(*lead, slab, hidden),
            shape(*lead[:-1], 2 * deep, width),
        ],
        scratch_shapes=[
            pltpu.VMEM(lead + (slab, 5 * width + 128), LOW),
            pltpu.VMEM((row_count, width), LOW),
            pltpu.VMEM((row_count, width), LOW),
            pltpu.VMEM((row_count, width), LOW),
            pltpu.VMEM((seq_count, HD, width), WIDE),
            pltpu.VMEM((seq_count, HD, width), LOW),
            pltpu.VMEM((seq_count, HD, width), LOW),
            pltpu.VMEM((HD, width), WIDE),
            pltpu.VMEM((deep, width), WIDE),
            pltpu.VMEM((2 * deep, width), LOW),
            pltpu.SemaphoreType.DMA((FORWARD_COPIES,)),
            pltpu.SemaphoreType.DMA((FORWARD_COPIES,)),
            pltpu.SemaphoreType.DMA((4,)),
        ],
        compiler_params=pltpu.CompilerParams(
            dimension_semantics=("arbitrary",),
            vmem_limit_bytes=58 << 20,
            collective_id=1,
            has_side_effects=True,
        ),
        cost_estimate=pl.CostEstimate(
            flops=16 * row_count * width * width, bytes_accessed=64 << 20, transcendentals=0
        ),
    )(tok, *shards_attn, gain_columns, s_one, s_two, s_three.astype(WIDE))
    return list(out[:12]) + [
        out[12].reshape(-1, 5 * width + 128),
        out[13].reshape(-1, hidden),
        out[14].reshape(-1, hidden),
        out[15].reshape(-1, width),
    ]


def plain_shards(
    tokens,
    lengths,
    w_query,
    w_key,
    w_value,
    w_gate,
    out_gain,
    w_out,
    w_one,
    w_two,
    w_three,
    cotangent,
):
    seq_count, local_length, width = tokens.shape
    row_count = seq_count * local_length
    hidden = w_one.shape[1]
    steps = row_count // BLOCK
    per_seq = local_length // BLOCK
    orders = stream_orders()
    tok = tokens.reshape(row_count, width)
    cot = cotangent.reshape(row_count, width)
    limits = lengths - lax.axis_index("fsdp") * local_length
    full_key = gather_rows(w_key, orders[0])
    full_value = gather_rows(w_value, orders[1])
    full_query = gather_rows(w_query, orders[2])
    full_gate = gather_rows(w_gate, orders[0])
    gain_columns = jnp.broadcast_to(out_gain[:, None], (out_gain.shape[0], 128))
    full_out = gather_rows(jnp.concatenate([w_out, gain_columns], axis=1), orders[1])
    full_one = gather_rows(w_one, orders[2])
    full_two = gather_rows(w_two, orders[0])
    full_three = gather_rows(w_three, orders[1])
    gain = full_out[:, width].astype(WIDE)[None, :]
    full_out = full_out[:, :width]

    rows = rows_spec(width)
    narrow = ((row_count, width), LOW, rows)
    wide = ((row_count, width), WIDE, rows)
    big = ((row_count, hidden), LOW, rows_spec(hidden))
    state_spec = pl.BlockSpec((1, HD, width), lambda i: (i // per_seq, 0, 0))
    state = ((seq_count, HD, width), WIDE, state_spec)
    square = 2 * row_count * width * width

    normed_low, pre_key, keys, values, totals = call(
        lambda *refs: key_value_kernel(per_seq, *refs),
        steps,
        [(tok, rows), (full_key, whole_spec(full_key)), (full_value, whole_spec(full_value))],
        [narrow, narrow, narrow, narrow, state],
        flops=2 * square,
    )
    incoming = shift_sum(totals, "fsdp", False)
    pre_query, queries, pre_gate = call(
        query_gate_kernel,
        steps,
        [(normed_low, rows), (full_query, whole_spec(full_query)), (full_gate, whole_spec(full_gate))],
        [narrow, narrow, narrow],
        flops=2 * square,
    )
    prefix_spec = pl.BlockSpec((1, HD, width), lambda i: (i, 0, 0))
    attended, mixed, residual, prefix = call(
        lambda *refs: attend_kernel(per_seq, *refs),
        steps,
        [(queries, rows), (keys, rows), (values, rows), (pre_gate, rows), (tok, rows),
         (incoming, state_spec), (gain, whole_spec(gain)), (full_out, whole_spec(full_out))],
        [narrow, narrow, wide, ((steps, HD, width), LOW, prefix_spec)],
        scratch=[pltpu.VMEM((HD, width), WIDE)],
        flops=3 * square,
    )
    (
        layer_out, normed_two, glu, grad_up_one, grad_up_two, upstream_low, grad_residual,
        grad_residual_low, grad_pre_gate, grad_attended, grad_totals, grad_gain_term,
    ) = call(
        lambda *refs: feed_kernel(per_seq, *refs),
        steps,
        [(limits, pl.BlockSpec(memory_space=pltpu.SMEM)), (residual, rows), (cot, rows),
         (full_one, whole_spec(full_one)), (full_two, whole_spec(full_two)),
         (full_three, whole_spec(full_three)), (full_out, whole_spec(full_out)),
         (gain, whole_spec(gain)), (pre_gate, rows), (attended, rows), (queries, rows)],
        [narrow, narrow, big, big, big, narrow, wide, narrow, narrow, narrow, state,
         ((1, width), WIDE, pl.BlockSpec((1, width), lambda i: (0, 0)))],
        flops=12 * row_count * width * hidden + square,
    )
    outgoing = shift_sum(grad_totals, "fsdp", True)
    grad_one = scatter_rows(dot_tn(normed_two, grad_up_one), orders[1])
    grad_two = scatter_rows(dot_tn(normed_two, grad_up_two), orders[2])
    grad_three = scatter_rows(dot_tn(glu, upstream_low), orders[0])
    gain_term = jnp.broadcast_to(grad_gain_term.reshape(width, 1), (width, 128))
    grad_out = scatter_rows(
        jnp.concatenate([dot_tn(mixed, grad_residual_low), gain_term], axis=1), orders[1]
    )
    grad_gain = grad_out[:, width]
    grad_out = grad_out[:, :width]

    def back(i):
        return (i // per_seq) * per_seq + per_seq - 1 - i % per_seq

    back_rows = rows_spec(width, order=back)
    back_narrow = ((row_count, width), LOW, back_rows)
    grad_pre_query, grad_pre_key, grad_pre_value = call(
        lambda *refs: attend_back_kernel(per_seq, *refs),
        steps,
        [(queries, back_rows), (keys, back_rows), (values, back_rows),
         (grad_attended, back_rows), (pre_query, back_rows), (pre_key, back_rows),
         (prefix, pl.BlockSpec((1, HD, width), lambda i: (back(i), 0, 0))),
         (outgoing, state_spec)],
        [back_narrow, back_narrow, back_narrow],
        scratch=[pltpu.VMEM((HD, width), WIDE)],
        flops=6 * square,
    )
    grad_query = scatter_rows(dot_tn(normed_low, grad_pre_query), orders[0])
    grad_key = scatter_rows(dot_tn(normed_low, grad_pre_key), orders[1])
    grad_value = scatter_rows(dot_tn(normed_low, grad_pre_value), orders[2])
    grad_gate = scatter_rows(dot_tn(normed_low, grad_pre_gate), orders[0])
    (input_grad,) = call(
        input_kernel,
        steps,
        [(grad_pre_query, rows), (grad_pre_key, rows), (grad_pre_value, rows),
         (grad_pre_gate, rows), (full_query, whole_spec(full_query)),
         (full_key, whole_spec(full_key)), (full_value, whole_spec(full_value)),
         (full_gate, whole_spec(full_gate)), (tok, rows), (grad_residual, rows)],
        [wide],
        flops=4 * square,
    )
    return (
        layer_out.reshape(tokens.shape),
        input_grad.reshape(tokens.shape),
        grad_query,
        grad_key,
        grad_value,
        grad_gate,
        grad_gain,
        grad_out,
        grad_one,
        grad_two,
        grad_three,
    )


def fused_shards(
    tokens,
    lengths,
    w_query,
    w_key,
    w_value,
    w_gate,
    out_gain,
    w_out,
    w_one,
    w_two,
    w_three,
    cotangent,
):
    seq_count, local_length, width = tokens.shape
    row_count = seq_count * local_length
    hidden = w_one.shape[1]
    steps = row_count // BLOCK
    per_seq = local_length // BLOCK
    orders = stream_orders()
    tok = tokens.reshape(row_count, width)
    cot = cotangent.reshape(row_count, width)
    limits = lengths - lax.axis_index("fsdp") * local_length
    gain_columns = jnp.broadcast_to(out_gain[:, None], (out_gain.shape[0], 128))
    rows = rows_spec(width)
    narrow = ((row_count, width), LOW, rows)
    wide = ((row_count, width), WIDE, rows)
    big = ((row_count, hidden), LOW, rows_spec(hidden))
    state_spec = pl.BlockSpec((1, HD, width), lambda i: (i // per_seq, 0, 0))
    state = ((seq_count, HD, width), WIDE, state_spec)
    square = 2 * row_count * width * width

    (
        normed_low, pre_key, keys, values, pre_query, queries, pre_gate, attended, mixed,
        residual, prefix, gain, full_attn, full_one, full_two, full_three,
    ) = forward(
        tok, seq_count, (w_key, w_value, w_query, w_gate, w_out), gain_columns, w_one, w_two, w_three
    )

    def part(n):
        return pl.BlockSpec((width, width), lambda i: (0, n), pipeline_mode=pl.Buffered(1))

    (
        layer_out, normed_two, glu, grad_up_one, grad_up_two, upstream_low, grad_residual,
        grad_residual_low, grad_pre_gate, grad_attended, grad_totals, grad_gain_term,
    ) = call(
        lambda *refs: feed_kernel(per_seq, *refs),
        steps,
        [(limits, pl.BlockSpec(memory_space=pltpu.SMEM)), (residual, rows), (cot, rows),
         (full_one, whole_spec(full_one)), (full_two, whole_spec(full_two)),
         (full_three, whole_spec(full_three)), (full_attn, part(4)),
         (gain, whole_spec(gain)), (pre_gate, rows), (attended, rows), (queries, rows)],
        [narrow, narrow, big, big, big, narrow, wide, narrow, narrow, narrow, state,
         ((1, width), WIDE, pl.BlockSpec((1, width), lambda i: (0, 0)))],
        flops=12 * row_count * width * hidden + square,
    )
    outgoing = shift_sum(grad_totals, "fsdp", True)
    grad_one = scatter_rows(dot_tn(normed_two, grad_up_one), orders[1])
    grad_two = scatter_rows(dot_tn(normed_two, grad_up_two), orders[2])
    grad_three = scatter_rows(dot_tn(glu, upstream_low), orders[0])
    gain_term = jnp.broadcast_to(grad_gain_term.reshape(width, 1), (width, 128))
    grad_out = scatter_rows(
        jnp.concatenate([dot_tn(mixed, grad_residual_low), gain_term], axis=1), orders[1]
    )
    grad_gain = grad_out[:, width]
    grad_out = grad_out[:, :width]

    def back(i):
        return (i // per_seq) * per_seq + per_seq - 1 - i % per_seq

    back_rows = rows_spec(width, order=back)
    back_narrow = ((row_count, width), LOW, back_rows)
    grad_pre_query, grad_pre_key, grad_pre_value = call(
        lambda *refs: attend_back_kernel(per_seq, *refs),
        steps,
        [(queries, back_rows), (keys, back_rows), (values, back_rows),
         (grad_attended, back_rows), (pre_query, back_rows), (pre_key, back_rows),
         (prefix, pl.BlockSpec((1, HD, width), lambda i: (back(i), 0, 0))),
         (outgoing, state_spec)],
        [back_narrow, back_narrow, back_narrow],
        scratch=[pltpu.VMEM((HD, width), WIDE)],
        flops=6 * square,
    )
    grad_query = scatter_rows(dot_tn(normed_low, grad_pre_query), orders[0])
    grad_key = scatter_rows(dot_tn(normed_low, grad_pre_key), orders[1])
    grad_value = scatter_rows(dot_tn(normed_low, grad_pre_value), orders[2])
    grad_gate = scatter_rows(dot_tn(normed_low, grad_pre_gate), orders[0])
    (input_grad,) = call(
        input_kernel,
        steps,
        [(grad_pre_query, rows), (grad_pre_key, rows), (grad_pre_value, rows),
         (grad_pre_gate, rows), (full_attn, part(2)), (full_attn, part(0)),
         (full_attn, part(1)), (full_attn, part(3)), (tok, rows), (grad_residual, rows)],
        [wide],
        flops=4 * square,
    )
    return (
        layer_out.reshape(tokens.shape),
        input_grad.reshape(tokens.shape),
        grad_query,
        grad_key,
        grad_value,
        grad_gate,
        grad_gain,
        grad_out,
        grad_one,
        grad_two,
        grad_three,
    )


def shards(*arrays):
    tokens, w_query, w_three = arrays[0], arrays[2], arrays[10]
    sizes = (lax.axis_size("dp"), lax.axis_size("fsdp"))
    fits = w_query.shape[0] % 16 == 0 and w_three.shape[0] % 8 == 0 and tokens.shape[1] >= 4 * BLOCK
    if sizes == (16, 2) and fits:
        return fused_shards(*arrays)
    return plain_shards(*arrays)


def solution(mesh):
    in_specs = (
        P("dp", "fsdp", None),
        P("dp"),
        P(("dp", "fsdp"), None),
        P(("dp", "fsdp"), None),
        P(("dp", "fsdp"), None),
        P(("dp", "fsdp"), None),
        P(("dp", "fsdp")),
        P(("dp", "fsdp"), None),
        P(("dp", "fsdp"), None),
        P(("dp", "fsdp"), None),
        P(("dp", "fsdp"), None),
        P("dp", "fsdp", None),
    )
    out_specs = (
        P("dp", "fsdp", None),
        P("dp", "fsdp", None),
        P(("dp", "fsdp"), None),
        P(("dp", "fsdp"), None),
        P(("dp", "fsdp"), None),
        P(("dp", "fsdp"), None),
        P(("dp", "fsdp")),
        P(("dp", "fsdp"), None),
        P(("dp", "fsdp"), None),
        P(("dp", "fsdp"), None),
        P(("dp", "fsdp"), None),
    )
    return jax.shard_map(shards, mesh=mesh, in_specs=in_specs, out_specs=out_specs, check_vma=False)
```

```python
import functools

import jax
import jax.numpy as jnp
from jax import lax
from jax.experimental import pallas as pl
from jax.experimental.pallas import tpu as pltpu
from jax.sharding import PartitionSpec as P

HD = 64
H = 16
BLOCK = 256


GROUP = 256
HEADS = GROUP // HD
LOW = jnp.bfloat16
WIDE = jnp.float32

norm_epsilon = 1e-06


def bit_steps():
    steps = []
    for axis in ("dp", "fsdp"):
        size = lax.axis_size(axis)
        bit = 0
        while (1 << bit) < size:
            steps.append((axis, bit, [(i, i ^ (1 << bit)) for i in range(size)]))
            bit += 1
    return steps


def stream_orders():
    steps = bit_steps()
    dp = [s for s in steps if s[0] == "dp"]
    fs = [s for s in steps if s[0] == "fsdp"]
    core, rest = dp[0], fs[:1] + dp[1:3]
    tail = dp[3:] + fs[1:]
    return [[core] + rest[k:] + rest[:k] + tail for k in range(3)]


def own_bit(step):
    axis, bit, _ = step
    return lax.rem(lax.div(lax.axis_index(axis), 1 << bit), 2)


def bit_dims():
    steps = bit_steps()
    dp = sorted([s for s in steps if s[0] == "dp"], key=lambda s: -s[1])
    fs = sorted([s for s in steps if s[0] == "fsdp"], key=lambda s: -s[1])
    return [(s[0], s[1]) for s in dp + fs]


def gather_rows(shard, order):
    dims = bit_dims()
    held = []
    data = shard
    for step in reversed(order):
        axis, bit, perm = step
        other = lax.ppermute(data, axis, perm)
        mine = own_bit(step) == 0
        place = sum(1 for d in held if dims.index(d) < dims.index((axis, bit)))
        held.append((axis, bit))
        data = jnp.stack(
            [jnp.where(mine, data, other), jnp.where(mine, other, data)], axis=place
        )
    return data.reshape((-1,) + shard.shape[1:])


def scatter_rows(full, order):
    dims = bit_dims()
    rows = full.shape[0] >> len(dims)
    data = full.astype(jnp.bfloat16).reshape((2,) * len(dims) + (rows,) + full.shape[1:])
    left = list(dims)
    for at, step in enumerate(order):
        axis, bit, perm = step
        place = left.index((axis, bit))
        left.pop(place)
        own = own_bit(step)
        send = lax.dynamic_index_in_dim(data, 1 - own, place, keepdims=False)
        keep = lax.dynamic_index_in_dim(data, own, place, keepdims=False)
        come = lax.ppermute(send, axis, perm)
        data = keep.astype(jnp.float32) + come.astype(jnp.float32)
        if at < len(order) - 1:
            data = data.astype(jnp.bfloat16)
    return data


def shift_sum(x, axis, reverse):
    size = lax.axis_size(axis)
    total = jnp.zeros_like(x)
    low = x.astype(jnp.bfloat16)
    for s in range(1, size):
        pairs = [(i + s, i) if reverse else (i, i + s) for i in range(size - s)]
        total = total + lax.ppermute(low, axis, pairs).astype(x.dtype)
    return total


def dot_nn(a, b):
    return jnp.dot(a, b, preferred_element_type=WIDE)


def dot_nt(a, b):
    return lax.dot_general(a, b, (((1,), (1,)), ((), ())), preferred_element_type=WIDE)


def dot_tn(a, b):
    return lax.dot_general(a, b, (((0,), (0,)), ((), ())), preferred_element_type=WIDE)


def rms_scale(values):
    return lax.rsqrt(jnp.mean(values * values, axis=-1, keepdims=True) + norm_epsilon)


def norm_back(values, scale, upstream):
    inner_mean = jnp.mean(upstream * values, axis=-1, keepdims=True)
    return scale * (upstream - values * (scale * scale) * inner_mean)


def silu_slope(pre_rows):
    logistic = jax.nn.sigmoid(pre_rows)
    return logistic * (1.0 + pre_rows * (1.0 - logistic))


def head_square():
    row = lax.broadcasted_iota(jnp.int32, (GROUP, GROUP), 0) // HD
    col = lax.broadcasted_iota(jnp.int32, (GROUP, GROUP), 1) // HD
    return (row == col).astype(WIDE)


def head_rows():
    lane = lax.broadcasted_iota(jnp.int32, (1, GROUP), 1) // HD
    return [(lane == h).astype(WIDE).astype(LOW) for h in range(HEADS)]


def split_heads(rows, marks):
    return jnp.concatenate([rows * mark for mark in marks], axis=0)


def pack_state(square, same):
    return jnp.sum((square * same).reshape(HEADS, HD, GROUP), axis=0)


def open_state(packed, same):
    return (jnp.concatenate([packed] * HEADS, axis=0) * same).astype(LOW)


def causal_masks():
    i = lax.broadcasted_iota(jnp.int32, (BLOCK, HEADS * BLOCK), 0)
    j = lax.broadcasted_iota(jnp.int32, (BLOCK, HEADS * BLOCK), 1) % BLOCK
    return (i >= j).astype(WIDE), (j >= i).astype(WIDE)


def groups(width):
    return [slice(g * GROUP, (g + 1) * GROUP) for g in range(width // GROUP)]


def key_value_kernel(per_seq, tok, w_key, w_value, normed, pre_key, keys, values, totals):
    x = tok[...].astype(WIDE)
    rows = (x * rms_scale(x)).astype(LOW)
    normed[...] = rows
    pre = dot_nn(rows, w_key[...])
    pre_key[...] = pre.astype(LOW)
    k = jax.nn.silu(pre).astype(LOW)
    keys[...] = k
    v = dot_nn(rows, w_value[...]).astype(LOW)
    values[...] = v

    @pl.when(pl.program_id(0) % per_seq == 0)
    def _():
        totals[...] = jnp.zeros_like(totals)

    same = head_square()
    for g in groups(k.shape[1]):
        totals[0, :, g] += pack_state(dot_tn(k[:, g], v[:, g]), same)


def query_gate_kernel(normed, w_query, w_gate, pre_query, queries, pre_gate):
    rows = normed[...]
    pre = dot_nn(rows, w_query[...])
    pre_query[...] = pre.astype(LOW)
    queries[...] = jax.nn.silu(pre).astype(LOW)
    pre_gate[...] = dot_nn(rows, w_gate[...]).astype(LOW)


def attend_kernel(
    per_seq, queries, keys, values, pre_gate, tok, incoming, gain, w_out,
    attended, mixed, residual, prefix, carry,
):
    @pl.when(pl.program_id(0) % per_seq == 0)
    def _():
        carry[...] = incoming[0]

    same, marks = head_square(), head_rows()
    causal, _ = causal_masks()
    prefix[0] = carry[...].astype(LOW)
    for g in groups(queries.shape[1]):
        q, k, v = queries[:, g], keys[:, g], values[:, g]
        scores = (dot_nt(q, split_heads(k, marks)) * causal).astype(LOW)
        out = dot_nn(scores, split_heads(v, marks))
        out += dot_nn(q, open_state(carry[:, g], same))
        attended[:, g] = out.astype(LOW)
        carry[:, g] += pack_state(dot_tn(k, v), same)
    rows = attended[...].astype(WIDE)
    gate = jax.nn.sigmoid(pre_gate[...].astype(WIDE))
    rows = (rows * rms_scale(rows) * gain[...] * gate).astype(LOW)
    mixed[...] = rows
    residual[...] = tok[...].astype(WIDE) + dot_nn(rows, w_out[...])


def feed_kernel(
    per_seq, turned, limits, residual, cotangent, w_one, w_two, w_three, w_out, gain, pre_gate,
    attended, queries,
    layer_out, normed, glu, grad_one, grad_two, upstream_low, grad_residual, grad_low,
    grad_gate, grad_attended, totals, grad_gain, held=None,
):
    step = pl.program_id(0)
    row_count = residual.shape[0]
    spot = lax.broadcasted_iota(jnp.int32, (row_count, 1), 0) + (step % per_seq) * row_count
    valid = (spot < limits[step // per_seq]).astype(WIDE)
    res = residual[...]
    scale = rms_scale(res)
    rows = (res * scale).astype(LOW)
    normed[...] = rows.T if turned else rows
    upstream = cotangent[...].astype(WIDE) * valid
    up_low = upstream.astype(LOW)
    upstream_low[...] = up_low
    for c in groups(w_one.shape[1]):
        one = dot_nn(rows, w_one[:, c])
        two = dot_nn(rows, w_two[:, c])
        back = dot_nt(up_low, w_three[c, :])
        product = (one * two).astype(LOW)
        if turned:
            held[:, c] = product
            glu[c, :] = product.T
        else:
            glu[:, c] = product
        grad_one[:, c] = (back * two).astype(LOW)
        grad_two[:, c] = (back * one).astype(LOW)
    layer_out[...] = (valid * (res + dot_nn(held[...] if turned else glu[...], w_three[...]))).astype(LOW)
    back = dot_nt(grad_one[...], w_one[...]) + dot_nt(grad_two[...], w_two[...])
    grad = upstream + norm_back(res, scale, back)
    grad_residual[...] = grad
    grad = grad.astype(LOW)
    grad_low[...] = grad
    grad = dot_nt(grad, w_out[...])
    gate = jax.nn.sigmoid(pre_gate[...].astype(WIDE))
    att = attended[...].astype(WIDE)
    scale = rms_scale(att)
    hat = att * scale
    gated = grad * gate

    @pl.when(step == 0)
    def _():
        grad_gain[...] = jnp.zeros_like(grad_gain)

    grad_gain[...] += jnp.sum(gated * hat, axis=0, keepdims=True)
    gated = gated * gain[...]
    grad_gate[...] = (gated * hat * (1.0 - gate)).astype(LOW)
    grad_att = norm_back(att, scale, gated).astype(LOW)
    grad_attended[...] = grad_att

    @pl.when(step % per_seq == 0)
    def _():
        totals[...] = jnp.zeros_like(totals)

    same = head_square()
    for g in groups(grad_att.shape[1]):
        totals[0, :, g] += pack_state(dot_tn(queries[:, g], grad_att[:, g]), same)


def attend_back_kernel(
    per_seq, queries, keys, values, grad_attended, pre_query, pre_key, prefix, incoming,
    grad_query, grad_key, grad_value, carry,
):
    @pl.when(pl.program_id(0) % per_seq == 0)
    def _():
        carry[...] = incoming[0]

    same, marks = head_square(), head_rows()
    causal, causal_t = causal_masks()
    for g in groups(queries.shape[1]):
        q, k, v, ga = queries[:, g], keys[:, g], values[:, g], grad_attended[:, g]
        qs, ks, vs, gs = (split_heads(rows, marks) for rows in (q, k, v, ga))
        state = open_state(prefix[0, :, g].astype(WIDE), same)
        grad_state = open_state(carry[:, g], same)
        grad_scores = (dot_nt(ga, vs) * causal).astype(LOW)
        gq = dot_nn(grad_scores, ks) + dot_nt(ga, state)
        grad_scores = (dot_nt(v, gs) * causal_t).astype(LOW)
        gk = dot_nn(grad_scores, qs) + dot_nt(v, grad_state)
        scores = (dot_nt(k, qs) * causal_t).astype(LOW)
        gv = dot_nn(scores, gs) + dot_nn(k, grad_state)
        grad_query[:, g] = (gq * silu_slope(pre_query[:, g].astype(WIDE))).astype(LOW)
        grad_key[:, g] = (gk * silu_slope(pre_key[:, g].astype(WIDE))).astype(LOW)
        grad_value[:, g] = gv.astype(LOW)
        carry[:, g] += pack_state(dot_tn(q, ga), same)


def input_kernel(
    grad_query, grad_key, grad_value, grad_gate, w_query, w_key, w_value, w_gate, tok,
    grad_residual, input_grad,
):
    grad = dot_nt(grad_query[...], w_query[...]) + dot_nt(grad_key[...], w_key[...])
    grad += dot_nt(grad_value[...], w_value[...]) + dot_nt(grad_gate[...], w_gate[...])
    x = tok[...].astype(WIDE)
    input_grad[...] = grad_residual[...] + norm_back(x, rms_scale(x), grad)


def rows_spec(width, block=BLOCK, order=lambda i: i):
    return pl.BlockSpec((block, width), lambda i: (order(i), 0))


def whole_spec(array):
    rank = array.ndim
    return pl.BlockSpec(array.shape, lambda i: (0,) * rank, pipeline_mode=pl.Buffered(1))


def call(kernel, steps, operands, results, scratch=(), flops=0, limit=56):
    moved = sum(a.size * a.dtype.itemsize for a, _ in operands)
    return pl.pallas_call(
        kernel,
        grid=(steps,),
        in_specs=[spec for _, spec in operands],
        out_specs=[spec for _, _, spec in results],
        out_shape=[jax.ShapeDtypeStruct(shape, dtype) for shape, dtype, _ in results],
        scratch_shapes=list(scratch),
        compiler_params=pltpu.CompilerParams(
            dimension_semantics=("arbitrary",), vmem_limit_bytes=limit << 20
        ),
        cost_estimate=pl.CostEstimate(flops=flops, bytes_accessed=moved, transcendentals=0),
    )(*[a for a, _ in operands])


def index_bits():
    bits = []
    for axis in ("dp", "fsdp"):
        count = lax.axis_size(axis).bit_length() - 1
        bits += [(axis, bit) for bit in reversed(range(count))]
    return bits


def bit_value(bit):
    axis, at = bit
    return lax.rem(lax.div(lax.axis_index(axis), 1 << at), 2)


def flip_device(bit):
    axis, at = bit
    return {axis: lax.axis_index(axis) + (1 - 2 * bit_value(bit)) * (1 << at)}


def greet(bits):
    barrier = pltpu.get_barrier_semaphore()
    for bit in bits:
        pl.semaphore_signal(
            barrier, inc=1, device_id=flip_device(bit), device_id_type=pl.DeviceIdType.MESH
        )
    pl.semaphore_wait(barrier, len(bits))


class Sems:
    def __init__(self, send, recv):
        self.send, self.recv, self.used = send, recv, 0

    def copy(self, src, dst, bit):
        at = self.used
        self.used += 1
        return pltpu.make_async_remote_copy(
            src_ref=src,
            dst_ref=dst,
            send_sem=self.send.at[at],
            recv_sem=self.recv.at[at],
            device_id=flip_device(bit),
            device_id_type=pl.DeviceIdType.MESH,
        )


class Gather:
    def __init__(self, buf, bits, order, sems, columns=slice(None)):
        self.stages = []
        held = []

        def cube(flipped=None):
            index = []
            for bit in bits:
                if bit == flipped:
                    index.append(1 - bit_value(bit))
                else:
                    index.append(slice(None) if bit in held else bit_value(bit))
            return buf.at[tuple(index) + (slice(None), columns)]

        for bit in order[:-1]:
            ref = cube()
            copies = [sems.copy(ref, ref, bit)]
            if bit == order[-2]:
                copies.append(sems.copy(ref, ref, order[-1]))
                far = cube(flipped=bit)
            self.stages.append(copies)
            held.append(bit)
        self.stages.append([sems.copy(far, far, order[-1])])

    def start(self, stage):
        for copy in self.stages[stage]:
            copy.start()

    def arrive(self, stage):
        self.stages[stage][0].wait_recv()

    def advance(self, stage):
        self.arrive(stage - 1)
        self.start(stage)

    def finish(self):
        self.stages[-2][1].wait_recv()
        self.stages[-1][0].wait_recv()

    def drain(self):
        for copies in self.stages:
            for copy in copies:
                copy.wait_send()


class Scatter:
    def __init__(self, sems, core, bits, order, acc, send, come, recvs, columns, slots):
        self.bits, self.order, self.acc, self.columns = bits, order, acc, columns
        self.come, self.recvs, self.slots = come, recvs, slots
        tail = (slice(None),)
        full = (slice(None),) * len(bits) + tail + (slots,)
        self.core = sems.copy(send.at[full], come.at[full], core)
        self.copies = []
        for k, bit in enumerate(order):
            done = order[:k]
            index = tuple(
                1 - bit_value(b) if b == bit else bit_value(b) if b in done else slice(None)
                for b in bits
            )
            free = (slice(None),) * (len(bits) - k - 1)
            self.copies.append(
                sems.copy(
                    acc.at[index + tail + (columns,)],
                    recvs[k].at[free + tail + (columns,)],
                    bit,
                )
            )

    def add(self, done, source, columns):
        free = [b for b in self.bits if b not in done]

        def one(k, _):
            at = [lax.rem(lax.div(k, 1 << (len(free) - 1 - n)), 2) for n in range(len(free))]
            mine = tuple(bit_value(b) if b in done else at[free.index(b)] for b in self.bits)
            here = mine + (slice(None), self.columns)
            there = tuple(at) + (slice(None), columns)
            total = self.acc[here].astype(WIDE) + source[there].astype(WIDE)
            self.acc[here] = total.astype(LOW)
            return 0

        lax.fori_loop(0, 1 << len(free), one, 0)

    def launch(self):
        self.core.start()

    def advance(self, k):
        if k == 0:
            self.core.wait_recv()
            self.add([], self.come, self.slots)
        else:
            self.copies[k - 1].wait_recv()
            self.add(self.order[:k], self.recvs[k - 1], self.columns)
        self.copies[k].start()

    def result(self):
        self.copies[-1].wait_recv()
        own = tuple(bit_value(b) for b in self.bits)
        here = (slice(None), self.columns)
        return self.acc[own + here].astype(WIDE) + self.recvs[-1][here].astype(WIDE)

    def drain(self, core=True):
        if core:
            self.core.wait_send()
        for copy in self.copies:
            copy.wait_send()


def run_events(step, events):
    for at in sorted(events):

        @pl.when(step == at)
        def _():
            for action in events[at]:
                action()


def half_rows(ref, core):
    rows = ref[:, core]
    return rows.reshape(rows.shape[0] * rows.shape[1], rows.shape[2])


def attend_back_step(
    same, queries, keys, values, grad_attended, pre_query, pre_key, prefix,
    grad_query, grad_key, grad_value, carry,
):
    marks = head_rows()
    causal, causal_t = causal_masks()
    for g in groups(queries.shape[1]):
        q, k, v, ga = queries[:, g], keys[:, g], values[:, g], grad_attended[:, g]
        qs, ks, vs, gs = (split_heads(rows, marks) for rows in (q, k, v, ga))
        state = open_state(prefix[0, :, g].astype(WIDE), same)
        grad_state = open_state(carry[:, g], same)
        grad_scores = (dot_nt(ga, vs) * causal).astype(LOW)
        gq = dot_nn(grad_scores, ks) + dot_nt(ga, state)
        grad_scores = (dot_nt(v, gs) * causal_t).astype(LOW)
        gk = dot_nn(grad_scores, qs) + dot_nt(v, grad_state)
        scores = (dot_nt(k, qs) * causal_t).astype(LOW)
        gv = dot_nn(scores, gs) + dot_nn(k, grad_state)
        grad_query[:, g] = (gq * silu_slope(pre_query[:, g].astype(WIDE))).astype(LOW)
        grad_key[:, g] = (gk * silu_slope(pre_key[:, g].astype(WIDE))).astype(LOW)
        grad_value[:, g] = gv.astype(LOW)
        carry[:, g] += pack_state(dot_tn(q, ga), same)


CHUNK = 256


def feed_back_kernel(
    plan, per_seq, bits, orders,
    normed, grad_one, grad_two, glu, upstream,
    queries, keys, values, grad_attended, pre_query, pre_key, prefix, totals,
    out_one, out_two, out_three, grad_query, grad_key, grad_value,
    acc, come1, come2, come3, come4, send, come,
    acc3, come31, come32, come33, send3, come3c, last_send, last_come,
    state_out, state_in, carry, send_sems, recv_sems,
):
    step = pl.program_id(0)
    parts, base = plan
    core, links = bits[-2], bits[:-2] + bits[-1:]
    mine = bit_value(core)
    other = 1 - mine
    sems = Sems(send_sems, recv_sems)
    hidden = out_one.shape[1]
    wide_a = parts[0][1] * CHUNK
    wide_b = hidden - wide_a
    recvs = (come1, come2, come3, come4)
    pieces = []
    for slot, (begin, span, order) in enumerate(
        ((0, wide_a, orders[0]), (hidden, wide_a, orders[2]),
         (wide_a, wide_b, orders[0]), (hidden + wide_a, wide_b, orders[2]))
    ):
        pieces.append(
            Scatter(
                sems, core, links, order, acc, send.at[slot % 2], come.at[slot], recvs,
                slice(begin, begin + span), slice(0, span),
            )
        )
    one_a, two_a, one_b, two_b = pieces
    half = upstream.shape[1] // 2
    threes = [
        Scatter(
            sems, core, links[:-1], [b for b in orders[1] if b != bits[-1]], acc3, send3, come3c,
            (come31, come32, come33), slice(n * half, (n + 1) * half),
            slice(n * half, (n + 1) * half),
        )
        for n in range(2)
    ]
    cuts = [slice(n * half, (n + 1) * half) for n in range(2)]
    swaps = [sems.copy(last_send.at[:, c], last_come.at[:, c], bits[-1]) for c in cuts]
    swap_state = sems.copy(state_out, state_in, bits[-1])
    side = bit_value(bits[-1])

    def swap_three(n):
        total = threes[n].result()
        deep = total.shape[0] // 2
        low, high = total[:deep], total[deep:]
        upper = side.astype(WIDE)
        out_three[:, cuts[n]] = low * (1 - upper) + high * upper
        last_send[:, cuts[n]] = low * upper + high * (1 - upper)
        swaps[n].start()

    def end_three(n):
        swaps[n].wait_recv()
        out_three[:, cuts[n]] += last_come[:, cuts[n]]

    def end(piece, out, begin):
        span = piece.columns.stop - piece.columns.start
        out[:, begin : begin + span] = piece.result()

    ends = [begin + count for begin, count in parts]

    @pl.when(step == 0)
    def _():
        greet(bits)
        state_out[...] = totals[...].astype(LOW)
        swap_state.start()

    run_events(step, {
        parts[3][0]: [one_a.core.wait_send],
        parts[4][0]: [two_a.core.wait_send],
        ends[0] + 4: [functools.partial(one_a.advance, 0)],
        ends[1] + 5: [functools.partial(two_a.advance, 0)],
        ends[2] + 3: [functools.partial(threes[0].advance, 0)],
        ends[3] + 4: [functools.partial(one_b.advance, 0)],
        ends[4] + 5: [functools.partial(two_b.advance, 0)],
        base - 2: [functools.partial(one_a.advance, 1)],
        base: [functools.partial(two_a.advance, 1)],
        base + 1: [functools.partial(threes[1].advance, 0),
                   functools.partial(threes[0].advance, 1),
                   functools.partial(one_a.advance, 2)],
        base + 2: [functools.partial(one_a.advance, 3),
                   functools.partial(two_a.advance, 2)],
        base + 3: [functools.partial(one_b.advance, 1),
                   functools.partial(two_b.advance, 1),
                   functools.partial(threes[0].advance, 2)],
        base + 4: [functools.partial(two_a.advance, 3),
                   functools.partial(swap_three, 0)],
        base + 5: [functools.partial(threes[1].advance, 1),
                   functools.partial(one_b.advance, 2),
                   functools.partial(two_b.advance, 2)],
        base + 6: [functools.partial(one_b.advance, 3),
                   functools.partial(two_b.advance, 3),
                   functools.partial(threes[1].advance, 2)],
        base + 7: [functools.partial(swap_three, 1),
                   functools.partial(end, one_a, out_one, 0),
                   functools.partial(end, two_a, out_two, 0),
                   functools.partial(end_three, 0)],
    })

    def weight_chunk(rhs, chunk, piece_base, slot, span_base):
        rows = rhs[...]
        lead = acc.shape[:-1]
        at = pl.ds(pl.multiple_of(chunk * CHUNK, CHUNK), CHUNK)
        give = dot_nn(half_rows(normed, other), rows).astype(LOW).reshape(lead + (CHUNK,))
        send[(slot,) + (slice(None),) * len(lead) + (at,)] = give
        keep = dot_nn(half_rows(normed, mine), rows).astype(LOW).reshape(lead + (CHUNK,))
        at = pl.ds(pl.multiple_of(span_base + chunk * CHUNK, CHUNK), CHUNK)
        acc[(slice(None),) * len(lead) + (at,)] = keep

    def chunk_phase(part, rhs, slot, span_base):
        begin, count = parts[part]

        @pl.when((step >= begin) & (step < begin + count))
        def _():
            weight_chunk(rhs, step - begin, None, slot, span_base)

    chunk_phase(0, grad_one, 0, 0)
    chunk_phase(1, grad_two, 1, hidden)
    chunk_phase(3, grad_one, 0, wide_a)
    chunk_phase(4, grad_two, 1, hidden + wide_a)

    for n in range(2):
        begin, count = parts[2 + 3 * n]

        @pl.when((step >= begin) & (step < begin + count))
        def _():
            k = step - begin
            at = tuple(lax.rem(lax.div(k, 1 << (2 - d)), 2) for d in range(3))
            deep = glu.shape[0] // 2
            rows = upstream[:, cuts[n]]

            def part(c):
                left = glu[pl.ds(pl.multiple_of(c * deep, 16), deep), :]
                return dot_nn(left, rows).astype(LOW)

            send3[at + (slice(None), cuts[n])] = part(other)
            acc3[at + (slice(None), cuts[n])] = part(mine)

    run_events(step, {
        ends[0] - 1: [one_a.launch],
        ends[1] - 1: [two_a.launch],
        ends[2] - 1: [threes[0].launch],
        ends[3] - 1: [one_b.launch],
        ends[4] - 1: [two_b.launch],
        ends[5] - 1: [threes[1].launch, swap_state.wait_recv],
    })

    @pl.when(step >= base)
    def _():
        at = step - base

        @pl.when(at % per_seq == 0)
        def _():
            carry[...] = state_in[at // per_seq].astype(WIDE) * (1 - side).astype(WIDE)

        attend_back_step(
            head_square(), queries, keys, values, grad_attended, pre_query, pre_key, prefix,
            grad_query, grad_key, grad_value, carry,
        )

    @pl.when(step == pl.num_programs(0) - 1)
    def _():
        end(one_b, out_one, wide_a)
        end(two_b, out_two, wide_a)
        end_three(1)
        one_a.drain(core=False)
        two_a.drain(core=False)
        for piece in [one_b, two_b] + threes:
            piece.drain()
        for copy in swaps:
            copy.wait_send()
        swap_state.wait_send()


def clip(value, low, high):
    return jnp.minimum(jnp.maximum(value, low), high)


def feed_back(
    seq_count, normed, grad_one, grad_two, glu, upstream, queries, keys, values, grad_attended,
    pre_query, pre_key, prefix, totals,
):
    row_count, width = queries.shape
    hidden = grad_one.shape[1]
    steps = row_count // BLOCK
    per_seq = steps // seq_count
    bits = index_bits()
    orders = [[(s[0], s[1]) for s in order[1:]] for order in stream_orders()]
    chunks = hidden // CHUNK
    more, less = chunks - chunks // 2, chunks // 2
    lead3 = 8
    counts = (more, more, lead3, less, less, lead3)
    parts = []
    for count in counts:
        parts.append((sum(c for _, c in parts), count))
    base = sum(counts)
    deep = hidden // lead3
    slab = width // 32
    p = parts

    def one_at(i):
        return clip(i - p[0][0], 0, more - 1) + clip(i - p[3][0] + 1, 0, less)

    def two_at(i):
        return clip(i - p[1][0], 0, more - 1) + clip(i - p[4][0] + 1, 0, less)

    def glu_at(i):
        return jnp.where(
            i < p[3][0], clip(i - p[2][0], 0, lead3 - 1), clip(i - p[5][0], 0, lead3 - 1)
        )

    def back(i):
        at = clip(i - base, 0, steps - 1)
        return (at // per_seq) * per_seq + per_seq - 1 - at % per_seq

    rows = pl.BlockSpec((BLOCK, width), lambda i: (back(i), 0))
    vmem = pl.BlockSpec(memory_space=pltpu.VMEM)
    rows_low = jax.ShapeDtypeStruct((row_count, width), LOW)
    wide = (more * CHUNK)
    low = functools.partial(pltpu.VMEM, dtype=LOW)
    kernel = functools.partial(feed_back_kernel, (parts, base), per_seq, bits, orders)
    return pl.pallas_call(
        kernel,
        grid=(base + steps,),
        in_specs=[
            vmem,
            pl.BlockSpec((row_count, CHUNK), lambda i: (0, one_at(i))),
            pl.BlockSpec((row_count, CHUNK), lambda i: (0, two_at(i))),
            pl.BlockSpec((deep, row_count), lambda i: (glu_at(i), 0)),
            vmem,
        ]
        + [rows] * 6
        + [pl.BlockSpec((1, HD, width), lambda i: (back(i), 0, 0)), vmem],
        out_specs=[vmem] * 3 + [rows] * 3,
        out_shape=[
            jax.ShapeDtypeStruct((slab, hidden), WIDE),
            jax.ShapeDtypeStruct((slab, hidden), WIDE),
            jax.ShapeDtypeStruct((hidden // 32, width), WIDE),
        ]
        + [rows_low] * 3,
        scratch_shapes=[
            low((2, 2, 2, 2, slab, 2 * hidden)),
            low((2, 2, 2, slab, 2 * hidden)),
            low((2, 2, slab, 2 * hidden)),
            low((2, slab, 2 * hidden)),
            low((slab, 2 * hidden)),
            low((2, 2, 2, 2, 2, slab, wide)),
            low((4, 2, 2, 2, 2, slab, wide)),
            low((2, 2, 2, deep // 2, width)),
            low((2, 2, deep // 2, width)),
            low((2, deep // 2, width)),
            low((deep // 2, width)),
            low((2, 2, 2, deep // 2, width)),
            low((2, 2, 2, deep // 2, width)),
            pltpu.VMEM((hidden // 32, width), WIDE),
            pltpu.VMEM((hidden // 32, width), WIDE),
            low((seq_count, HD, width)),
            low((seq_count, HD, width)),
            pltpu.VMEM((HD, width), WIDE),
            pltpu.SemaphoreType.DMA((31,)),
            pltpu.SemaphoreType.DMA((31,)),
        ],
        compiler_params=pltpu.CompilerParams(
            dimension_semantics=("arbitrary",),
            vmem_limit_bytes=62 << 20,
            collective_id=2,
            has_side_effects=True,
        ),
        cost_estimate=pl.CostEstimate(
            flops=6 * row_count * width * hidden + 12 * row_count * width * width,
            bytes_accessed=128 << 20,
            transcendentals=0,
        ),
    )(
        normed.reshape(8, 2, width // 16, row_count), grad_one, grad_two, glu, upstream,
        queries, keys, values, grad_attended, pre_query, pre_key, prefix, totals,
    )


def attend_weights_kernel(
    bits, orders,
    normed, mixed, grad_low, grad_query, grad_key, grad_value, grad_gate, gain_term,
    rows_query, rows_key, rows_value, rows_gate, w_key, w_value, w_query, w_gate, tok,
    grad_residual,
    out, input_grad,
    acc, come1, come2, come3, come4, send, come, send_sems, recv_sems,
):
    step = pl.program_id(0)
    core, links = bits[-2], bits[:-2] + bits[-1:]
    mine = bit_value(core)
    other = 1 - mine
    sems = Sems(send_sems, recv_sems)
    width = tok.shape[1]
    per = width // CHUNK
    chunks = 5 * per
    lead = acc.shape[:-1]
    fill = (slice(None),) * len(lead)
    pieces, first = [], 0
    sizes = (3, 3, 3, 3, 3, 3, 2)
    for n, size in enumerate(sizes):
        begin = first * CHUNK + (128 if first >= per else 0)
        first += size
        stop = first * CHUNK + (128 if first >= per else 0)
        pieces.append(
            Scatter(
                sems, core, links, orders[n % 3], acc, send, come, (come1, come2, come3, come4),
                slice(begin, stop), slice(begin, stop),
            )
        )

    def end(n):
        piece = pieces[n]
        out[:, piece.columns] = piece.result()

    @pl.when(step == 0)
    def _():
        greet(bits)

    table = {
        5: [(0, 0)], 8: [(1, 0)], 11: [(2, 0)], 14: [(3, 0), (0, 1)], 17: [(4, 0), (1, 1)],
        20: [(5, 0), (2, 1), (0, 2)], 21: [(6, 0), (3, 1), (1, 2), (0, 3)],
        22: [(4, 1), (2, 2), (1, 3)], 23: [(5, 1), (6, 1), (3, 2), (2, 3)],
        24: [(4, 2), (3, 3)], 25: [(5, 2), (6, 2), (4, 3)], 26: [(5, 3), (6, 3)],
    }
    run_events(step, {
        at: [functools.partial(pieces[n].advance, k) for n, k in todo]
        for at, todo in table.items()
    })

    def chunk_phase(n, lhs, rhs):
        @pl.when((step >= n * per) & (step < (n + 1) * per))
        def _():
            shift = 128 if n else 0
            at = pl.ds(pl.multiple_of(step * CHUNK + shift, 128), CHUNK)
            rows = rhs[...]
            give = dot_nn(half_rows(lhs, other), rows).astype(LOW)
            send[fill + (at,)] = give.reshape(lead + (CHUNK,))
            keep = dot_nn(half_rows(lhs, mine), rows).astype(LOW)
            acc[fill + (at,)] = keep.reshape(lead + (CHUNK,))

    chunk_phase(0, mixed, grad_low)
    chunk_phase(1, normed, grad_query)
    chunk_phase(2, normed, grad_key)
    chunk_phase(3, normed, grad_value)
    chunk_phase(4, normed, grad_gate)

    @pl.when(step == 0)
    def _():
        column = jnp.broadcast_to(gain_term[...], (128, width)).T
        column = column.reshape(8, 2, width // 16, 128)
        upper = mine.astype(WIDE)
        low, high = column[:, 0], column[:, 1]
        at = fill + (slice(width, width + 128),)
        acc[at] = (low * (1 - upper) + high * upper).astype(LOW).reshape(lead + (128,))
        send[at] = (low * upper + high * (1 - upper)).astype(LOW).reshape(lead + (128,))

    launches, first = {}, 0
    for n, size in enumerate(sizes):
        first += size
        launches[first - 1] = [pieces[n].launch]
    run_events(step, launches)

    @pl.when(step >= chunks)
    def _():
        grad = dot_nt(rows_query[...], w_query[...]) + dot_nt(rows_key[...], w_key[...])
        grad += dot_nt(rows_value[...], w_value[...]) + dot_nt(rows_gate[...], w_gate[...])
        x = tok[...].astype(WIDE)
        input_grad[...] = grad_residual[...] + norm_back(x, rms_scale(x), grad)

    @pl.when(step == pl.num_programs(0) - 1)
    def _():
        for n in range(len(pieces)):
            end(n)
        for piece in pieces:
            piece.drain()


def attend_weights(
    normed, mixed, grad_low, grad_query, grad_key, grad_value, grad_gate, gain_term, full_attn,
    tok, grad_residual,
):
    row_count, width = tok.shape
    steps = row_count // BLOCK
    bits = index_bits()
    orders = [[(s[0], s[1]) for s in order[1:]] for order in stream_orders()]
    per = width // CHUNK
    chunks = 5 * per
    slab = width // 32
    vmem = pl.BlockSpec(memory_space=pltpu.VMEM)
    rows = pl.BlockSpec((BLOCK, width), lambda i: (clip(i - chunks, 0, steps - 1), 0))

    def chunk(n):
        return pl.BlockSpec((row_count, CHUNK), lambda i: (0, clip(i - n * per, 0, per - 1)))

    def part(n):
        return pl.BlockSpec((width, width), lambda i: (0, n), pipeline_mode=pl.Buffered(1))

    low = functools.partial(pltpu.VMEM, dtype=LOW)
    columns = 5 * width + 128
    split = (8, 2, width // 16, row_count)
    return pl.pallas_call(
        functools.partial(attend_weights_kernel, bits, orders),
        grid=(chunks + steps,),
        in_specs=[vmem, vmem] + [chunk(n) for n in range(5)] + [vmem] + [rows] * 4
        + [part(n) for n in range(4)] + [rows, rows],
        out_specs=[vmem, rows],
        out_shape=[
            jax.ShapeDtypeStruct((slab, columns), WIDE),
            jax.ShapeDtypeStruct((row_count, width), WIDE),
        ],
        scratch_shapes=[
            low((2, 2, 2, 2, slab, columns)),
            low((2, 2, 2, slab, columns)),
            low((2, 2, slab, columns)),
            low((2, slab, columns)),
            low((slab, columns)),
            low((2, 2, 2, 2, slab, columns)),
            low((2, 2, 2, 2, slab, columns)),
            pltpu.SemaphoreType.DMA((35,)),
            pltpu.SemaphoreType.DMA((35,)),
        ],
        compiler_params=pltpu.CompilerParams(
            dimension_semantics=("arbitrary",),
            vmem_limit_bytes=62 << 20,
            collective_id=3,
            has_side_effects=True,
        ),
        cost_estimate=pl.CostEstimate(
            flops=18 * row_count * width * width, bytes_accessed=64 << 20, transcendentals=0
        ),
    )(
        normed.reshape(split), mixed.reshape(split), grad_low, grad_query, grad_key, grad_value,
        grad_gate, gain_term, grad_query, grad_key, grad_value, grad_gate,
        full_attn, full_attn, full_attn, full_attn, tok, grad_residual,
    )


FORWARD_COPIES = 80


def forward_kernel(
    steps, per_seq, bits, waves, feed_orders, three_order,
    tok, s_key, s_value, s_query, s_gate, s_out, s_gain, s_one, s_two, s_three,
    normed, pre_key, keys, values, pre_query, queries, pre_gate, attended, mixed, residual,
    prefix, gain_row, full_attn, full_one, full_two, full_three,
    held, all_keys, all_values, all_normed, totals, state_out, state_in, carry,
    three_in, three_slab, send, recv, local,
):
    step = pl.program_id(0)
    width = tok.shape[1]
    last = bits[-1]
    sems = Sems(send, recv)
    attn = [
        [Gather(held, bits, order, sems, columns) for order, columns in wave] for wave in waves
    ]
    feed = [
        Gather(buf, bits, order, sems)
        for buf, order in zip((full_one, full_two), feed_orders)
    ]
    three = Gather(full_three, bits[:-1], three_order, sems)
    swap_three = sems.copy(s_three, three_in, last)
    swap_state = sems.copy(state_out, state_in, last)
    own = tuple(bit_value(bit) for bit in bits)
    keep_attn = pltpu.make_async_copy(held, full_attn, local.at[3])

    def feed_advance(stage):
        for piece in feed:
            piece.advance(stage)
        if stage > 1:
            three.advance(stage - 1)

    @pl.when(step == 0)
    def _():
        place = [
            pltpu.make_async_copy(s_one, full_one.at[own], local.at[0]),
            pltpu.make_async_copy(s_two, full_two.at[own], local.at[1]),
        ]
        for copy in place:
            copy.start()
        for n, shard in enumerate((s_key, s_value, s_query, s_gate, s_out)):
            held[own + (slice(None), slice(n * width, (n + 1) * width))] = shard[...]
        held[own + (slice(None), slice(5 * width, 5 * width + 128))] = s_gain[...]
        greet(bits)
        for wave in attn:
            for piece in wave:
                piece.start(0)
        swap_three.start()
        for copy in place:
            copy.wait()
        for stage in range(1, len(bits)):
            for wave in attn:
                for piece in wave:
                    piece.advance(stage)
            if stage == 1:
                for piece in feed:
                    piece.start(0)
                swap_three.wait_recv()
                mine = (own[-1] == 0).astype(WIDE)
                low, high = s_three[...], three_in[...]
                three_slab[...] = jnp.concatenate(
                    [mine * low + (1 - mine) * high, mine * high + (1 - mine) * low], axis=0
                ).astype(LOW)
                lay = pltpu.make_async_copy(three_slab, full_three.at[own[:-1]], local.at[2])
                lay.start()
                lay.wait()
                three.start(0)
        for piece in attn[0]:
            piece.finish()
        feed_advance(1)

    @pl.when(step == 3)
    def _():
        feed_advance(2)

    @pl.when(step == steps)
    def _():
        for wave in attn[1:]:
            for piece in wave:
                piece.finish()
        keep_attn.start()
        column = held[..., 5 * width : 5 * width + 128].reshape(width, 128)
        gain_row[...] = column.astype(WIDE).T[:1]

    @pl.when(step == steps + 1)
    def _():
        feed_advance(3)

    def weight(n):
        return held[..., n * width : (n + 1) * width].reshape(width, width)

    same = head_square()

    @pl.when(step < steps)
    def _():
        x = tok[...].astype(WIDE)
        rows = (x * rms_scale(x)).astype(LOW)
        normed[...] = rows.T
        here = pl.ds(pl.multiple_of(step * BLOCK, BLOCK), BLOCK)
        all_normed[here, :] = rows
        pre = dot_nn(rows, weight(0))
        pre_key[...] = pre.astype(LOW)
        k = jax.nn.silu(pre).astype(LOW)
        keys[...] = k
        all_keys[here, :] = k
        v = dot_nn(rows, weight(1)).astype(LOW)
        values[...] = v
        all_values[here, :] = v
        seq = step // per_seq

        @pl.when(step % per_seq == 0)
        def _():
            totals[seq] = jnp.zeros((HD, width), WIDE)

        for g in groups(width):
            totals[seq, :, g] += pack_state(dot_tn(k[:, g], v[:, g]), same)

    @pl.when(step == steps - 1)
    def _():
        state_out[...] = totals[...].astype(LOW)
        swap_state.start()

    @pl.when(step >= steps)
    def _():
        at = step - steps
        here = pl.ds(pl.multiple_of(at * BLOCK, BLOCK), BLOCK)
        rows = all_normed[here, :]
        pre = dot_nn(rows, weight(2))
        pre_query[...] = pre.astype(LOW)
        queries[...] = jax.nn.silu(pre).astype(LOW)
        gate = dot_nn(rows, weight(3))
        pre_gate[...] = gate.astype(LOW)

        @pl.when(at == 0)
        def _():
            swap_state.wait_recv()

        @pl.when(at % per_seq == 0)
        def _():
            carry[...] = state_in[at // per_seq].astype(WIDE) * own[-1].astype(WIDE)

        marks = head_rows()
        causal, _ = causal_masks()
        prefix[0] = carry[...].astype(LOW)
        for g in groups(width):
            q, k, v = queries[:, g], all_keys[here, g], all_values[here, g]
            scores = (dot_nt(q, split_heads(k, marks)) * causal).astype(LOW)
            out = dot_nn(scores, split_heads(v, marks))
            out += dot_nn(q, open_state(carry[:, g], same))
            attended[:, g] = out.astype(LOW)
            carry[:, g] += pack_state(dot_tn(k, v), same)
        rows = attended[...].astype(WIDE)
        rows = rows * rms_scale(rows) * gain_row[...] * jax.nn.sigmoid(gate)
        rows = rows.astype(LOW)
        mixed[...] = rows.T
        residual[...] = tok[...].astype(WIDE) + dot_nn(rows, weight(4))

    @pl.when(step == 2 * steps - 1)
    def _():
        feed_advance(4)
        for piece in feed:
            piece.finish()
        three.finish()
        for piece in [p for wave in attn for p in wave] + feed + [three]:
            piece.drain()
        swap_three.wait_send()
        swap_state.wait_send()
        keep_attn.wait()


def tile_cuts(start, tiles):
    cuts = []
    for count in tiles:
        cuts.append(slice(start, start + 128 * count))
        start += 128 * count
    return cuts


def forward(tok, seq_count, shards_attn, gain_columns, s_one, s_two, s_three):
    row_count, width = tok.shape
    hidden = s_one.shape[1]
    steps = row_count // BLOCK
    per_seq = steps // seq_count
    bits = index_bits()
    orders = [[(s[0], s[1]) for s in reversed(order)] for order in stream_orders()]
    third = width // 128
    waves = [
        list(zip(orders, tile_cuts(0, (6, 5, 5)))),
        list(zip(orders, tile_cuts(2 * width, (5, 6, 5)))),
        list(zip(orders, tile_cuts(4 * width, (3, 3, 3)))),
    ]
    feed_orders = [orders[0], orders[2]]
    three_order = [bit for bit in orders[1] if bit != bits[-1]]
    lead = (2,) * len(bits)
    slab = s_one.shape[0]
    deep = s_three.shape[0]
    in_rows = pl.BlockSpec((BLOCK, width), lambda i: (i % steps, 0))
    first = pl.BlockSpec((BLOCK, width), lambda i: (jnp.minimum(i, steps - 1), 0))
    second = pl.BlockSpec((BLOCK, width), lambda i: (jnp.maximum(i - steps, 0), 0))
    first_turned = pl.BlockSpec((width, BLOCK), lambda i: (0, jnp.minimum(i, steps - 1)))
    second_turned = pl.BlockSpec((width, BLOCK), lambda i: (0, jnp.maximum(i - steps, 0)))
    turned_low = jax.ShapeDtypeStruct((width, row_count), LOW)
    any_spec = pl.BlockSpec(memory_space=pl.ANY)
    vmem = pl.BlockSpec(memory_space=pltpu.VMEM)
    rows_low = jax.ShapeDtypeStruct((row_count, width), LOW)

    def shape(*dims, dtype=LOW):
        return jax.ShapeDtypeStruct(dims, dtype)

    kernel = functools.partial(
        forward_kernel, steps, per_seq, bits, waves, feed_orders, three_order
    )
    out = pl.pallas_call(
        kernel,
        grid=(2 * steps,),
        in_specs=[in_rows] + [vmem] * 6 + [any_spec] * 2 + [vmem],
        out_specs=[first_turned] + [first] * 3 + [second] * 4 + [second_turned, second]
        + [
            pl.BlockSpec((1, HD, width), lambda i: (jnp.maximum(i - steps, 0), 0, 0)),
            pl.BlockSpec((1, width), lambda i: (0, 0)),
        ]
        + [any_spec] * 4,
        out_shape=[turned_low] + [rows_low] * 7 + [turned_low]
        + [
            shape(row_count, width, dtype=WIDE),
            shape(steps, HD, width),
            shape(1, width, dtype=WIDE),
            shape(*lead, slab, 5 * width + 128),
            shape(*lead, slab, hidden),
            shape(*lead, slab, hidden),
            shape(*lead[:-1], 2 * deep, width),
        ],
        scratch_shapes=[
            pltpu.VMEM(lead + (slab, 5 * width + 128), LOW),
            pltpu.VMEM((row_count, width), LOW),
            pltpu.VMEM((row_count, width), LOW),
            pltpu.VMEM((row_count, width), LOW),
            pltpu.VMEM((seq_count, HD, width), WIDE),
            pltpu.VMEM((seq_count, HD, width), LOW),
            pltpu.VMEM((seq_count, HD, width), LOW),
            pltpu.VMEM((HD, width), WIDE),
            pltpu.VMEM((deep, width), WIDE),
            pltpu.VMEM((2 * deep, width), LOW),
            pltpu.SemaphoreType.DMA((FORWARD_COPIES,)),
            pltpu.SemaphoreType.DMA((FORWARD_COPIES,)),
            pltpu.SemaphoreType.DMA((4,)),
        ],
        compiler_params=pltpu.CompilerParams(
            dimension_semantics=("arbitrary",),
            vmem_limit_bytes=58 << 20,
            collective_id=1,
            has_side_effects=True,
        ),
        cost_estimate=pl.CostEstimate(
            flops=16 * row_count * width * width, bytes_accessed=64 << 20, transcendentals=0
        ),
    )(tok, *shards_attn, gain_columns, s_one, s_two, s_three.astype(WIDE))
    return list(out[:12]) + [
        out[12].reshape(-1, 5 * width + 128),
        out[13].reshape(-1, hidden),
        out[14].reshape(-1, hidden),
        out[15].reshape(-1, width),
    ]


def plain_shards(
    tokens,
    lengths,
    w_query,
    w_key,
    w_value,
    w_gate,
    out_gain,
    w_out,
    w_one,
    w_two,
    w_three,
    cotangent,
):
    seq_count, local_length, width = tokens.shape
    row_count = seq_count * local_length
    hidden = w_one.shape[1]
    steps = row_count // BLOCK
    per_seq = local_length // BLOCK
    orders = stream_orders()
    tok = tokens.reshape(row_count, width)
    cot = cotangent.reshape(row_count, width)
    limits = lengths - lax.axis_index("fsdp") * local_length
    full_key = gather_rows(w_key, orders[0])
    full_value = gather_rows(w_value, orders[1])
    full_query = gather_rows(w_query, orders[2])
    full_gate = gather_rows(w_gate, orders[0])
    gain_columns = jnp.broadcast_to(out_gain[:, None], (out_gain.shape[0], 128))
    full_out = gather_rows(jnp.concatenate([w_out, gain_columns], axis=1), orders[1])
    full_one = gather_rows(w_one, orders[2])
    full_two = gather_rows(w_two, orders[0])
    full_three = gather_rows(w_three, orders[1])
    gain = full_out[:, width].astype(WIDE)[None, :]
    full_out = full_out[:, :width]

    rows = rows_spec(width)
    narrow = ((row_count, width), LOW, rows)
    wide = ((row_count, width), WIDE, rows)
    big = ((row_count, hidden), LOW, rows_spec(hidden))
    state_spec = pl.BlockSpec((1, HD, width), lambda i: (i // per_seq, 0, 0))
    state = ((seq_count, HD, width), WIDE, state_spec)
    square = 2 * row_count * width * width

    normed_low, pre_key, keys, values, totals = call(
        lambda *refs: key_value_kernel(per_seq, *refs),
        steps,
        [(tok, rows), (full_key, whole_spec(full_key)), (full_value, whole_spec(full_value))],
        [narrow, narrow, narrow, narrow, state],
        flops=2 * square,
    )
    incoming = shift_sum(totals, "fsdp", False)
    pre_query, queries, pre_gate = call(
        query_gate_kernel,
        steps,
        [(normed_low, rows), (full_query, whole_spec(full_query)), (full_gate, whole_spec(full_gate))],
        [narrow, narrow, narrow],
        flops=2 * square,
    )
    prefix_spec = pl.BlockSpec((1, HD, width), lambda i: (i, 0, 0))
    attended, mixed, residual, prefix = call(
        lambda *refs: attend_kernel(per_seq, *refs),
        steps,
        [(queries, rows), (keys, rows), (values, rows), (pre_gate, rows), (tok, rows),
         (incoming, state_spec), (gain, whole_spec(gain)), (full_out, whole_spec(full_out))],
        [narrow, narrow, wide, ((steps, HD, width), LOW, prefix_spec)],
        scratch=[pltpu.VMEM((HD, width), WIDE)],
        flops=3 * square,
    )
    (
        layer_out, normed_two, glu, grad_up_one, grad_up_two, upstream_low, grad_residual,
        grad_residual_low, grad_pre_gate, grad_attended, grad_totals, grad_gain_term,
    ) = call(
        lambda *refs: feed_kernel(per_seq, False, *refs),
        steps,
        [(limits, pl.BlockSpec(memory_space=pltpu.SMEM)), (residual, rows), (cot, rows),
         (full_one, whole_spec(full_one)), (full_two, whole_spec(full_two)),
         (full_three, whole_spec(full_three)), (full_out, whole_spec(full_out)),
         (gain, whole_spec(gain)), (pre_gate, rows), (attended, rows), (queries, rows)],
        [narrow, narrow, big, big, big, narrow, wide, narrow, narrow, narrow, state,
         ((1, width), WIDE, pl.BlockSpec((1, width), lambda i: (0, 0)))],
        flops=12 * row_count * width * hidden + square,
    )
    outgoing = shift_sum(grad_totals, "fsdp", True)
    grad_one = scatter_rows(dot_tn(normed_two, grad_up_one), orders[1])
    grad_two = scatter_rows(dot_tn(normed_two, grad_up_two), orders[2])
    grad_three = scatter_rows(dot_tn(glu, upstream_low), orders[0])
    gain_term = jnp.broadcast_to(grad_gain_term.reshape(width, 1), (width, 128))
    grad_out = scatter_rows(
        jnp.concatenate([dot_tn(mixed, grad_residual_low), gain_term], axis=1), orders[1]
    )
    grad_gain = grad_out[:, width]
    grad_out = grad_out[:, :width]

    def back(i):
        return (i // per_seq) * per_seq + per_seq - 1 - i % per_seq

    back_rows = rows_spec(width, order=back)
    back_narrow = ((row_count, width), LOW, back_rows)
    grad_pre_query, grad_pre_key, grad_pre_value = call(
        lambda *refs: attend_back_kernel(per_seq, *refs),
        steps,
        [(queries, back_rows), (keys, back_rows), (values, back_rows),
         (grad_attended, back_rows), (pre_query, back_rows), (pre_key, back_rows),
         (prefix, pl.BlockSpec((1, HD, width), lambda i: (back(i), 0, 0))),
         (outgoing, state_spec)],
        [back_narrow, back_narrow, back_narrow],
        scratch=[pltpu.VMEM((HD, width), WIDE)],
        flops=6 * square,
    )
    grad_query = scatter_rows(dot_tn(normed_low, grad_pre_query), orders[0])
    grad_key = scatter_rows(dot_tn(normed_low, grad_pre_key), orders[1])
    grad_value = scatter_rows(dot_tn(normed_low, grad_pre_value), orders[2])
    grad_gate = scatter_rows(dot_tn(normed_low, grad_pre_gate), orders[0])
    (input_grad,) = call(
        input_kernel,
        steps,
        [(grad_pre_query, rows), (grad_pre_key, rows), (grad_pre_value, rows),
         (grad_pre_gate, rows), (full_query, whole_spec(full_query)),
         (full_key, whole_spec(full_key)), (full_value, whole_spec(full_value)),
         (full_gate, whole_spec(full_gate)), (tok, rows), (grad_residual, rows)],
        [wide],
        flops=4 * square,
    )
    return (
        layer_out.reshape(tokens.shape),
        input_grad.reshape(tokens.shape),
        grad_query,
        grad_key,
        grad_value,
        grad_gate,
        grad_gain,
        grad_out,
        grad_one,
        grad_two,
        grad_three,
    )


def fused_shards(
    tokens,
    lengths,
    w_query,
    w_key,
    w_value,
    w_gate,
    out_gain,
    w_out,
    w_one,
    w_two,
    w_three,
    cotangent,
):
    seq_count, local_length, width = tokens.shape
    row_count = seq_count * local_length
    hidden = w_one.shape[1]
    steps = row_count // BLOCK
    per_seq = local_length // BLOCK
    orders = stream_orders()
    tok = tokens.reshape(row_count, width)
    cot = cotangent.reshape(row_count, width)
    limits = lengths - lax.axis_index("fsdp") * local_length
    gain_columns = jnp.broadcast_to(out_gain[:, None], (out_gain.shape[0], 128))
    rows = rows_spec(width)
    narrow = ((row_count, width), LOW, rows)
    wide = ((row_count, width), WIDE, rows)

    def turned_rows(size):
        return pl.BlockSpec((size, BLOCK), lambda i: (0, i))

    turned = ((width, row_count), LOW, turned_rows(width))
    big = ((row_count, hidden), LOW, rows_spec(hidden))
    state_spec = pl.BlockSpec((1, HD, width), lambda i: (i // per_seq, 0, 0))
    state = ((seq_count, HD, width), WIDE, state_spec)
    square = 2 * row_count * width * width

    (
        normed_low, pre_key, keys, values, pre_query, queries, pre_gate, attended, mixed,
        residual, prefix, gain, full_attn, full_one, full_two, full_three,
    ) = forward(
        tok, seq_count, (w_key, w_value, w_query, w_gate, w_out), gain_columns, w_one, w_two, w_three
    )

    def part(n):
        return pl.BlockSpec((width, width), lambda i: (0, n), pipeline_mode=pl.Buffered(1))

    (
        layer_out, normed_two, glu, grad_up_one, grad_up_two, upstream_low, grad_residual,
        grad_residual_low, grad_pre_gate, grad_attended, grad_totals, grad_gain_term,
    ) = call(
        lambda *refs: feed_kernel(per_seq, True, *refs),
        steps,
        [(limits, pl.BlockSpec(memory_space=pltpu.SMEM)), (residual, rows), (cot, rows),
         (full_one, whole_spec(full_one)), (full_two, whole_spec(full_two)),
         (full_three, whole_spec(full_three)), (full_attn, part(4)),
         (gain, whole_spec(gain)), (pre_gate, rows), (attended, rows), (queries, rows)],
        [narrow, turned, ((hidden, row_count), LOW, turned_rows(hidden)), big, big, narrow, wide, narrow, narrow, narrow, state,
         ((1, width), WIDE, pl.BlockSpec((1, width), lambda i: (0, 0)))],
        scratch=[pltpu.VMEM((BLOCK, hidden), LOW)],
        flops=12 * row_count * width * hidden + square,
    )
    grad_one, grad_two, grad_three, grad_pre_query, grad_pre_key, grad_pre_value = feed_back(
        seq_count, normed_two, grad_up_one, grad_up_two, glu, upstream_low, queries, keys, values,
        grad_attended, pre_query, pre_key, prefix, grad_totals,
    )
    grads, input_grad = attend_weights(
        normed_low, mixed, grad_residual_low, grad_pre_query, grad_pre_key, grad_pre_value,
        grad_pre_gate, grad_gain_term, full_attn, tok, grad_residual,
    )
    grad_out, grad_gain = grads[:, :width], grads[:, width]
    grad_query, grad_key, grad_value, grad_gate = (
        grads[:, 128 + n * width : 128 + (n + 1) * width] for n in range(1, 5)
    )
    return (
        layer_out.reshape(tokens.shape),
        input_grad.reshape(tokens.shape),
        grad_query,
        grad_key,
        grad_value,
        grad_gate,
        grad_gain,
        grad_out,
        grad_one,
        grad_two,
        grad_three,
    )


def shards(*arrays):
    tokens, w_query, w_three = arrays[0], arrays[2], arrays[10]
    sizes = (lax.axis_size("dp"), lax.axis_size("fsdp"))
    fits = w_query.shape[0] % 16 == 0 and w_three.shape[0] % 8 == 0 and tokens.shape[1] >= 4 * BLOCK
    if sizes == (16, 2) and fits:
        return fused_shards(*arrays)
    return plain_shards(*arrays)


def solution(mesh):
    in_specs = (
        P("dp", "fsdp", None),
        P("dp"),
        P(("dp", "fsdp"), None),
        P(("dp", "fsdp"), None),
        P(("dp", "fsdp"), None),
        P(("dp", "fsdp"), None),
        P(("dp", "fsdp")),
        P(("dp", "fsdp"), None),
        P(("dp", "fsdp"), None),
        P(("dp", "fsdp"), None),
        P(("dp", "fsdp"), None),
        P("dp", "fsdp", None),
    )
    out_specs = (
        P("dp", "fsdp", None),
        P("dp", "fsdp", None),
        P(("dp", "fsdp"), None),
        P(("dp", "fsdp"), None),
        P(("dp", "fsdp"), None),
        P(("dp", "fsdp"), None),
        P(("dp", "fsdp")),
        P(("dp", "fsdp"), None),
        P(("dp", "fsdp"), None),
        P(("dp", "fsdp"), None),
        P(("dp", "fsdp"), None),
    )
    return jax.shard_map(shards, mesh=mesh, in_specs=in_specs, out_specs=out_specs, check_vma=False)
```

```python
import functools

import jax
import jax.numpy as jnp
from jax import lax
from jax.experimental import pallas as pl
from jax.experimental.pallas import tpu as pltpu
from jax.sharding import PartitionSpec as P

HD = 64
H = 16
BLOCK = 256


GROUP = 256
HEADS = GROUP // HD
LOW = jnp.bfloat16
WIDE = jnp.float32

norm_epsilon = 1e-06


def bit_steps():
    steps = []
    for axis in ("dp", "fsdp"):
        size = lax.axis_size(axis)
        bit = 0
        while (1 << bit) < size:
            steps.append((axis, bit, [(i, i ^ (1 << bit)) for i in range(size)]))
            bit += 1
    return steps


def stream_orders():
    steps = bit_steps()
    dp = [s for s in steps if s[0] == "dp"]
    fs = [s for s in steps if s[0] == "fsdp"]
    core, rest = dp[0], fs[:1] + dp[1:3]
    tail = dp[3:] + fs[1:]
    return [[core] + rest[k:] + rest[:k] + tail for k in range(3)]


def own_bit(step):
    axis, bit, _ = step
    return lax.rem(lax.div(lax.axis_index(axis), 1 << bit), 2)


def bit_dims():
    steps = bit_steps()
    dp = sorted([s for s in steps if s[0] == "dp"], key=lambda s: -s[1])
    fs = sorted([s for s in steps if s[0] == "fsdp"], key=lambda s: -s[1])
    return [(s[0], s[1]) for s in dp + fs]


def gather_rows(shard, order):
    dims = bit_dims()
    held = []
    data = shard
    for step in reversed(order):
        axis, bit, perm = step
        other = lax.ppermute(data, axis, perm)
        mine = own_bit(step) == 0
        place = sum(1 for d in held if dims.index(d) < dims.index((axis, bit)))
        held.append((axis, bit))
        data = jnp.stack(
            [jnp.where(mine, data, other), jnp.where(mine, other, data)], axis=place
        )
    return data.reshape((-1,) + shard.shape[1:])


def scatter_rows(full, order):
    dims = bit_dims()
    rows = full.shape[0] >> len(dims)
    data = full.astype(jnp.bfloat16).reshape((2,) * len(dims) + (rows,) + full.shape[1:])
    left = list(dims)
    for at, step in enumerate(order):
        axis, bit, perm = step
        place = left.index((axis, bit))
        left.pop(place)
        own = own_bit(step)
        send = lax.dynamic_index_in_dim(data, 1 - own, place, keepdims=False)
        keep = lax.dynamic_index_in_dim(data, own, place, keepdims=False)
        come = lax.ppermute(send, axis, perm)
        data = keep.astype(jnp.float32) + come.astype(jnp.float32)
        if at < len(order) - 1:
            data = data.astype(jnp.bfloat16)
    return data


def shift_sum(x, axis, reverse):
    size = lax.axis_size(axis)
    total = jnp.zeros_like(x)
    low = x.astype(jnp.bfloat16)
    for s in range(1, size):
        pairs = [(i + s, i) if reverse else (i, i + s) for i in range(size - s)]
        total = total + lax.ppermute(low, axis, pairs).astype(x.dtype)
    return total


def dot_nn(a, b):
    return jnp.dot(a, b, preferred_element_type=WIDE)


def dot_nt(a, b):
    return lax.dot_general(a, b, (((1,), (1,)), ((), ())), preferred_element_type=WIDE)


def dot_tn(a, b):
    return lax.dot_general(a, b, (((0,), (0,)), ((), ())), preferred_element_type=WIDE)


def rms_scale(values):
    return lax.rsqrt(jnp.mean(values * values, axis=-1, keepdims=True) + norm_epsilon)


def norm_back(values, scale, upstream):
    inner_mean = jnp.mean(upstream * values, axis=-1, keepdims=True)
    return scale * (upstream - values * (scale * scale) * inner_mean)


def silu_slope(pre_rows):
    logistic = jax.nn.sigmoid(pre_rows)
    return logistic * (1.0 + pre_rows * (1.0 - logistic))


def head_square():
    row = lax.broadcasted_iota(jnp.int32, (GROUP, GROUP), 0) // HD
    col = lax.broadcasted_iota(jnp.int32, (GROUP, GROUP), 1) // HD
    return (row == col).astype(WIDE)


def head_rows():
    lane = lax.broadcasted_iota(jnp.int32, (1, GROUP), 1) // HD
    return [(lane == h).astype(WIDE).astype(LOW) for h in range(HEADS)]


def split_heads(rows, marks):
    return jnp.concatenate([rows * mark for mark in marks], axis=0)


def pack_state(square, same):
    return jnp.sum((square * same).reshape(HEADS, HD, GROUP), axis=0)


def open_state(packed, same):
    return (jnp.concatenate([packed] * HEADS, axis=0) * same).astype(LOW)


def causal_masks():
    i = lax.broadcasted_iota(jnp.int32, (BLOCK, HEADS * BLOCK), 0)
    j = lax.broadcasted_iota(jnp.int32, (BLOCK, HEADS * BLOCK), 1) % BLOCK
    return (i >= j).astype(WIDE), (j >= i).astype(WIDE)


def groups(width):
    return [slice(g * GROUP, (g + 1) * GROUP) for g in range(width // GROUP)]


def key_value_kernel(per_seq, tok, w_key, w_value, normed, pre_key, keys, values, totals):
    x = tok[...].astype(WIDE)
    rows = (x * rms_scale(x)).astype(LOW)
    normed[...] = rows
    pre = dot_nn(rows, w_key[...])
    pre_key[...] = pre.astype(LOW)
    k = jax.nn.silu(pre).astype(LOW)
    keys[...] = k
    v = dot_nn(rows, w_value[...]).astype(LOW)
    values[...] = v

    @pl.when(pl.program_id(0) % per_seq == 0)
    def _():
        totals[...] = jnp.zeros_like(totals)

    same = head_square()
    for g in groups(k.shape[1]):
        totals[0, :, g] += pack_state(dot_tn(k[:, g], v[:, g]), same)


def query_gate_kernel(normed, w_query, w_gate, pre_query, queries, pre_gate):
    rows = normed[...]
    pre = dot_nn(rows, w_query[...])
    pre_query[...] = pre.astype(LOW)
    queries[...] = jax.nn.silu(pre).astype(LOW)
    pre_gate[...] = dot_nn(rows, w_gate[...]).astype(LOW)


def attend_kernel(
    per_seq, queries, keys, values, pre_gate, tok, incoming, gain, w_out,
    attended, mixed, residual, prefix, carry,
):
    @pl.when(pl.program_id(0) % per_seq == 0)
    def _():
        carry[...] = incoming[0]

    same, marks = head_square(), head_rows()
    causal, _ = causal_masks()
    prefix[0] = carry[...].astype(LOW)
    for g in groups(queries.shape[1]):
        q, k, v = queries[:, g], keys[:, g], values[:, g]
        scores = (dot_nt(q, split_heads(k, marks)) * causal).astype(LOW)
        out = dot_nn(scores, split_heads(v, marks))
        out += dot_nn(q, open_state(carry[:, g], same))
        attended[:, g] = out.astype(LOW)
        carry[:, g] += pack_state(dot_tn(k, v), same)
    rows = attended[...].astype(WIDE)
    gate = jax.nn.sigmoid(pre_gate[...].astype(WIDE))
    rows = (rows * rms_scale(rows) * gain[...] * gate).astype(LOW)
    mixed[...] = rows
    residual[...] = tok[...].astype(WIDE) + dot_nn(rows, w_out[...])


def feed_kernel(
    per_seq, turned, lengths, residual, cotangent, w_one, w_two, w_three, w_out, gain, pre_gate,
    attended, queries,
    layer_out, normed, glu, grad_one, grad_two, upstream_low, grad_residual, gated,
    grad_attended, totals, grad_gain, held=None,
):
    step = pl.program_id(0)
    row_count = residual.shape[0]
    spot = lax.broadcasted_iota(jnp.int32, (row_count, 1), 0) + (step % per_seq) * row_count
    limit = lengths[step // per_seq] - lax.axis_index("fsdp") * per_seq * row_count
    valid = (spot < limit).astype(WIDE)
    res = residual[...]
    scale = rms_scale(res)
    rows = (res * scale).astype(LOW)
    normed[...] = rows.T if turned else rows
    upstream = cotangent[...].astype(WIDE) * valid
    up_low = upstream.astype(LOW)
    upstream_low[...] = up_low
    for c in groups(w_one.shape[1]):
        one = dot_nn(rows, w_one[:, c])
        two = dot_nn(rows, w_two[:, c])
        back = dot_nt(up_low, w_three[c, :])
        product = (one * two).astype(LOW)
        if turned:
            held[:, c] = product
            glu[c, :] = product.T
        else:
            glu[:, c] = product
        grad_one[:, c] = (back * two).astype(LOW)
        grad_two[:, c] = (back * one).astype(LOW)
    layer_out[...] = (valid * (res + dot_nn(held[...] if turned else glu[...], w_three[...]))).astype(LOW)
    back = dot_nt(grad_one[...], w_one[...]) + dot_nt(grad_two[...], w_two[...])
    grad = upstream + norm_back(res, scale, back)
    grad_residual[...] = grad
    grad = grad.astype(LOW)
    width = grad.shape[1]
    gated[:, :width] = grad
    grad = dot_nt(grad, w_out[...])
    gate = jax.nn.sigmoid(pre_gate[...].astype(WIDE))
    att = attended[...].astype(WIDE)
    scale = rms_scale(att)
    hat = att * scale
    grad = grad * gate

    @pl.when(step == 0)
    def _():
        grad_gain[...] = jnp.zeros_like(grad_gain)

    grad_gain[...] += jnp.sum(grad * hat, axis=0, keepdims=True)
    grad = grad * gain[...]
    gated[:, width:] = (grad * hat * (1.0 - gate)).astype(LOW)
    grad_att = norm_back(att, scale, grad).astype(LOW)
    grad_attended[...] = grad_att

    @pl.when(step % per_seq == 0)
    def _():
        totals[...] = jnp.zeros_like(totals)

    same = head_square()
    for g in groups(grad_att.shape[1]):
        totals[0, :, g] += pack_state(dot_tn(queries[:, g], grad_att[:, g]), same)


def attend_back_kernel(
    per_seq, queries, keys, values, grad_attended, pre_query, pre_key, prefix, incoming,
    grad_query, grad_key, grad_value, carry,
):
    @pl.when(pl.program_id(0) % per_seq == 0)
    def _():
        carry[...] = incoming[0]

    same, marks = head_square(), head_rows()
    causal, causal_t = causal_masks()
    for g in groups(queries.shape[1]):
        q, k, v, ga = queries[:, g], keys[:, g], values[:, g], grad_attended[:, g]
        qs, ks, vs, gs = (split_heads(rows, marks) for rows in (q, k, v, ga))
        state = open_state(prefix[0, :, g].astype(WIDE), same)
        grad_state = open_state(carry[:, g], same)
        grad_scores = (dot_nt(ga, vs) * causal).astype(LOW)
        gq = dot_nn(grad_scores, ks) + dot_nt(ga, state)
        grad_scores = (dot_nt(v, gs) * causal_t).astype(LOW)
        gk = dot_nn(grad_scores, qs) + dot_nt(v, grad_state)
        scores = (dot_nt(k, qs) * causal_t).astype(LOW)
        gv = dot_nn(scores, gs) + dot_nn(k, grad_state)
        grad_query[:, g] = (gq * silu_slope(pre_query[:, g].astype(WIDE))).astype(LOW)
        grad_key[:, g] = (gk * silu_slope(pre_key[:, g].astype(WIDE))).astype(LOW)
        grad_value[:, g] = gv.astype(LOW)
        carry[:, g] += pack_state(dot_tn(q, ga), same)


def input_kernel(
    grad_query, grad_key, grad_value, grad_gate, w_query, w_key, w_value, w_gate, tok,
    grad_residual, input_grad,
):
    grad = dot_nt(grad_query[...], w_query[...]) + dot_nt(grad_key[...], w_key[...])
    grad += dot_nt(grad_value[...], w_value[...]) + dot_nt(grad_gate[...], w_gate[...])
    x = tok[...].astype(WIDE)
    input_grad[...] = grad_residual[...] + norm_back(x, rms_scale(x), grad)


def rows_spec(width, block=BLOCK, order=lambda i: i):
    return pl.BlockSpec((block, width), lambda i: (order(i), 0))


def whole_spec(array):
    rank = array.ndim
    return pl.BlockSpec(array.shape, lambda i: (0,) * rank, pipeline_mode=pl.Buffered(1))


def call(kernel, steps, operands, results, scratch=(), flops=0, limit=56):
    moved = sum(a.size * a.dtype.itemsize for a, _ in operands)
    return pl.pallas_call(
        kernel,
        grid=(steps,),
        in_specs=[spec for _, spec in operands],
        out_specs=[spec for _, _, spec in results],
        out_shape=[jax.ShapeDtypeStruct(shape, dtype) for shape, dtype, _ in results],
        scratch_shapes=list(scratch),
        compiler_params=pltpu.CompilerParams(
            dimension_semantics=("arbitrary",), vmem_limit_bytes=limit << 20
        ),
        cost_estimate=pl.CostEstimate(flops=flops, bytes_accessed=moved, transcendentals=0),
    )(*[a for a, _ in operands])


def index_bits():
    bits = []
    for axis in ("dp", "fsdp"):
        count = lax.axis_size(axis).bit_length() - 1
        bits += [(axis, bit) for bit in reversed(range(count))]
    return bits


LINKS = {
    "1": (("dp", 3),),
    "0": (("dp", 2),),
    "z": (("dp", 3), ("dp", 2)),
    "y": (("dp", 1),),
    "x": (("fsdp", 0),),
}
CORE = ("dp", 0)
SIDE = ("fsdp", 0)


def bit_value(bit):
    axis, at = bit
    return lax.rem(lax.div(lax.axis_index(axis), 1 << at), 2)


def flips_of(name):
    group = LINKS[name]
    if len(group) == 1:
        return [group]
    return [group[:1], group[1:], group]


def flip_device(flips):
    place = {}
    for axis, at in flips:
        moved = place.get(axis, lax.axis_index(axis))
        place[axis] = moved + (1 - 2 * bit_value((axis, at))) * (1 << at)
    return place


def greet(bits, far=True):
    partners = [(bit,) for bit in bits] + ([LINKS["z"]] if far else [])
    barrier = pltpu.get_barrier_semaphore()
    for flips in partners:
        pl.semaphore_signal(
            barrier, inc=1, device_id=flip_device(flips), device_id_type=pl.DeviceIdType.MESH
        )
    pl.semaphore_wait(barrier, len(partners))


class Sems:
    def __init__(self, send, recv):
        self.send, self.recv, self.used = send, recv, 0

    def copy(self, src, dst, flips):
        at = self.used
        self.used += 1
        return pltpu.make_async_remote_copy(
            src_ref=src,
            dst_ref=dst,
            send_sem=self.send.at[at],
            recv_sem=self.recv.at[at],
            device_id=flip_device(flips),
            device_id_type=pl.DeviceIdType.MESH,
        )


class Gather:
    def __init__(self, buf, bits, order, sems, columns=slice(None)):
        self.stages, held = [], []

        def cube(flips=()):
            index = []
            for bit in bits:
                if bit in held:
                    index.append(slice(None))
                else:
                    index.append(1 - bit_value(bit) if bit in flips else bit_value(bit))
            return buf.at[tuple(index) + (slice(None), columns)]

        for n, name in enumerate(order):
            ref, flips = cube(), flips_of(name)
            self.stages.append([sems.copy(ref, ref, flip) for flip in flips])
            if n == len(order) - 1:
                self.near = sems.copy(ref, ref, (CORE,))
                far = [cube(flip) for flip in flips]
                self.stages.append([sems.copy(ref, ref, (CORE,)) for ref in far])
            held.extend(LINKS[name])

    def start(self, k):
        for copy in self.stages[k]:
            copy.start()
        if k == len(self.stages) - 2:
            self.near.start()

    def advance(self, k):
        if k:
            for copy in self.stages[k - 1]:
                copy.wait_recv()
        self.start(k)

    def finish(self):
        self.near.wait_recv()
        for copy in self.stages[-1]:
            copy.wait_recv()

    def drain(self):
        for copy in [c for stage in self.stages for c in stage] + [self.near]:
            copy.wait_send()


class Scatter:
    def __init__(self, sems, bits, order, acc, send, come, recvs, columns, slots):
        self.bits, self.order, self.acc, self.columns = bits, order, acc, columns
        self.come, self.recvs, self.slots = come, recvs, slots
        rows = (slice(None),)
        full = (slice(None),) * len(bits) + rows
        self.core = sems.copy(send.at[full + (slots,)], come.at[full + (slots,)], (CORE,))
        self.copies, self.done = [], []
        for k, name in enumerate(order):
            (bit,) = LINKS[name]
            done = [LINKS[n][0] for n in order[:k]]
            index = tuple(
                1 - bit_value(b) if b == bit else bit_value(b) if b in done else slice(None)
                for b in bits
            )
            free = (slice(None),) * (len(bits) - k - 1)
            source = acc.at[index + rows + (columns,)]
            self.copies.append(sems.copy(source, recvs[k].at[free + rows + (columns,)], (bit,)))
            self.done.append(done)

    def add(self, done, source, columns):
        free = [b for b in self.bits if b not in done]

        def one(k):
            at = [(k // (1 << (len(free) - 1 - n))) % 2 for n in range(len(free))]
            mine = tuple(bit_value(b) if b in done else at[free.index(b)] for b in self.bits)
            here = mine + (slice(None), self.columns)
            self.acc[here] = self.acc[here] + source[tuple(at) + (slice(None), columns)]

        if len(free) <= 2:
            for k in range(1 << len(free)):
                one(k)
        else:
            lax.fori_loop(0, 1 << len(free), lambda k, c: (one(k), c)[1], 0)

    def launch(self):
        self.core.start()

    def advance(self, k):
        if k == 0:
            self.core.wait_recv()
            self.add([], self.come, self.slots)
        else:
            self.copies[k - 1].wait_recv()
            self.add(self.done[k - 1] + [LINKS[self.order[k - 1]][0]], self.recvs[k - 1], self.columns)
        self.copies[k].start()

    def result(self):
        self.copies[-1].wait_recv()
        own = tuple(bit_value(b) for b in self.bits)
        here = (slice(None), self.columns)
        return self.acc[own + here].astype(WIDE) + self.recvs[-1][here].astype(WIDE)

    def drain(self, core=True):
        if core:
            self.core.wait_send()
        for copy in self.copies:
            copy.wait_send()


def run_events(step, events):
    for at in sorted(events):

        @pl.when(step == at)
        def _():
            for action in events[at]:
                action()


def planned(table, pieces, low, high):
    events = {}
    for at, todo in table:
        if low <= at < high:
            events[at] = [functools.partial(pieces[name].advance, k) for name, k in todo]
    return events


FORWARD_PLAN = (
    (0, (
        ("a00", 0), ("a01", 0), ("a11", 0), ("f5", 0), ("f0", 0), ("f4", 0), ("a02", 0),
        ("a00", 1), ("a01", 1), ("a10", 0), ("a12", 0), ("a02", 1), ("a00", 2), ("a11", 1),
        ("a01", 2), ("a12", 1), ("a02", 2), ("a11", 2), ("a20", 0), ("a12", 2), ("a21", 0),
        ("a10", 1), ("a22", 0), ("a20", 1), ("a00", 3), ("a21", 1), ("f1", 0), ("f3", 0),
        ("a11", 3), ("a20", 2), ("a01", 3), ("a02", 3), ("f5", 1), ("a12", 3), ("a10", 2),
        ("f1", 1), ("a22", 1), ("f3", 1), ("a11", 4), ("a00", 4), ("a21", 2),
    )),
    (1, (("a20", 3), ("a12", 4), ("f0", 1), ("f2", 0))),
    (2, (("f1", 2),)),
    (3, (("f5", 2),)),
    (4, (("a22", 2),)),
    (5, (("f3", 2),)),
    (6, (("a20", 4), ("f2", 1))),
    (7, (("a21", 3),)),
    (8, (("f0", 2), ("a22", 3), ("f1", 3), ("a10", 3), ("a21", 4))),
    (9, (("f2", 2), ("f4", 1))),
    (10, (("f5", 3), ("f2", 3))),
    (11, (("f3", 3), ("f1", 4))),
    (12, (("f0", 3),)),
    (13, (("f4", 2),)),
    (14, (("f2", 4), ("f5", 4))),
    (16, (("f4", 3), ("f0", 4), ("f3", 4))),
)
FEED_BACK_PLAN = (
    (7, (("one0", 0), ("two0", 0))),
    (13, (("one0", 1), ("two0", 1))),
    (15, (("three0", 0), ("three1", 0))),
    (16, (("one0", 2),)),
    (17, (("two0", 2),)),
    (18, (("one1", 0), ("two1", 0), ("two0", 3))),
    (20, (("one0", 3), ("one2", 0))),
    (21, (("two2", 0), ("three1", 1), ("three0", 1))),
    (24, (("one1", 1), ("two1", 1), ("one2", 1))),
    (25, (("three1", 2), ("two2", 1), ("three0", 2))),
    (26, (("one1", 2), ("three0", 3), ("one2", 2))),
    (27, (
        ("three1", 3), ("two1", 2), ("two2", 2), ("one2", 3), ("one1", 3), ("two1", 3),
        ("two2", 3),
    )),
)
ATTEND_BACK_PLAN = (
    (4, (("p0", 0),)),
    (6, (("p1", 0), ("p2", 0))),
    (9, (("p3", 0), ("p0", 1), ("p2", 1), ("p4", 0))),
    (10, (("p5", 0),)),
    (11, (("p1", 1), ("p6", 0))),
    (12, (("p2", 2),)),
    (14, (("p2", 3), ("p4", 1), ("p0", 2), ("p3", 1), ("p5", 1))),
    (15, (("p1", 2), ("p6", 1))),
    (16, (("p4", 2), ("p0", 3), ("p3", 2), ("p5", 2))),
    (17, (("p4", 3), ("p1", 3), ("p6", 2))),
    (18, (("p6", 3), ("p5", 3), ("p3", 3))),
)


def attend_back_step(
    same, queries, keys, values, grad_attended, pre_query, pre_key, prefix, grads, carry,
):
    marks = head_rows()
    causal, causal_t = causal_masks()
    width = queries.shape[1]
    for g in groups(width):
        q, k, v, ga = queries[:, g], keys[:, g], values[:, g], grad_attended[:, g]
        qs, ks, vs, gs = (split_heads(rows, marks) for rows in (q, k, v, ga))
        state = open_state(prefix[0, :, g].astype(WIDE), same)
        grad_state = open_state(carry[:, g], same)
        grad_scores = (dot_nt(ga, vs) * causal).astype(LOW)
        gq = dot_nn(grad_scores, ks) + dot_nt(ga, state)
        grad_scores = (dot_nt(v, gs) * causal_t).astype(LOW)
        gk = dot_nn(grad_scores, qs) + dot_nt(v, grad_state)
        scores = (dot_nt(k, qs) * causal_t).astype(LOW)
        gv = dot_nn(scores, gs) + dot_nn(k, grad_state)
        gq = gq * silu_slope(pre_query[:, g].astype(WIDE))
        gk = gk * silu_slope(pre_key[:, g].astype(WIDE))
        for n, grad in enumerate((gq, gk, gv)):
            grads[:, n * width + g.start : n * width + g.stop] = grad.astype(LOW)
        carry[:, g] += pack_state(dot_tn(q, ga), same)


def clip(value, low, high):
    return jnp.minimum(jnp.maximum(value, low), high)


CHUNK = 256
PAIRS = (4, 4, 3)
PAIR_ORDERS = (("0xy1", "y0x1"), ("xy10", "x0y1"), ("yx01", "yx01"))
THREE_ORDERS = ("01y", "y01")
THREE_AFTER = 1


def feed_back_blocks():
    pairs, three, at = [], None, 0
    for n, count in enumerate(PAIRS):
        if n == THREE_AFTER:
            three = (at, 8)
            at += 8
        pairs.append((at, count))
        at += count
    return pairs, three, at


class ThreeScatter(Scatter):
    def last_swap(self, sems, out, give, take):
        self.out, self.give, self.take = out, give, take
        cols = self.columns
        self.swap = sems.copy(give.at[:, cols], take.at[:, cols], (SIDE,))

    def advance(self, k):
        if k < len(self.order):
            super().advance(k)
            return
        cols = self.columns
        total = self.result()
        deep = total.shape[0] // 2
        low, high = total[:deep], total[deep:]
        upper = bit_value(SIDE).astype(WIDE)
        self.out[:, cols] = low * (1 - upper) + high * upper
        self.give[:, cols] = low * upper + high * (1 - upper)
        self.swap.start()

    def finish(self):
        self.swap.wait_recv()
        self.out[:, self.columns] += self.take[:, self.columns]
        self.swap.wait_send()


def feed_back_kernel(
    per_seq, bits,
    normed_hbm, grad_one, grad_two, glu, upstream_hbm,
    queries, keys, values, grad_attended, pre_query, pre_key, prefix, totals,
    out_one, out_two, out_three, grads,
    normed, upstream, acc, come1, come2, come3, come4, send, come,
    acc3, come31, come32, come33, send3, take3, last_send, last_come,
    state_out, state_in, carry, part, part3, send_sems, recv_sems, local,
):
    step = pl.program_id(0)
    pairs, three_block, base = feed_back_blocks()
    links = [bit for bit in bits if bit != CORE]
    mine, side = bit_value(CORE), bit_value(SIDE)
    other = 1 - mine
    sems = Sems(send_sems, recv_sems)
    hidden, width = out_one.shape[1], out_three.shape[1]
    recvs = (come1, come2, come3, come4)
    pieces, ends, first = {}, [], 0
    for n, count in enumerate(PAIRS):
        for w, (name, out) in enumerate((("one", out_one), ("two", out_two))):
            begin = w * hidden + first * CHUNK
            span = count * CHUNK
            pieces[f"{name}{n}"] = Scatter(
                sems, links, PAIR_ORDERS[n][w], acc, send.at[n % 2, w], come.at[n, w], recvs,
                slice(begin, begin + span), slice(0, span),
            )
            ends.append((pieces[f"{name}{n}"], out, first * CHUNK))
        first += count
    half = width // 2
    threes = []
    for n in range(2):
        cols = slice(n * half, (n + 1) * half)
        piece = ThreeScatter(
            sems, links[:-1], THREE_ORDERS[n], acc3, send3, take3, (come31, come32, come33),
            cols, cols,
        )
        piece.last_swap(sems, out_three, last_send, last_come)
        pieces[f"three{n}"] = piece
        threes.append(piece)
    swap_state = sems.copy(state_out, state_in, (SIDE,))
    load = [
        pltpu.make_async_copy(normed_hbm, normed, local.at[0]),
        pltpu.make_async_copy(upstream_hbm, upstream, local.at[1]),
    ]

    @pl.when(step == 0)
    def _():
        for copy in load:
            copy.start()
        greet(bits, far=False)
        state_out[...] = totals[...].astype(LOW)
        swap_state.start()
        load[0].wait()

    @pl.when(step == three_block[0])
    def _():
        load[1].wait()

    for n in range(2, len(PAIRS)):

        @pl.when(step == pairs[n][0])
        def _():
            pieces[f"one{n - 2}"].core.wait_send()
            pieces[f"two{n - 2}"].core.wait_send()

    @pl.when(step < base)
    def _():
        run_events(step, planned(FEED_BACK_PLAN, pieces, 0, base))

    @pl.when(step >= base)
    def _():
        run_events(step, planned(FEED_BACK_PLAN, pieces, base, base + 8))

    lead = acc.shape[:-1]
    fill = (slice(None),) * len(lead)

    def weight_chunk(w, rhs, chunk, group, first):
        part[...] = dot_nn(normed[...], rhs[...]).astype(LOW).reshape(part.shape)
        at = pl.ds(pl.multiple_of(chunk * CHUNK, CHUNK), CHUNK)
        send[(group % 2, w) + fill + (at,)] = part[:, other].reshape(lead + (CHUNK,))
        at = pl.ds(pl.multiple_of(w * hidden + (first + chunk) * CHUNK, CHUNK), CHUNK)
        acc[fill + (at,)] = part[:, mine].reshape(lead + (CHUNK,))

    first = 0
    for n, (begin, count) in enumerate(pairs):

        @pl.when((step >= begin) & (step < begin + count))
        def _():
            weight_chunk(0, grad_one, step - begin, n, first)
            weight_chunk(1, grad_two, step - begin, n, first)

        @pl.when(step == begin + count - 1)
        def _():
            pieces[f"one{n}"].launch()
            pieces[f"two{n}"].launch()

        first += count

    begin, count = three_block

    @pl.when((step >= begin) & (step < begin + count))
    def _():
        k = step - begin
        at = tuple((k // (1 << (2 - d))) % 2 for d in range(3))
        part3[...] = dot_nn(glu[...], upstream[...]).astype(LOW).reshape(part3.shape)
        send3[at] = part3[other]
        acc3[at] = part3[mine]

    @pl.when(step == begin + count - 1)
    def _():
        for piece in threes:
            piece.launch()

    @pl.when(step >= base)
    def _():
        at = step - base

        @pl.when(at == 0)
        def _():
            swap_state.wait_recv()

        @pl.when(at % per_seq == 0)
        def _():
            carry[...] = state_in[at // per_seq].astype(WIDE) * (1 - side).astype(WIDE)

        attend_back_step(
            head_square(), queries, keys, values, grad_attended, pre_query, pre_key, prefix,
            grads, carry,
        )

    @pl.when(step == pl.num_programs(0) - 1)
    def _():
        for actions in planned(FEED_BACK_PLAN, pieces, base + 8, 1000).values():
            for action in actions:
                action()
        for piece, out, begin in ends:
            span = piece.columns.stop - piece.columns.start
            out[:, begin : begin + span] = piece.result()
        for n in range(len(PAIRS)):
            for name in ("one", "two"):
                pieces[f"{name}{n}"].drain(core=n + 2 >= len(PAIRS))
        for piece in threes:
            piece.finish()
            piece.drain()
        swap_state.wait_send()


def feed_back(
    seq_count, normed, grad_one, grad_two, glu, upstream, queries, keys, values, grad_attended,
    pre_query, pre_key, prefix, totals,
):
    row_count, width = queries.shape
    hidden = grad_one.shape[1]
    steps = row_count // BLOCK
    per_seq = steps // seq_count
    bits = index_bits()
    pairs, three, base = feed_back_blocks()
    deep = hidden // 8
    slab = width // 32

    def pair_at(i):
        done = sum(clip(i - begin, 0, count) for begin, count in pairs)
        return jnp.minimum(done, sum(PAIRS) - 1)

    def back(i):
        at = clip(i - base, 0, steps - 1)
        return (at // per_seq) * per_seq + per_seq - 1 - at % per_seq

    rows = pl.BlockSpec((BLOCK, width), lambda i: (back(i), 0))
    pair = pl.BlockSpec((row_count, CHUNK), lambda i: (0, pair_at(i)))
    vmem = pl.BlockSpec(memory_space=pltpu.VMEM)
    hbm = pl.BlockSpec(memory_space=pl.ANY)
    low = functools.partial(pltpu.VMEM, dtype=LOW)
    span = max(PAIRS) * CHUNK
    copies = 10 * len(PAIRS) + 2 * 5 + 1
    return pl.pallas_call(
        functools.partial(feed_back_kernel, per_seq, bits),
        grid=(base + steps,),
        in_specs=[
            hbm, pair, pair,
            pl.BlockSpec((deep, row_count), lambda i: (clip(i - three[0], 0, 7), 0)),
            hbm,
        ]
        + [rows] * 6
        + [pl.BlockSpec((1, HD, width), lambda i: (back(i), 0, 0)), vmem],
        out_specs=[vmem] * 3 + [pl.BlockSpec((BLOCK, 3 * width), lambda i: (back(i), 0))],
        out_shape=[
            jax.ShapeDtypeStruct((slab, hidden), WIDE),
            jax.ShapeDtypeStruct((slab, hidden), WIDE),
            jax.ShapeDtypeStruct((hidden // 32, width), WIDE),
            jax.ShapeDtypeStruct((row_count, 3 * width), LOW),
        ],
        scratch_shapes=[
            low((width, row_count)),
            low((row_count, width)),
            low((2, 2, 2, 2, slab, 2 * hidden)),
            low((2, 2, 2, slab, 2 * hidden)),
            low((2, 2, slab, 2 * hidden)),
            low((2, slab, 2 * hidden)),
            low((slab, 2 * hidden)),
            low((2, 2, 2, 2, 2, 2, slab, span)),
            low((len(PAIRS), 2, 2, 2, 2, 2, slab, span)),
            low((2, 2, 2, deep // 2, width)),
            low((2, 2, deep // 2, width)),
            low((2, deep // 2, width)),
            low((deep // 2, width)),
            low((2, 2, 2, deep // 2, width)),
            low((2, 2, 2, deep // 2, width)),
            pltpu.VMEM((hidden // 32, width), WIDE),
            pltpu.VMEM((hidden // 32, width), WIDE),
            low((seq_count, HD, width)),
            low((seq_count, HD, width)),
            pltpu.VMEM((HD, width), WIDE),
            low((8, 2, width // 16, CHUNK)),
            low((2, deep // 2, width)),
            pltpu.SemaphoreType.DMA((copies,)),
            pltpu.SemaphoreType.DMA((copies,)),
            pltpu.SemaphoreType.DMA((2,)),
        ],
        compiler_params=pltpu.CompilerParams(
            dimension_semantics=("arbitrary",),
            vmem_limit_bytes=63 << 20,
            collective_id=2,
            has_side_effects=True,
        ),
        cost_estimate=pl.CostEstimate(
            flops=6 * row_count * width * hidden + 12 * row_count * width * width,
            bytes_accessed=128 << 20,
            transcendentals=0,
        ),
    )(
        normed, grad_one, grad_two, glu, upstream, queries, keys, values, grad_attended,
        pre_query, pre_key, prefix, totals,
    )


WIDE_CHUNK = 512
PARTS = (2, 2, 1, 2, 1, 1, 1)
PART_ORDERS = ("01xy", "y01x", "x0y1", "xy01", "y0x1", "yx10", "x0y1")


def attend_weights_kernel(
    bits,
    normed_hbm, mixed_hbm, gated, grads, gain_term, rows_three, rows_gate, weights_hbm, tok,
    grad_residual,
    out, input_grad,
    normed, mixed, weights, acc, come1, come2, come3, come4, send, come, part,
    send_sems, recv_sems, local,
):
    step = pl.program_id(0)
    links = [bit for bit in bits if bit != CORE]
    mine = bit_value(CORE)
    other = 1 - mine
    sems = Sems(send_sems, recv_sems)
    width = tok.shape[1]
    per = width // WIDE_CHUNK
    chunks = 5 * per
    lead = acc.shape[:-1]
    fill = (slice(None),) * len(lead)

    def column(chunk):
        return chunk * WIDE_CHUNK + (128 if chunk >= per else 0)

    pieces, first = {}, 0
    launches = {}
    for n, count in enumerate(PARTS):
        cols = slice(column(first), column(first + count))
        first += count
        pieces[f"p{n}"] = Scatter(
            sems, links, PART_ORDERS[n], acc, send, come, (come1, come2, come3, come4), cols, cols
        )
        launches[first - 1] = [pieces[f"p{n}"].launch]
    load = [
        pltpu.make_async_copy(mixed_hbm, mixed, local.at[0]),
        pltpu.make_async_copy(normed_hbm, normed, local.at[1]),
        pltpu.make_async_copy(weights_hbm.at[:, : 4 * width], weights, local.at[2]),
    ]

    @pl.when(step == 0)
    def _():
        for copy in load:
            copy.start()
        greet(bits, far=False)
        load[0].wait()

    @pl.when(step == per)
    def _():
        load[1].wait()

    @pl.when(step == chunks)
    def _():
        load[2].wait()

    run_events(step, planned(ATTEND_BACK_PLAN, pieces, 0, chunks + 8))

    def chunk_phase(begin, end, lhs, rhs, shift):
        @pl.when((step >= begin) & (step < end))
        def _():
            at = pl.ds(pl.multiple_of(step * WIDE_CHUNK + shift, 128), WIDE_CHUNK)
            part[...] = dot_nn(lhs[...], rhs[...]).astype(LOW).reshape(part.shape)
            send[fill + (at,)] = part[:, other].reshape(lead + (WIDE_CHUNK,))
            acc[fill + (at,)] = part[:, mine].reshape(lead + (WIDE_CHUNK,))

    chunk_phase(0, per, mixed, gated, 0)
    chunk_phase(per, 2 * per, normed, gated, 128)
    chunk_phase(2 * per, chunks, normed, grads, 128)

    @pl.when(step == 0)
    def _():
        column = jnp.broadcast_to(gain_term[...], (128, width)).T
        column = column.reshape(8, 2, width // 16, 128)
        upper = mine.astype(WIDE)
        low, high = column[:, 0], column[:, 1]
        at = fill + (slice(width, width + 128),)
        acc[at] = (low * (1 - upper) + high * upper).astype(LOW).reshape(lead + (128,))
        send[at] = (low * upper + high * (1 - upper)).astype(LOW).reshape(lead + (128,))

    run_events(step, launches)

    @pl.when(step >= chunks)
    def _():
        def weight(n):
            return weights[:, n * width : (n + 1) * width]

        def row(n):
            return rows_three[:, n * width : (n + 1) * width]

        grad = dot_nt(row(0), weight(2)) + dot_nt(row(1), weight(0))
        grad += dot_nt(row(2), weight(1)) + dot_nt(rows_gate[...], weight(3))
        x = tok[...].astype(WIDE)
        grad = grad_residual[...] + norm_back(x, rms_scale(x), grad)
        input_grad[...] = grad.astype(input_grad.dtype)

    @pl.when(step == pl.num_programs(0) - 1)
    def _():
        for actions in planned(ATTEND_BACK_PLAN, pieces, chunks + 8, 1000).values():
            for action in actions:
                action()
        for piece in pieces.values():
            out[:, piece.columns] = piece.result()
        for piece in pieces.values():
            piece.drain()


def attend_weights(normed, mixed, gated, grads, gain_term, full_attn, tok, grad_residual):
    row_count, width = tok.shape
    steps = row_count // BLOCK
    bits = index_bits()
    per = width // WIDE_CHUNK
    chunks = 5 * per
    slab = width // 32
    vmem = pl.BlockSpec(memory_space=pltpu.VMEM)
    hbm = pl.BlockSpec(memory_space=pl.ANY)

    def rows(size, column=0):
        return pl.BlockSpec((BLOCK, size), lambda i: (clip(i - chunks, 0, steps - 1), column))

    def chunk(begin, count):
        return pl.BlockSpec(
            (row_count, WIDE_CHUNK), lambda i: (0, clip(i - begin, 0, count - 1))
        )

    low = functools.partial(pltpu.VMEM, dtype=LOW)
    columns = 5 * width + 128
    copies = 5 * len(PARTS)
    return pl.pallas_call(
        functools.partial(attend_weights_kernel, bits),
        grid=(chunks + steps,),
        in_specs=[hbm, hbm, chunk(0, 2 * per), chunk(2 * per, 3 * per), vmem, rows(3 * width),
                  rows(width, 1), hbm, rows(width), rows(width)],
        out_specs=[vmem, rows(width)],
        out_shape=[
            jax.ShapeDtypeStruct((slab, columns), WIDE),
            jax.ShapeDtypeStruct((row_count, width), WIDE),
        ],
        scratch_shapes=[
            low((width, row_count)),
            low((width, row_count)),
            low((width, 4 * width)),
            low((2, 2, 2, 2, slab, columns)),
            low((2, 2, 2, slab, columns)),
            low((2, 2, slab, columns)),
            low((2, slab, columns)),
            low((slab, columns)),
            low((2, 2, 2, 2, slab, columns)),
            low((2, 2, 2, 2, slab, columns)),
            low((8, 2, width // 16, WIDE_CHUNK)),
            pltpu.SemaphoreType.DMA((copies,)),
            pltpu.SemaphoreType.DMA((copies,)),
            pltpu.SemaphoreType.DMA((3,)),
        ],
        compiler_params=pltpu.CompilerParams(
            dimension_semantics=("arbitrary",),
            vmem_limit_bytes=62 << 20,
            collective_id=3,
            has_side_effects=True,
        ),
        cost_estimate=pl.CostEstimate(
            flops=18 * row_count * width * width, bytes_accessed=64 << 20, transcendentals=0
        ),
    )(normed, mixed, gated, grads, gain_term, grads, gated, full_attn, tok, grad_residual)


ATTEND_PIECES = (
    (("a00", "10yx", 6), ("a01", "zxy", 5), ("a02", "zyx", 5)),
    (("a10", "zyx", 9), ("a11", "x10y", 4), ("a12", "10xy", 3)),
    (("a20", "10xy", 4), ("a21", "10yx", 2), ("a22", "zyx", 3)),
)
FEED_PIECES = (
    (("f0", "y10x", 13), ("f1", "10yx", 9)),
    (("f2", "10yx", 7), ("f3", "1xy0", 15)),
)
THREE_PIECES = (("f4", "zy", 3), ("f5", "10y", 5))
FORWARD_COPIES = 128


class ThreeGather(Gather):
    def first_swap(self, sems, columns, give, take, slab, target, local):
        self.cols, self.give, self.take, self.slab = columns, give, take, slab
        self.swap = sems.copy(give.at[:, columns], take.at[:, columns], (SIDE,))
        self.place = pltpu.make_async_copy(slab.at[:, columns], target.at[:, columns], local)

    def advance(self, k):
        if k == 0:
            self.swap.start()
            return
        if k == 1:
            self.swap.wait_recv()
            upper = bit_value(SIDE).astype(WIDE)
            mine, theirs = self.give[:, self.cols], self.take[:, self.cols]
            low = mine * (1 - upper) + theirs * upper
            high = mine * upper + theirs * (1 - upper)
            self.slab[:, self.cols] = jnp.concatenate([low, high], axis=0).astype(LOW)
            self.place.start()
            self.place.wait()
        super().advance(k - 1)

    def drain(self):
        super().drain()
        self.swap.wait_send()


def forward_kernel(
    steps, per_seq, bits,
    tok, s_key, s_value, s_query, s_gate, s_out, s_gain, s_one, s_two, s_three,
    normed, pre_key, keys, values, pre_query, queries, pre_gate, attended, mixed, residual,
    prefix, gain_row, full_attn, full_one, full_two, full_three,
    held, all_keys, all_values, all_normed, totals, state_out, state_in, carry,
    three_out, three_in, three_slab, send, recv, local,
):
    step = pl.program_id(0)
    width = tok.shape[1]
    sems = Sems(send, recv)
    own = tuple(bit_value(bit) for bit in bits)
    side = bit_value(SIDE).astype(WIDE)
    pieces, waves, start = {}, [], 0
    for wave in ATTEND_PIECES:
        waves.append([])
        for name, order, tiles in wave:
            cols = slice(start, start + 128 * tiles)
            start += 128 * tiles
            pieces[name] = Gather(held, bits, order, sems, cols)
            waves[-1].append(pieces[name])
    feed = []
    for buf, parts in zip((full_one, full_two), FEED_PIECES):
        start = 0
        for name, order, tiles in parts:
            cols = slice(start, start + 128 * tiles)
            start += 128 * tiles
            pieces[name] = Gather(buf, bits, order, sems, cols)
            feed.append(pieces[name])
    start = 0
    for n, (name, order, tiles) in enumerate(THREE_PIECES):
        cols = slice(start, start + 128 * tiles)
        start += 128 * tiles
        pieces[name] = ThreeGather(full_three, bits[:-1], order, sems, cols)
        pieces[name].first_swap(
            sems, cols, three_out, three_in, three_slab, full_three.at[own[:-1]], local.at[2 + n]
        )
        feed.append(pieces[name])
    swap_state = sems.copy(state_out, state_in, (SIDE,))
    keep_attn = pltpu.make_async_copy(held, full_attn, local.at[4])

    @pl.when(step == 0)
    def _():
        place = [
            pltpu.make_async_copy(s_one, full_one.at[own], local.at[0]),
            pltpu.make_async_copy(s_two, full_two.at[own], local.at[1]),
        ]
        for copy in place:
            copy.start()
        for n, shard in enumerate((s_key, s_value, s_query, s_gate, s_out)):
            held[own + (slice(None), slice(n * width, (n + 1) * width))] = shard[...]
        held[own + (slice(None), slice(5 * width, 5 * width + 128))] = s_gain[...]
        three_out[...] = s_three[...].astype(WIDE)
        greet(bits)
        for copy in place:
            copy.wait()
        for actions in planned(FORWARD_PLAN, pieces, 0, 1).values():
            for action in actions:
                action()
        for piece in waves[0]:
            piece.finish()

    @pl.when(step == steps)
    def _():
        for wave in waves[1:]:
            for piece in wave:
                piece.finish()
        keep_attn.start()
        column = held[..., 5 * width : 5 * width + 128].reshape(width, 128)
        gain_row[...] = column.astype(WIDE).T[:1]

    run_events(step + 1, planned(FORWARD_PLAN, pieces, 1, 2 * steps + 1))

    def weight(n):
        return held[..., n * width : (n + 1) * width].reshape(width, width)

    same = head_square()

    @pl.when(step < steps)
    def _():
        x = tok[...].astype(WIDE)
        rows = (x * rms_scale(x)).astype(LOW)
        normed[...] = rows.T
        here = pl.ds(pl.multiple_of(step * BLOCK, BLOCK), BLOCK)
        all_normed[here, :] = rows
        pre = dot_nn(rows, weight(0))
        pre_key[...] = pre.astype(LOW)
        k = jax.nn.silu(pre).astype(LOW)
        keys[...] = k
        all_keys[here, :] = k
        v = dot_nn(rows, weight(1)).astype(LOW)
        values[...] = v
        all_values[here, :] = v
        seq = step // per_seq

        @pl.when(step % per_seq == 0)
        def _():
            totals[seq] = jnp.zeros((HD, width), WIDE)

        for g in groups(width):
            totals[seq, :, g] += pack_state(dot_tn(k[:, g], v[:, g]), same)

    @pl.when(step == steps - 1)
    def _():
        state_out[...] = totals[...].astype(LOW)
        swap_state.start()

    @pl.when(step >= steps)
    def _():
        at = step - steps
        here = pl.ds(pl.multiple_of(at * BLOCK, BLOCK), BLOCK)
        rows = all_normed[here, :]
        pre = dot_nn(rows, weight(2))
        pre_query[...] = pre.astype(LOW)
        queries[...] = jax.nn.silu(pre).astype(LOW)
        gate = dot_nn(rows, weight(3))
        pre_gate[...] = gate.astype(LOW)

        @pl.when(at == 0)
        def _():
            swap_state.wait_recv()

        @pl.when(at % per_seq == 0)
        def _():
            carry[...] = state_in[at // per_seq].astype(WIDE) * side

        marks = head_rows()
        causal, _ = causal_masks()
        prefix[0] = carry[...].astype(LOW)
        for g in groups(width):
            q, k, v = queries[:, g], all_keys[here, g], all_values[here, g]
            scores = (dot_nt(q, split_heads(k, marks)) * causal).astype(LOW)
            out = dot_nn(scores, split_heads(v, marks))
            out += dot_nn(q, open_state(carry[:, g], same))
            attended[:, g] = out.astype(LOW)
            carry[:, g] += pack_state(dot_tn(k, v), same)
        rows = attended[...].astype(WIDE)
        rows = rows * rms_scale(rows) * gain_row[...] * jax.nn.sigmoid(gate)
        rows = rows.astype(LOW)
        mixed[...] = rows.T
        residual[...] = tok[...].astype(WIDE) + dot_nn(rows, weight(4))

    @pl.when(step == 2 * steps - 1)
    def _():
        for actions in planned(FORWARD_PLAN, pieces, 2 * steps + 1, 1000).values():
            for action in actions:
                action()
        for piece in feed:
            piece.finish()
        for piece in pieces.values():
            piece.drain()
        swap_state.wait_send()
        keep_attn.wait()


def forward(tok, seq_count, shards_attn, gain_columns, s_one, s_two, s_three):
    row_count, width = tok.shape
    hidden = s_one.shape[1]
    steps = row_count // BLOCK
    per_seq = steps // seq_count
    bits = index_bits()
    lead = (2,) * len(bits)
    slab = s_one.shape[0]
    deep = s_three.shape[0]
    columns = 5 * width + 128
    in_rows = pl.BlockSpec((BLOCK, width), lambda i: (i % steps, 0))
    first = pl.BlockSpec((BLOCK, width), lambda i: (jnp.minimum(i, steps - 1), 0))
    second = pl.BlockSpec((BLOCK, width), lambda i: (jnp.maximum(i - steps, 0), 0))
    first_turned = pl.BlockSpec((width, BLOCK), lambda i: (0, jnp.minimum(i, steps - 1)))
    second_turned = pl.BlockSpec((width, BLOCK), lambda i: (0, jnp.maximum(i - steps, 0)))
    any_spec = pl.BlockSpec(memory_space=pl.ANY)
    vmem = pl.BlockSpec(memory_space=pltpu.VMEM)

    def shape(*dims, dtype=LOW):
        return jax.ShapeDtypeStruct(dims, dtype)

    rows_low, turned_low = shape(row_count, width), shape(width, row_count)
    low = functools.partial(pltpu.VMEM, dtype=LOW)
    out = pl.pallas_call(
        functools.partial(forward_kernel, steps, per_seq, bits),
        grid=(2 * steps,),
        in_specs=[in_rows] + [vmem] * 6 + [any_spec] * 2 + [vmem],
        out_specs=[first_turned] + [first] * 3 + [second] * 4 + [second_turned, second]
        + [
            pl.BlockSpec((1, HD, width), lambda i: (jnp.maximum(i - steps, 0), 0, 0)),
            pl.BlockSpec((1, width), lambda i: (0, 0)),
        ]
        + [any_spec] * 4,
        out_shape=[turned_low] + [rows_low] * 7 + [turned_low]
        + [
            shape(row_count, width, dtype=WIDE),
            shape(steps, HD, width),
            shape(1, width, dtype=WIDE),
            shape(*lead, slab, columns),
            shape(*lead, slab, hidden),
            shape(*lead, slab, hidden),
            shape(*lead[:-1], 2 * deep, width),
        ],
        scratch_shapes=[
            low(lead + (slab, columns)),
            low((row_count, width)),
            low((row_count, width)),
            low((row_count, width)),
            pltpu.VMEM((seq_count, HD, width), WIDE),
            low((seq_count, HD, width)),
            low((seq_count, HD, width)),
            pltpu.VMEM((HD, width), WIDE),
            pltpu.VMEM((deep, width), WIDE),
            pltpu.VMEM((deep, width), WIDE),
            low((2 * deep, width)),
            pltpu.SemaphoreType.DMA((FORWARD_COPIES,)),
            pltpu.SemaphoreType.DMA((FORWARD_COPIES,)),
            pltpu.SemaphoreType.DMA((5,)),
        ],
        compiler_params=pltpu.CompilerParams(
            dimension_semantics=("arbitrary",),
            vmem_limit_bytes=58 << 20,
            collective_id=1,
            has_side_effects=True,
        ),
        cost_estimate=pl.CostEstimate(
            flops=16 * row_count * width * width, bytes_accessed=64 << 20, transcendentals=0
        ),
    )(tok, *shards_attn, gain_columns, s_one, s_two, s_three)
    return list(out[:12]) + [
        out[12].reshape(-1, columns),
        out[13].reshape(-1, hidden),
        out[14].reshape(-1, hidden),
        out[15].reshape(-1, width),
    ]


def plain_shards(
    tokens,
    lengths,
    w_query,
    w_key,
    w_value,
    w_gate,
    out_gain,
    w_out,
    w_one,
    w_two,
    w_three,
    cotangent,
):
    seq_count, local_length, width = tokens.shape
    row_count = seq_count * local_length
    hidden = w_one.shape[1]
    steps = row_count // BLOCK
    per_seq = local_length // BLOCK
    orders = stream_orders()
    tok = tokens.reshape(row_count, width)
    cot = cotangent.reshape(row_count, width)
    full_key = gather_rows(w_key, orders[0])
    full_value = gather_rows(w_value, orders[1])
    full_query = gather_rows(w_query, orders[2])
    full_gate = gather_rows(w_gate, orders[0])
    gain_columns = jnp.broadcast_to(out_gain[:, None], (out_gain.shape[0], 128))
    full_out = gather_rows(jnp.concatenate([w_out, gain_columns], axis=1), orders[1])
    full_one = gather_rows(w_one, orders[2])
    full_two = gather_rows(w_two, orders[0])
    full_three = gather_rows(w_three, orders[1])
    gain = full_out[:, width].astype(WIDE)[None, :]
    full_out = full_out[:, :width]

    rows = rows_spec(width)
    narrow = ((row_count, width), LOW, rows)
    wide = ((row_count, width), WIDE, rows)
    big = ((row_count, hidden), LOW, rows_spec(hidden))
    state_spec = pl.BlockSpec((1, HD, width), lambda i: (i // per_seq, 0, 0))
    state = ((seq_count, HD, width), WIDE, state_spec)
    square = 2 * row_count * width * width

    normed_low, pre_key, keys, values, totals = call(
        lambda *refs: key_value_kernel(per_seq, *refs),
        steps,
        [(tok, rows), (full_key, whole_spec(full_key)), (full_value, whole_spec(full_value))],
        [narrow, narrow, narrow, narrow, state],
        flops=2 * square,
    )
    incoming = shift_sum(totals, "fsdp", False)
    pre_query, queries, pre_gate = call(
        query_gate_kernel,
        steps,
        [(normed_low, rows), (full_query, whole_spec(full_query)), (full_gate, whole_spec(full_gate))],
        [narrow, narrow, narrow],
        flops=2 * square,
    )
    prefix_spec = pl.BlockSpec((1, HD, width), lambda i: (i, 0, 0))
    attended, mixed, residual, prefix = call(
        lambda *refs: attend_kernel(per_seq, *refs),
        steps,
        [(queries, rows), (keys, rows), (values, rows), (pre_gate, rows), (tok, rows),
         (incoming, state_spec), (gain, whole_spec(gain)), (full_out, whole_spec(full_out))],
        [narrow, narrow, wide, ((steps, HD, width), LOW, prefix_spec)],
        scratch=[pltpu.VMEM((HD, width), WIDE)],
        flops=3 * square,
    )
    (
        layer_out, normed_two, glu, grad_up_one, grad_up_two, upstream_low, grad_residual,
        gated, grad_attended, grad_totals, grad_gain_term,
    ) = call(
        lambda *refs: feed_kernel(per_seq, False, *refs),
        steps,
        [(lengths, pl.BlockSpec(memory_space=pltpu.SMEM)), (residual, rows), (cot, rows),
         (full_one, whole_spec(full_one)), (full_two, whole_spec(full_two)),
         (full_three, whole_spec(full_three)), (full_out, whole_spec(full_out)),
         (gain, whole_spec(gain)), (pre_gate, rows), (attended, rows), (queries, rows)],
        [narrow, narrow, big, big, big, narrow, wide,
         ((row_count, 2 * width), LOW, rows_spec(2 * width)), narrow, state,
         ((1, width), WIDE, pl.BlockSpec((1, width), lambda i: (0, 0)))],
        flops=12 * row_count * width * hidden + square,
    )
    grad_residual_low, grad_pre_gate = gated[:, :width], gated[:, width:]
    outgoing = shift_sum(grad_totals, "fsdp", True)
    grad_one = scatter_rows(dot_tn(normed_two, grad_up_one), orders[1])
    grad_two = scatter_rows(dot_tn(normed_two, grad_up_two), orders[2])
    grad_three = scatter_rows(dot_tn(glu, upstream_low), orders[0])
    gain_term = jnp.broadcast_to(grad_gain_term.reshape(width, 1), (width, 128))
    grad_out = scatter_rows(
        jnp.concatenate([dot_tn(mixed, grad_residual_low), gain_term], axis=1), orders[1]
    )
    grad_gain = grad_out[:, width]
    grad_out = grad_out[:, :width]

    def back(i):
        return (i // per_seq) * per_seq + per_seq - 1 - i % per_seq

    back_rows = rows_spec(width, order=back)
    back_narrow = ((row_count, width), LOW, back_rows)
    grad_pre_query, grad_pre_key, grad_pre_value = call(
        lambda *refs: attend_back_kernel(per_seq, *refs),
        steps,
        [(queries, back_rows), (keys, back_rows), (values, back_rows),
         (grad_attended, back_rows), (pre_query, back_rows), (pre_key, back_rows),
         (prefix, pl.BlockSpec((1, HD, width), lambda i: (back(i), 0, 0))),
         (outgoing, state_spec)],
        [back_narrow, back_narrow, back_narrow],
        scratch=[pltpu.VMEM((HD, width), WIDE)],
        flops=6 * square,
    )
    grad_query = scatter_rows(dot_tn(normed_low, grad_pre_query), orders[0])
    grad_key = scatter_rows(dot_tn(normed_low, grad_pre_key), orders[1])
    grad_value = scatter_rows(dot_tn(normed_low, grad_pre_value), orders[2])
    grad_gate = scatter_rows(dot_tn(normed_low, grad_pre_gate), orders[0])
    (input_grad,) = call(
        input_kernel,
        steps,
        [(grad_pre_query, rows), (grad_pre_key, rows), (grad_pre_value, rows),
         (grad_pre_gate, rows), (full_query, whole_spec(full_query)),
         (full_key, whole_spec(full_key)), (full_value, whole_spec(full_value)),
         (full_gate, whole_spec(full_gate)), (tok, rows), (grad_residual, rows)],
        [wide],
        flops=4 * square,
    )
    return (
        layer_out.reshape(tokens.shape),
        input_grad.reshape(tokens.shape),
        grad_query,
        grad_key,
        grad_value,
        grad_gate,
        grad_gain,
        grad_out,
        grad_one,
        grad_two,
        grad_three,
    )


def feed(
    seq_count, lengths, residual, cot, full_one, full_two, full_three, full_attn, gain, pre_gate,
    attended, queries,
):
    row_count, width = residual.shape
    hidden = full_one.shape[1]
    steps = row_count // BLOCK
    per_seq = steps // seq_count
    rows = rows_spec(width)
    narrow = ((row_count, width), LOW, rows)
    wide = ((row_count, width), WIDE, rows)
    big = ((row_count, hidden), LOW, rows_spec(hidden))

    def turned(size):
        return ((size, row_count), LOW, pl.BlockSpec((size, BLOCK), lambda i: (0, i)))

    state_spec = pl.BlockSpec((1, HD, width), lambda i: (i // per_seq, 0, 0))
    out_part = pl.BlockSpec((width, width), lambda i: (0, 4), pipeline_mode=pl.Buffered(1))
    return call(
        lambda *refs: feed_kernel(per_seq, True, *refs),
        steps,
        [(lengths, pl.BlockSpec(memory_space=pltpu.SMEM)), (residual, rows), (cot, rows),
         (full_one, whole_spec(full_one)), (full_two, whole_spec(full_two)),
         (full_three, whole_spec(full_three)), (full_attn, out_part),
         (gain, whole_spec(gain)), (pre_gate, rows), (attended, rows), (queries, rows)],
        [narrow, turned(width), turned(hidden), big, big, narrow, wide,
         ((row_count, 2 * width), LOW, rows_spec(2 * width)), narrow,
         ((seq_count, HD, width), WIDE, state_spec),
         ((1, width), WIDE, pl.BlockSpec((1, width), lambda i: (0, 0)))],
        scratch=[pltpu.VMEM((BLOCK, hidden), LOW)],
        flops=12 * row_count * width * hidden + 2 * row_count * width * width,
    )


def fused_shards(
    tokens,
    lengths,
    w_query,
    w_key,
    w_value,
    w_gate,
    out_gain,
    w_out,
    w_one,
    w_two,
    w_three,
    cotangent,
):
    seq_count, local_length, width = tokens.shape
    row_count = seq_count * local_length
    tok = tokens.reshape(row_count, width)
    cot = cotangent.reshape(row_count, width)
    gain_columns = jnp.broadcast_to(out_gain[:, None], (out_gain.shape[0], 128))
    (
        normed_low, pre_key, keys, values, pre_query, queries, pre_gate, attended, mixed,
        residual, prefix, gain, full_attn, full_one, full_two, full_three,
    ) = forward(
        tok, seq_count, (w_key, w_value, w_query, w_gate, w_out), gain_columns, w_one, w_two, w_three
    )

    (
        layer_out, normed_two, glu, grad_up_one, grad_up_two, upstream_low, grad_residual,
        gated, grad_attended, grad_totals, grad_gain_term,
    ) = feed(
        seq_count, lengths, residual, cot, full_one, full_two, full_three, full_attn, gain,
        pre_gate, attended, queries,
    )
    grad_one, grad_two, grad_three, grad_three_pre = feed_back(
        seq_count, normed_two, grad_up_one, grad_up_two, glu, upstream_low, queries, keys, values,
        grad_attended, pre_query, pre_key, prefix, grad_totals,
    )
    grads, input_grad = attend_weights(
        normed_low, mixed, gated, grad_three_pre, grad_gain_term, full_attn, tok, grad_residual
    )
    grad_out, grad_gain = grads[:, :width], grads[:, width]
    grad_gate, grad_query, grad_key, grad_value = (
        grads[:, 128 + n * width : 128 + (n + 1) * width] for n in range(1, 5)
    )
    return (
        layer_out.reshape(tokens.shape),
        input_grad.reshape(tokens.shape),
        grad_query,
        grad_key,
        grad_value,
        grad_gate,
        grad_gain,
        grad_out,
        grad_one,
        grad_two,
        grad_three,
    )


def shards(*arrays):
    tokens, w_query, w_three = arrays[0], arrays[2], arrays[10]
    sizes = (lax.axis_size("dp"), lax.axis_size("fsdp"))
    fits = w_query.shape[0] % 16 == 0 and w_three.shape[0] % 8 == 0 and tokens.shape[1] >= 4 * BLOCK
    if sizes == (16, 2) and fits:
        return fused_shards(*arrays)
    return plain_shards(*arrays)


def solution(mesh):
    in_specs = (
        P("dp", "fsdp", None),
        P("dp"),
        P(("dp", "fsdp"), None),
        P(("dp", "fsdp"), None),
        P(("dp", "fsdp"), None),
        P(("dp", "fsdp"), None),
        P(("dp", "fsdp")),
        P(("dp", "fsdp"), None),
        P(("dp", "fsdp"), None),
        P(("dp", "fsdp"), None),
        P(("dp", "fsdp"), None),
        P("dp", "fsdp", None),
    )
    out_specs = (
        P("dp", "fsdp", None),
        P("dp", "fsdp", None),
        P(("dp", "fsdp"), None),
        P(("dp", "fsdp"), None),
        P(("dp", "fsdp"), None),
        P(("dp", "fsdp"), None),
        P(("dp", "fsdp")),
        P(("dp", "fsdp"), None),
        P(("dp", "fsdp"), None),
        P(("dp", "fsdp"), None),
        P(("dp", "fsdp"), None),
    )
    return jax.shard_map(shards, mesh=mesh, in_specs=in_specs, out_specs=out_specs, check_vma=False)
```

```python
import functools

import jax
import jax.numpy as jnp
from jax import lax
from jax.experimental import pallas as pl
from jax.experimental.pallas import tpu as pltpu
from jax.sharding import PartitionSpec as P

HD = 64
H = 16
BLOCK = 256


GROUP = 256
HEADS = GROUP // HD
LOW = jnp.bfloat16
WIDE = jnp.float32

norm_epsilon = 1e-06


def bit_steps():
    steps = []
    for axis in ("dp", "fsdp"):
        size = lax.axis_size(axis)
        bit = 0
        while (1 << bit) < size:
            steps.append((axis, bit, [(i, i ^ (1 << bit)) for i in range(size)]))
            bit += 1
    return steps


def stream_orders():
    steps = bit_steps()
    dp = [s for s in steps if s[0] == "dp"]
    fs = [s for s in steps if s[0] == "fsdp"]
    core, rest = dp[0], fs[:1] + dp[1:3]
    tail = dp[3:] + fs[1:]
    return [[core] + rest[k:] + rest[:k] + tail for k in range(3)]


def own_bit(step):
    axis, bit, _ = step
    return lax.rem(lax.div(lax.axis_index(axis), 1 << bit), 2)


def bit_dims():
    steps = bit_steps()
    dp = sorted([s for s in steps if s[0] == "dp"], key=lambda s: -s[1])
    fs = sorted([s for s in steps if s[0] == "fsdp"], key=lambda s: -s[1])
    return [(s[0], s[1]) for s in dp + fs]


def gather_rows(shard, order):
    dims = bit_dims()
    held = []
    data = shard
    for step in reversed(order):
        axis, bit, perm = step
        other = lax.ppermute(data, axis, perm)
        mine = own_bit(step) == 0
        place = sum(1 for d in held if dims.index(d) < dims.index((axis, bit)))
        held.append((axis, bit))
        data = jnp.stack(
            [jnp.where(mine, data, other), jnp.where(mine, other, data)], axis=place
        )
    return data.reshape((-1,) + shard.shape[1:])


def scatter_rows(full, order):
    dims = bit_dims()
    rows = full.shape[0] >> len(dims)
    data = full.astype(jnp.bfloat16).reshape((2,) * len(dims) + (rows,) + full.shape[1:])
    left = list(dims)
    for at, step in enumerate(order):
        axis, bit, perm = step
        place = left.index((axis, bit))
        left.pop(place)
        own = own_bit(step)
        send = lax.dynamic_index_in_dim(data, 1 - own, place, keepdims=False)
        keep = lax.dynamic_index_in_dim(data, own, place, keepdims=False)
        come = lax.ppermute(send, axis, perm)
        data = keep.astype(jnp.float32) + come.astype(jnp.float32)
        if at < len(order) - 1:
            data = data.astype(jnp.bfloat16)
    return data


def shift_sum(x, axis, reverse):
    size = lax.axis_size(axis)
    total = jnp.zeros_like(x)
    low = x.astype(jnp.bfloat16)
    for s in range(1, size):
        pairs = [(i + s, i) if reverse else (i, i + s) for i in range(size - s)]
        total = total + lax.ppermute(low, axis, pairs).astype(x.dtype)
    return total


def dot_nn(a, b):
    return jnp.dot(a, b, preferred_element_type=WIDE)


def dot_nt(a, b):
    return lax.dot_general(a, b, (((1,), (1,)), ((), ())), preferred_element_type=WIDE)


def dot_tn(a, b):
    return lax.dot_general(a, b, (((0,), (0,)), ((), ())), preferred_element_type=WIDE)


def rms_scale(values):
    return lax.rsqrt(jnp.mean(values * values, axis=-1, keepdims=True) + norm_epsilon)


def norm_back(values, scale, upstream):
    inner_mean = jnp.mean(upstream * values, axis=-1, keepdims=True)
    return scale * (upstream - values * (scale * scale) * inner_mean)


def silu_slope(pre_rows):
    logistic = jax.nn.sigmoid(pre_rows)
    return logistic * (1.0 + pre_rows * (1.0 - logistic))


def head_square():
    row = lax.broadcasted_iota(jnp.int32, (GROUP, GROUP), 0) // HD
    col = lax.broadcasted_iota(jnp.int32, (GROUP, GROUP), 1) // HD
    return (row == col).astype(WIDE)


def head_rows():
    lane = lax.broadcasted_iota(jnp.int32, (1, GROUP), 1) // HD
    return [(lane == h).astype(WIDE).astype(LOW) for h in range(HEADS)]


def split_heads(rows, marks):
    return jnp.concatenate([rows * mark for mark in marks], axis=0)


def pack_state(square, same):
    return jnp.sum((square * same).reshape(HEADS, HD, GROUP), axis=0)


def open_state(packed, same):
    return (jnp.concatenate([packed] * HEADS, axis=0) * same).astype(LOW)


def causal_masks():
    i = lax.broadcasted_iota(jnp.int32, (BLOCK, HEADS * BLOCK), 0)
    j = lax.broadcasted_iota(jnp.int32, (BLOCK, HEADS * BLOCK), 1) % BLOCK
    return (i >= j).astype(WIDE), (j >= i).astype(WIDE)


def groups(width):
    return [slice(g * GROUP, (g + 1) * GROUP) for g in range(width // GROUP)]


def key_value_kernel(per_seq, tok, w_key, w_value, normed, pre_key, keys, values, totals):
    x = tok[...].astype(WIDE)
    rows = (x * rms_scale(x)).astype(LOW)
    normed[...] = rows
    pre = dot_nn(rows, w_key[...])
    pre_key[...] = pre.astype(LOW)
    k = jax.nn.silu(pre).astype(LOW)
    keys[...] = k
    v = dot_nn(rows, w_value[...]).astype(LOW)
    values[...] = v

    @pl.when(pl.program_id(0) % per_seq == 0)
    def _():
        totals[...] = jnp.zeros_like(totals)

    same = head_square()
    for g in groups(k.shape[1]):
        totals[0, :, g] += pack_state(dot_tn(k[:, g], v[:, g]), same)


def query_gate_kernel(normed, w_query, w_gate, pre_query, queries, pre_gate):
    rows = normed[...]
    pre = dot_nn(rows, w_query[...])
    pre_query[...] = pre.astype(LOW)
    queries[...] = jax.nn.silu(pre).astype(LOW)
    pre_gate[...] = dot_nn(rows, w_gate[...]).astype(LOW)


def attend_kernel(
    per_seq, queries, keys, values, pre_gate, tok, incoming, gain, w_out,
    attended, mixed, residual, prefix, carry,
):
    @pl.when(pl.program_id(0) % per_seq == 0)
    def _():
        carry[...] = incoming[0]

    same, marks = head_square(), head_rows()
    causal, _ = causal_masks()
    prefix[0] = carry[...].astype(LOW)
    for g in groups(queries.shape[1]):
        q, k, v = queries[:, g], keys[:, g], values[:, g]
        scores = (dot_nt(q, split_heads(k, marks)) * causal).astype(LOW)
        out = dot_nn(scores, split_heads(v, marks))
        out += dot_nn(q, open_state(carry[:, g], same))
        attended[:, g] = out.astype(LOW)
        carry[:, g] += pack_state(dot_tn(k, v), same)
    rows = attended[...].astype(WIDE)
    gate = jax.nn.sigmoid(pre_gate[...].astype(WIDE))
    rows = (rows * rms_scale(rows) * gain[...] * gate).astype(LOW)
    mixed[...] = rows
    residual[...] = tok[...].astype(WIDE) + dot_nn(rows, w_out[...])


def feed_kernel(
    per_seq, turned, lengths, residual, cotangent, w_one, w_two, w_three, w_out, gain, pre_gate,
    attended, queries,
    layer_out, normed, glu, grad_one, grad_two, upstream_low, grad_residual, gated,
    grad_attended, totals, grad_gain, held=None,
):
    step = pl.program_id(0)
    row_count = residual.shape[0]
    spot = lax.broadcasted_iota(jnp.int32, (row_count, 1), 0) + (step % per_seq) * row_count
    limit = lengths[step // per_seq] - lax.axis_index("fsdp") * per_seq * row_count
    valid = (spot < limit).astype(WIDE)
    res = residual[...]
    scale = rms_scale(res)
    rows = (res * scale).astype(LOW)
    normed[...] = rows.T if turned else rows
    upstream = cotangent[...].astype(WIDE) * valid
    up_low = upstream.astype(LOW)
    upstream_low[...] = up_low
    for c in groups(w_one.shape[1]):
        one = dot_nn(rows, w_one[:, c])
        two = dot_nn(rows, w_two[:, c])
        back = dot_nt(up_low, w_three[c, :])
        product = (one * two).astype(LOW)
        if turned:
            held[:, c] = product
            glu[c, :] = product.T
        else:
            glu[:, c] = product
        grad_one[:, c] = (back * two).astype(LOW)
        grad_two[:, c] = (back * one).astype(LOW)
    layer_out[...] = (valid * (res + dot_nn(held[...] if turned else glu[...], w_three[...]))).astype(LOW)
    back = dot_nt(grad_one[...], w_one[...]) + dot_nt(grad_two[...], w_two[...])
    grad = upstream + norm_back(res, scale, back)
    grad_residual[...] = grad
    grad = grad.astype(LOW)
    width = grad.shape[1]
    gated[:, :width] = grad
    grad = dot_nt(grad, w_out[...])
    gate = jax.nn.sigmoid(pre_gate[...].astype(WIDE))
    att = attended[...].astype(WIDE)
    scale = rms_scale(att)
    hat = att * scale
    grad = grad * gate

    @pl.when(step == 0)
    def _():
        grad_gain[...] = jnp.zeros_like(grad_gain)

    grad_gain[...] += jnp.sum(grad * hat, axis=0, keepdims=True)
    grad = grad * gain[...]
    gated[:, width:] = (grad * hat * (1.0 - gate)).astype(LOW)
    grad_att = norm_back(att, scale, grad).astype(LOW)
    grad_attended[...] = grad_att

    @pl.when(step % per_seq == 0)
    def _():
        totals[...] = jnp.zeros_like(totals)

    same = head_square()
    for g in groups(grad_att.shape[1]):
        totals[0, :, g] += pack_state(dot_tn(queries[:, g], grad_att[:, g]), same)


def attend_back_kernel(
    per_seq, queries, keys, values, grad_attended, pre_query, pre_key, prefix, incoming,
    grad_query, grad_key, grad_value, carry,
):
    @pl.when(pl.program_id(0) % per_seq == 0)
    def _():
        carry[...] = incoming[0]

    same, marks = head_square(), head_rows()
    causal, causal_t = causal_masks()
    for g in groups(queries.shape[1]):
        q, k, v, ga = queries[:, g], keys[:, g], values[:, g], grad_attended[:, g]
        qs, ks, vs, gs = (split_heads(rows, marks) for rows in (q, k, v, ga))
        state = open_state(prefix[0, :, g].astype(WIDE), same)
        grad_state = open_state(carry[:, g], same)
        grad_scores = (dot_nt(ga, vs) * causal).astype(LOW)
        gq = dot_nn(grad_scores, ks) + dot_nt(ga, state)
        grad_scores = (dot_nt(v, gs) * causal_t).astype(LOW)
        gk = dot_nn(grad_scores, qs) + dot_nt(v, grad_state)
        scores = (dot_nt(k, qs) * causal_t).astype(LOW)
        gv = dot_nn(scores, gs) + dot_nn(k, grad_state)
        grad_query[:, g] = (gq * silu_slope(pre_query[:, g].astype(WIDE))).astype(LOW)
        grad_key[:, g] = (gk * silu_slope(pre_key[:, g].astype(WIDE))).astype(LOW)
        grad_value[:, g] = gv.astype(LOW)
        carry[:, g] += pack_state(dot_tn(q, ga), same)


def input_kernel(
    grad_query, grad_key, grad_value, grad_gate, w_query, w_key, w_value, w_gate, tok,
    grad_residual, input_grad,
):
    grad = dot_nt(grad_query[...], w_query[...]) + dot_nt(grad_key[...], w_key[...])
    grad += dot_nt(grad_value[...], w_value[...]) + dot_nt(grad_gate[...], w_gate[...])
    x = tok[...].astype(WIDE)
    input_grad[...] = grad_residual[...] + norm_back(x, rms_scale(x), grad)


def rows_spec(width, block=BLOCK, order=lambda i: i):
    return pl.BlockSpec((block, width), lambda i: (order(i), 0))


def whole_spec(array):
    rank = array.ndim
    return pl.BlockSpec(array.shape, lambda i: (0,) * rank, pipeline_mode=pl.Buffered(1))


def call(kernel, steps, operands, results, scratch=(), flops=0, limit=56):
    moved = sum(a.size * a.dtype.itemsize for a, _ in operands)
    return pl.pallas_call(
        kernel,
        grid=(steps,),
        in_specs=[spec for _, spec in operands],
        out_specs=[spec for _, _, spec in results],
        out_shape=[jax.ShapeDtypeStruct(shape, dtype) for shape, dtype, _ in results],
        scratch_shapes=list(scratch),
        compiler_params=pltpu.CompilerParams(
            dimension_semantics=("arbitrary",), vmem_limit_bytes=limit << 20
        ),
        cost_estimate=pl.CostEstimate(flops=flops, bytes_accessed=moved, transcendentals=0),
    )(*[a for a, _ in operands])


def index_bits():
    bits = []
    for axis in ("dp", "fsdp"):
        count = lax.axis_size(axis).bit_length() - 1
        bits += [(axis, bit) for bit in reversed(range(count))]
    return bits


LINKS = {
    "1": (("dp", 3),),
    "0": (("dp", 2),),
    "z": (("dp", 3), ("dp", 2)),
    "y": (("dp", 1),),
    "x": (("fsdp", 0),),
}
CORE = ("dp", 0)
SIDE = ("fsdp", 0)


def bit_value(bit):
    axis, at = bit
    return lax.rem(lax.div(lax.axis_index(axis), 1 << at), 2)


def flips_of(name):
    group = LINKS[name]
    if len(group) == 1:
        return [group]
    return [group[:1], group[1:], group]


def flip_device(flips):
    place = {}
    for axis, at in flips:
        moved = place.get(axis, lax.axis_index(axis))
        place[axis] = moved + (1 - 2 * bit_value((axis, at))) * (1 << at)
    return place


def greet(bits, far=True):
    partners = [(bit,) for bit in bits] + ([LINKS["z"]] if far else [])
    barrier = pltpu.get_barrier_semaphore()
    for flips in partners:
        pl.semaphore_signal(
            barrier, inc=1, device_id=flip_device(flips), device_id_type=pl.DeviceIdType.MESH
        )
    pl.semaphore_wait(barrier, len(partners))


class Sems:
    def __init__(self, send, recv):
        self.send, self.recv, self.used = send, recv, 0

    def copy(self, src, dst, flips):
        at = self.used
        self.used += 1
        return pltpu.make_async_remote_copy(
            src_ref=src,
            dst_ref=dst,
            send_sem=self.send.at[at],
            recv_sem=self.recv.at[at],
            device_id=flip_device(flips),
            device_id_type=pl.DeviceIdType.MESH,
        )


class Gather:
    def __init__(self, buf, bits, order, sems, columns=slice(None)):
        self.stages, held = [], []

        def cube(flips=()):
            index = []
            for bit in bits:
                if bit in held:
                    index.append(slice(None))
                else:
                    index.append(1 - bit_value(bit) if bit in flips else bit_value(bit))
            return buf.at[tuple(index) + (slice(None), columns)]

        for n, name in enumerate(order):
            ref, flips = cube(), flips_of(name)
            self.stages.append([sems.copy(ref, ref, flip) for flip in flips])
            if n == len(order) - 1:
                self.near = sems.copy(ref, ref, (CORE,))
                far = [cube(flip) for flip in flips]
                self.stages.append([sems.copy(ref, ref, (CORE,)) for ref in far])
            held.extend(LINKS[name])

    def start(self, k):
        for copy in self.stages[k]:
            copy.start()
        if k == len(self.stages) - 2:
            self.near.start()

    def advance(self, k):
        if k:
            for copy in self.stages[k - 1]:
                copy.wait_recv()
        self.start(k)

    def finish(self):
        self.near.wait_recv()
        for copy in self.stages[-1]:
            copy.wait_recv()

    def drain(self):
        for copy in [c for stage in self.stages for c in stage] + [self.near]:
            copy.wait_send()


class Scatter:
    def __init__(self, sems, bits, order, acc, send, come, recvs, columns, slots):
        self.bits, self.order, self.acc, self.columns = bits, order, acc, columns
        self.come, self.recvs, self.slots = come, recvs, slots
        rows = (slice(None),)
        full = (slice(None),) * len(bits) + rows
        self.core = sems.copy(send.at[full + (slots,)], come.at[full + (slots,)], (CORE,))
        self.copies, self.done = [], []
        for k, name in enumerate(order):
            (bit,) = LINKS[name]
            done = [LINKS[n][0] for n in order[:k]]
            index = tuple(
                1 - bit_value(b) if b == bit else bit_value(b) if b in done else slice(None)
                for b in bits
            )
            free = (slice(None),) * (len(bits) - k - 1)
            source = acc.at[index + rows + (columns,)]
            self.copies.append(sems.copy(source, recvs[k].at[free + rows + (columns,)], (bit,)))
            self.done.append(done)

    def add(self, done, source, columns):
        free = [b for b in self.bits if b not in done]

        def one(k):
            at = [(k // (1 << (len(free) - 1 - n))) % 2 for n in range(len(free))]
            mine = tuple(bit_value(b) if b in done else at[free.index(b)] for b in self.bits)
            here = mine + (slice(None), self.columns)
            self.acc[here] = self.acc[here] + source[tuple(at) + (slice(None), columns)]

        if len(free) <= 2:
            for k in range(1 << len(free)):
                one(k)
        else:
            lax.fori_loop(0, 1 << len(free), lambda k, c: (one(k), c)[1], 0)

    def launch(self):
        self.core.start()

    def advance(self, k):
        if k == 0:
            self.core.wait_recv()
            self.add([], self.come, self.slots)
        else:
            self.copies[k - 1].wait_recv()
            self.add(self.done[k - 1] + [LINKS[self.order[k - 1]][0]], self.recvs[k - 1], self.columns)
        self.copies[k].start()

    def result(self):
        self.copies[-1].wait_recv()
        own = tuple(bit_value(b) for b in self.bits)
        here = (slice(None), self.columns)
        return self.acc[own + here].astype(WIDE) + self.recvs[-1][here].astype(WIDE)

    def drain(self, core=True):
        if core:
            self.core.wait_send()
        for copy in self.copies:
            copy.wait_send()


def run_events(step, events):
    for at in sorted(events):

        @pl.when(step == at)
        def _():
            for action in events[at]:
                action()


def planned(table, pieces, low, high):
    events = {}
    for at, todo in table:
        if low <= at < high:
            events[at] = [functools.partial(pieces[name].advance, k) for name, k in todo]
    return events


FORWARD_PLAN = (
    (0, (
        ("a00", 0), ("f5", 0), ("a02", 0), ("a02", 1), ("a01", 0), ("f3", 0), ("f0", 0),
        ("a00", 1), ("f5", 1), ("a22", 0), ("a10", 0), ("a01", 1), ("a21", 0), ("a02", 2),
        ("a22", 1), ("a00", 2), ("a11", 0), ("a10", 1), ("a02", 3), ("a20", 0), ("a01", 2),
        ("a20", 1), ("a12", 0), ("f1", 0), ("a21", 1), ("a12", 1), ("f2", 0), ("a10", 2),
        ("a00", 3), ("a22", 2), ("a20", 2), ("a11", 1), ("a02", 4), ("a12", 2), ("a01", 3),
    )),
    (1, (("a22", 3), ("a21", 2),)),
    (2, (("a11", 2),)),
    (3, (("a12", 3), ("f0", 1),)),
    (4, (("a20", 3),)),
    (5, (("a22", 4), ("f2", 1),)),
    (6, (("f1", 1), ("a20", 4),)),
    (7, (("a21", 3),)),
    (8, (("a11", 3), ("f3", 1), ("a12", 4), ("f4", 0), ("a10", 3),)),
    (9, (("f0", 2), ("f2", 2),)),
    (11, (("f1", 2), ("f4", 1),)),
    (12, (("f3", 2),)),
    (13, (("f5", 2),)),
    (14, (("f0", 3),)),
    (15, (("f2", 3),)),
    (16, (("f1", 3), ("f3", 3),)),
    (17, (("f4", 2),)),
    (23, (("f4", 3), ("f5", 3),)),
)
FEED_BACK_PLAN = (
    (11, (("three0", 0),)),
    (12, (("three1", 0),)),
    (13, (("one0", 0),)),
    (16, (("two0", 0),)),
    (17, (("three0", 1), ("one1", 0), ("one0", 1),)),
    (18, (("two1", 0),)),
    (20, (("three1", 1), ("two0", 1),)),
    (22, (("one0", 2), ("one2", 0),)),
    (23, (("one1", 1), ("two2", 0),)),
    (25, (("three1", 2), ("two1", 1),)),
    (28, (("one1", 2), ("one2", 1), ("two0", 2),)),
    (29, (("two2", 1), ("three0", 2),)),
    (30, (("one1", 3),)),
    (31, (("two1", 2), ("one2", 2), ("three1", 3),)),
    (32, (("two2", 2), ("two0", 3), ("one0", 3), ("three0", 3),)),
    (33, (("two1", 3),)),
    (34, (("one2", 3), ("two2", 3),)),
)
ATTEND_BACK_PLAN = (
    (4, (("p0", 0),)),
    (5, (("p1", 0), ("p2", 0),)),
    (7, (("p3", 0),)),
    (9, (("p4", 0),)),
    (10, (("p5", 0), ("p0", 1),)),
    (11, (("p2", 1), ("p1", 1), ("p6", 0),)),
    (12, (("p0", 2), ("p3", 1),)),
    (13, (("p4", 1),)),
    (14, (("p1", 2), ("p5", 1), ("p2", 2),)),
    (15, (("p6", 1), ("p3", 2), ("p2", 3),)),
    (16, (("p1", 3), ("p5", 2), ("p3", 3),)),
    (17, (("p6", 2), ("p4", 2),)),
    (18, (("p0", 3), ("p5", 3), ("p6", 3), ("p4", 3),)),
)


HALF = BLOCK // 2


def causal_pair(a, firsts, seconds, later):
    row = lax.broadcasted_iota(jnp.int32, (HALF, HEADS * HALF), 0)
    col = lax.broadcasted_iota(jnp.int32, (HALF, HEADS * HALF), 1) % HALF
    if later:
        mask = (row >= col).astype(WIDE)
        full, part = dot_nt(a, firsts), dot_nt(a[HALF:], seconds)
        full = [(full[:HALF] * mask).astype(LOW), full[HALF:].astype(LOW)]
    else:
        mask = (col >= row).astype(WIDE)
        full, part = dot_nt(a, seconds), dot_nt(a[:HALF], firsts)
        full = [full[:HALF].astype(LOW), (full[HALF:] * mask).astype(LOW)]
    return jnp.concatenate(full, axis=0), (part * mask).astype(LOW)


def causal_apply(scores, firsts, seconds, later, carried):
    full, part = scores
    if later:
        total = dot_nn(full, firsts) + carried
        return jnp.concatenate([total[:HALF], total[HALF:] + dot_nn(part, seconds)], axis=0)
    total = dot_nn(full, seconds) + carried
    return jnp.concatenate([total[:HALF] + dot_nn(part, firsts), total[HALF:]], axis=0)


def attend_back_step(
    same, queries, keys, values, grad_attended, pre_query, pre_key, prefix, grads, carry, middle,
):
    marks = head_rows()
    width = queries.shape[1]
    for g in groups(width):
        if g.start == width // 2:
            middle()
        q, k, v, ga = queries[:, g], keys[:, g], values[:, g], grad_attended[:, g]
        qs, ks, vs, gs = (
            (split_heads(rows[:HALF], marks), split_heads(rows[HALF:], marks))
            for rows in (q, k, v, ga)
        )
        state = open_state(prefix[0, :, g].astype(WIDE), same)
        grad_state = open_state(carry[:, g], same)
        gq = causal_apply(causal_pair(ga, *vs, True), *ks, True, dot_nt(ga, state))
        gk = causal_apply(causal_pair(v, *gs, False), *qs, False, dot_nt(v, grad_state))
        gv = causal_apply(causal_pair(k, *qs, False), *gs, False, dot_nn(k, grad_state))
        gq = gq * silu_slope(pre_query[:, g].astype(WIDE))
        gk = gk * silu_slope(pre_key[:, g].astype(WIDE))
        for n, grad in enumerate((gq, gk, gv)):
            grads[:, n * width + g.start : n * width + g.stop] = grad.astype(LOW)
        carry[:, g] += pack_state(dot_tn(q, ga), same)


def clip(value, low, high):
    return jnp.minimum(jnp.maximum(value, low), high)


CHUNK = 256
PAIRS = (3, 4, 4)
PAIR_ORDERS = (("x01y", "x01y"), ("y0x1", "x0y1"), ("xy10", "yx01"))
THREE_ORDERS = ("y10", "0y1")
THREE_AFTER = 0


def feed_back_blocks():
    pairs, three, at = [], None, 0
    for n, count in enumerate(PAIRS):
        if n == THREE_AFTER:
            three = (at, 8)
            at += 8
        pairs.append((at, count))
        at += count
    return pairs, three, at


class ThreeScatter(Scatter):
    def last_swap(self, sems, out, give, take):
        self.out, self.give, self.take = out, give, take
        cols = self.columns
        self.swap = sems.copy(give.at[:, cols], take.at[:, cols], (SIDE,))

    def advance(self, k):
        if k < len(self.order):
            super().advance(k)
            return
        cols = self.columns
        total = self.result()
        deep = total.shape[0] // 2
        low, high = total[:deep], total[deep:]
        upper = bit_value(SIDE).astype(WIDE)
        self.out[:, cols] = low * (1 - upper) + high * upper
        self.give[:, cols] = low * upper + high * (1 - upper)
        self.swap.start()

    def finish(self):
        self.swap.wait_recv()
        self.out[:, self.columns] += self.take[:, self.columns]
        self.swap.wait_send()


def feed_back_kernel(
    per_seq, bits,
    normed_hbm, grad_one, grad_two, glu, upstream_hbm,
    queries, keys, values, grad_attended, pre_query, pre_key, prefix, totals,
    out_one, out_two, out_three, grads,
    normed, upstream, acc, come1, come2, come3, come4, send, come,
    acc3, come31, come32, come33, send3, take3, last_send, last_come,
    state_out, state_in, carry, part, part3, send_sems, recv_sems, local,
):
    step = pl.program_id(0)
    pairs, three_block, base = feed_back_blocks()
    links = [bit for bit in bits if bit != CORE]
    mine, side = bit_value(CORE), bit_value(SIDE)
    other = 1 - mine
    sems = Sems(send_sems, recv_sems)
    hidden, width = out_one.shape[1], out_three.shape[1]
    recvs = (come1, come2, come3, come4)
    pieces, ends, first = {}, [], 0
    for n, count in enumerate(PAIRS):
        for w, (name, out) in enumerate((("one", out_one), ("two", out_two))):
            begin = w * hidden + first * CHUNK
            span = count * CHUNK
            pieces[f"{name}{n}"] = Scatter(
                sems, links, PAIR_ORDERS[n][w], acc, send.at[n % 2, w], come.at[n, w], recvs,
                slice(begin, begin + span), slice(0, span),
            )
            ends.append((pieces[f"{name}{n}"], out, first * CHUNK))
        first += count
    half = width // 2
    threes = []
    for n in range(2):
        cols = slice(n * half, (n + 1) * half)
        piece = ThreeScatter(
            sems, links[:-1], THREE_ORDERS[n], acc3, send3, take3, (come31, come32, come33),
            cols, cols,
        )
        piece.last_swap(sems, out_three, last_send, last_come)
        pieces[f"three{n}"] = piece
        threes.append(piece)
    swap_state = sems.copy(state_out, state_in, (SIDE,))
    load = [
        pltpu.make_async_copy(normed_hbm, normed, local.at[0]),
        pltpu.make_async_copy(upstream_hbm, upstream, local.at[1]),
    ]

    @pl.when(step == 0)
    def _():
        for copy in load:
            copy.start()
        greet(bits, far=False)
        state_out[...] = totals[...].astype(LOW)
        swap_state.start()

    for first_use, copy in ((pairs[0][0], load[0]), (three_block[0], load[1])):

        @pl.when(step == first_use)
        def _():
            copy.wait()

    for n in range(2, len(PAIRS)):

        @pl.when(step == pairs[n][0])
        def _():
            pieces[f"one{n - 2}"].core.wait_send()
            pieces[f"two{n - 2}"].core.wait_send()

    later = planned(FEED_BACK_PLAN, pieces, base, base + 16)
    at_start = {base + (at - base) // 2: todo for at, todo in later.items() if (at - base) % 2 == 0}
    at_middle = {base + (at - base) // 2: todo for at, todo in later.items() if (at - base) % 2}

    @pl.when(step < base)
    def _():
        run_events(step, planned(FEED_BACK_PLAN, pieces, 0, base))

    @pl.when(step >= base)
    def _():
        run_events(step, at_start)

    lead = acc.shape[:-1]
    fill = (slice(None),) * len(lead)

    def weight_chunk(w, rhs, chunk, group, first):
        part[...] = dot_nn(normed[...], rhs[...]).astype(LOW).reshape(part.shape)
        at = pl.ds(pl.multiple_of(chunk * CHUNK, CHUNK), CHUNK)
        send[(group % 2, w) + fill + (at,)] = part[:, other].reshape(lead + (CHUNK,))
        at = pl.ds(pl.multiple_of(w * hidden + (first + chunk) * CHUNK, CHUNK), CHUNK)
        acc[fill + (at,)] = part[:, mine].reshape(lead + (CHUNK,))

    first = 0
    for n, (begin, count) in enumerate(pairs):

        @pl.when((step >= begin) & (step < begin + count))
        def _():
            weight_chunk(0, grad_one, step - begin, n, first)
            weight_chunk(1, grad_two, step - begin, n, first)

        @pl.when(step == begin + count - 1)
        def _():
            pieces[f"one{n}"].launch()
            pieces[f"two{n}"].launch()

        first += count

    begin, count = three_block

    @pl.when((step >= begin) & (step < begin + count))
    def _():
        k = step - begin
        at = tuple((k // (1 << (2 - d))) % 2 for d in range(3))
        part3[...] = dot_nn(glu[...], upstream[...]).astype(LOW).reshape(part3.shape)
        send3[at] = part3[other]
        acc3[at] = part3[mine]

    @pl.when(step == begin + count - 1)
    def _():
        for piece in threes:
            piece.launch()

    @pl.when(step >= base)
    def _():
        at = step - base

        @pl.when(at == 0)
        def _():
            swap_state.wait_recv()

        @pl.when(at % per_seq == 0)
        def _():
            carry[...] = state_in[at // per_seq].astype(WIDE) * (1 - side).astype(WIDE)

        attend_back_step(
            head_square(), queries, keys, values, grad_attended, pre_query, pre_key, prefix,
            grads, carry, lambda: run_events(step, at_middle),
        )

    @pl.when(step == pl.num_programs(0) - 1)
    def _():
        for actions in planned(FEED_BACK_PLAN, pieces, base + 16, 1000).values():
            for action in actions:
                action()
        for piece, out, begin in ends:
            span = piece.columns.stop - piece.columns.start
            out[:, begin : begin + span] = piece.result()
        for n in range(len(PAIRS)):
            for name in ("one", "two"):
                pieces[f"{name}{n}"].drain(core=n + 2 >= len(PAIRS))
        for piece in threes:
            piece.finish()
            piece.drain()
        swap_state.wait_send()


def feed_back(
    seq_count, normed, grad_one, grad_two, glu, upstream, queries, keys, values, grad_attended,
    pre_query, pre_key, prefix, totals,
):
    row_count, width = queries.shape
    hidden = grad_one.shape[1]
    steps = row_count // BLOCK
    per_seq = steps // seq_count
    bits = index_bits()
    pairs, three, base = feed_back_blocks()
    deep = hidden // 8
    slab = width // 32

    def pair_at(i):
        done = sum(clip(i - begin, 0, count) for begin, count in pairs)
        return jnp.minimum(done, sum(PAIRS) - 1)

    def back(i):
        at = clip(i - base, 0, steps - 1)
        return (at // per_seq) * per_seq + per_seq - 1 - at % per_seq

    rows = pl.BlockSpec((BLOCK, width), lambda i: (back(i), 0))
    pair = pl.BlockSpec((row_count, CHUNK), lambda i: (0, pair_at(i)))
    vmem = pl.BlockSpec(memory_space=pltpu.VMEM)
    hbm = pl.BlockSpec(memory_space=pl.ANY)
    low = functools.partial(pltpu.VMEM, dtype=LOW)
    span = max(PAIRS) * CHUNK
    copies = 10 * len(PAIRS) + 2 * 5 + 1
    return pl.pallas_call(
        functools.partial(feed_back_kernel, per_seq, bits),
        grid=(base + steps,),
        in_specs=[
            hbm, pair, pair,
            pl.BlockSpec((deep, row_count), lambda i: (clip(i - three[0], 0, 7), 0)),
            hbm,
        ]
        + [rows] * 6
        + [pl.BlockSpec((1, HD, width), lambda i: (back(i), 0, 0)), vmem],
        out_specs=[vmem] * 3 + [pl.BlockSpec((BLOCK, 3 * width), lambda i: (back(i), 0))],
        out_shape=[
            jax.ShapeDtypeStruct((slab, hidden), WIDE),
            jax.ShapeDtypeStruct((slab, hidden), WIDE),
            jax.ShapeDtypeStruct((hidden // 32, width), WIDE),
            jax.ShapeDtypeStruct((row_count, 3 * width), LOW),
        ],
        scratch_shapes=[
            low((width, row_count)),
            low((row_count, width)),
            low((2, 2, 2, 2, slab, 2 * hidden)),
            low((2, 2, 2, slab, 2 * hidden)),
            low((2, 2, slab, 2 * hidden)),
            low((2, slab, 2 * hidden)),
            low((slab, 2 * hidden)),
            low((2, 2, 2, 2, 2, 2, slab, span)),
            low((len(PAIRS), 2, 2, 2, 2, 2, slab, span)),
            low((2, 2, 2, deep // 2, width)),
            low((2, 2, deep // 2, width)),
            low((2, deep // 2, width)),
            low((deep // 2, width)),
            low((2, 2, 2, deep // 2, width)),
            low((2, 2, 2, deep // 2, width)),
            pltpu.VMEM((hidden // 32, width), WIDE),
            pltpu.VMEM((hidden // 32, width), WIDE),
            low((seq_count, HD, width)),
            low((seq_count, HD, width)),
            pltpu.VMEM((HD, width), WIDE),
            low((8, 2, width // 16, CHUNK)),
            low((2, deep // 2, width)),
            pltpu.SemaphoreType.DMA((copies,)),
            pltpu.SemaphoreType.DMA((copies,)),
            pltpu.SemaphoreType.DMA((2,)),
        ],
        compiler_params=pltpu.CompilerParams(
            dimension_semantics=("arbitrary",),
            vmem_limit_bytes=63 << 20,
            collective_id=2,
            has_side_effects=True,
        ),
        cost_estimate=pl.CostEstimate(
            flops=6 * row_count * width * hidden + 12 * row_count * width * width,
            bytes_accessed=128 << 20,
            transcendentals=0,
        ),
    )(
        normed, grad_one, grad_two, glu, upstream, queries, keys, values, grad_attended,
        pre_query, pre_key, prefix, totals,
    )


WIDE_CHUNK = 512
PARTS = (1, 2, 1, 1, 2, 1, 2)
PART_ORDERS = ("yx10", "yx01", "0xy1", "x0y1", "01xy", "yx01", "yx01")


def attend_weights_kernel(
    bits,
    normed_hbm, mixed_hbm, gated, grads, gain_term, rows_three, rows_gate, weights_hbm, tok,
    grad_residual,
    out, input_grad,
    normed, mixed, weights, acc, come1, come2, come3, come4, send, come, part,
    send_sems, recv_sems, local,
):
    step = pl.program_id(0)
    links = [bit for bit in bits if bit != CORE]
    mine = bit_value(CORE)
    other = 1 - mine
    sems = Sems(send_sems, recv_sems)
    width = tok.shape[1]
    per = width // WIDE_CHUNK
    chunks = 5 * per
    lead = acc.shape[:-1]
    fill = (slice(None),) * len(lead)

    def column(chunk):
        return chunk * WIDE_CHUNK + (128 if chunk >= per else 0)

    pieces, first = {}, 0
    launches = {}
    for n, count in enumerate(PARTS):
        cols = slice(column(first), column(first + count))
        first += count
        pieces[f"p{n}"] = Scatter(
            sems, links, PART_ORDERS[n], acc, send, come, (come1, come2, come3, come4), cols, cols
        )
        launches[first - 1] = [pieces[f"p{n}"].launch]
    load = [
        pltpu.make_async_copy(mixed_hbm, mixed, local.at[0]),
        pltpu.make_async_copy(normed_hbm, normed, local.at[1]),
        pltpu.make_async_copy(weights_hbm.at[:, : 4 * width], weights, local.at[2]),
    ]

    @pl.when(step == 0)
    def _():
        for copy in load:
            copy.start()
        greet(bits, far=False)
        load[0].wait()

    @pl.when(step == per)
    def _():
        load[1].wait()

    @pl.when(step == chunks)
    def _():
        load[2].wait()

    run_events(step, planned(ATTEND_BACK_PLAN, pieces, 0, chunks + 8))

    def chunk_phase(begin, end, lhs, rhs, shift):
        @pl.when((step >= begin) & (step < end))
        def _():
            at = pl.ds(pl.multiple_of(step * WIDE_CHUNK + shift, 128), WIDE_CHUNK)
            part[...] = dot_nn(lhs[...], rhs[...]).astype(LOW).reshape(part.shape)
            send[fill + (at,)] = part[:, other].reshape(lead + (WIDE_CHUNK,))
            acc[fill + (at,)] = part[:, mine].reshape(lead + (WIDE_CHUNK,))

    chunk_phase(0, per, mixed, gated, 0)
    chunk_phase(per, 2 * per, normed, gated, 128)
    chunk_phase(2 * per, chunks, normed, grads, 128)

    @pl.when(step == 0)
    def _():
        column = jnp.broadcast_to(gain_term[...], (128, width)).T
        column = column.reshape(8, 2, width // 16, 128)
        upper = mine.astype(WIDE)
        low, high = column[:, 0], column[:, 1]
        at = fill + (slice(width, width + 128),)
        acc[at] = (low * (1 - upper) + high * upper).astype(LOW).reshape(lead + (128,))
        send[at] = (low * upper + high * (1 - upper)).astype(LOW).reshape(lead + (128,))

    run_events(step, launches)

    @pl.when(step >= chunks)
    def _():
        def weight(n):
            return weights[:, n * width : (n + 1) * width]

        def row(n):
            return rows_three[:, n * width : (n + 1) * width]

        grad = dot_nt(row(0), weight(2)) + dot_nt(row(1), weight(0))
        grad += dot_nt(row(2), weight(1)) + dot_nt(rows_gate[...], weight(3))
        x = tok[...].astype(WIDE)
        grad = grad_residual[...] + norm_back(x, rms_scale(x), grad)
        input_grad[...] = grad.astype(input_grad.dtype)

    @pl.when(step == pl.num_programs(0) - 1)
    def _():
        for actions in planned(ATTEND_BACK_PLAN, pieces, chunks + 8, 1000).values():
            for action in actions:
                action()
        for piece in pieces.values():
            out[:, piece.columns] = piece.result()
        for piece in pieces.values():
            piece.drain()


def attend_weights(normed, mixed, gated, grads, gain_term, full_attn, tok, grad_residual):
    row_count, width = tok.shape
    steps = row_count // BLOCK
    bits = index_bits()
    per = width // WIDE_CHUNK
    chunks = 5 * per
    slab = width // 32
    vmem = pl.BlockSpec(memory_space=pltpu.VMEM)
    hbm = pl.BlockSpec(memory_space=pl.ANY)

    def rows(size, column=0):
        return pl.BlockSpec((BLOCK, size), lambda i: (clip(i - chunks, 0, steps - 1), column))

    def chunk(begin, count):
        return pl.BlockSpec(
            (row_count, WIDE_CHUNK), lambda i: (0, clip(i - begin, 0, count - 1))
        )

    low = functools.partial(pltpu.VMEM, dtype=LOW)
    columns = 5 * width + 128
    copies = 5 * len(PARTS)
    return pl.pallas_call(
        functools.partial(attend_weights_kernel, bits),
        grid=(chunks + steps,),
        in_specs=[hbm, hbm, chunk(0, 2 * per), chunk(2 * per, 3 * per), vmem, rows(3 * width),
                  rows(width, 1), hbm, rows(width), rows(width)],
        out_specs=[vmem, rows(width)],
        out_shape=[
            jax.ShapeDtypeStruct((slab, columns), WIDE),
            jax.ShapeDtypeStruct((row_count, width), LOW),
        ],
        scratch_shapes=[
            low((width, row_count)),
            low((width, row_count)),
            low((width, 4 * width)),
            low((2, 2, 2, 2, slab, columns)),
            low((2, 2, 2, slab, columns)),
            low((2, 2, slab, columns)),
            low((2, slab, columns)),
            low((slab, columns)),
            low((2, 2, 2, 2, slab, columns)),
            low((2, 2, 2, 2, slab, columns)),
            low((8, 2, width // 16, WIDE_CHUNK)),
            pltpu.SemaphoreType.DMA((copies,)),
            pltpu.SemaphoreType.DMA((copies,)),
            pltpu.SemaphoreType.DMA((3,)),
        ],
        compiler_params=pltpu.CompilerParams(
            dimension_semantics=("arbitrary",),
            vmem_limit_bytes=62 << 20,
            collective_id=3,
            has_side_effects=True,
        ),
        cost_estimate=pl.CostEstimate(
            flops=18 * row_count * width * width, bytes_accessed=64 << 20, transcendentals=0
        ),
    )(normed, mixed, gated, grads, gain_term, grads, gated, full_attn, tok, grad_residual)


ATTEND_PIECES = (
    (("a00", "zxy", 7), ("a01", "zyx", 6), ("a02", "1yx0", 3)),
    (("a10", "zxy", 6), ("a11", "zxy", 7), ("a12", "1xy0", 3)),
    (("a20", "1y0x", 1), ("a21", "zyx", 7), ("a22", "y1x0", 1)),
)
FEED_PIECES = (
    (("f0", "yzx", 6), ("f1", "zyx", 16)),
    (("f2", "zxy", 11), ("f3", "xzy", 11)),
)
THREE_PIECES = (("f4", "zy", 4), ("f5", "yz", 4))
FORWARD_COPIES = 128


class ThreeGather(Gather):
    def first_swap(self, sems, columns, give, take, slab, target, local):
        self.cols, self.give, self.take, self.slab = columns, give, take, slab
        self.swap = sems.copy(give.at[:, columns], take.at[:, columns], (SIDE,))
        self.place = pltpu.make_async_copy(slab.at[:, columns], target.at[:, columns], local)

    def advance(self, k):
        if k == 0:
            self.swap.start()
            return
        if k == 1:
            self.swap.wait_recv()
            upper = bit_value(SIDE).astype(WIDE)
            mine, theirs = self.give[:, self.cols], self.take[:, self.cols]
            low = mine * (1 - upper) + theirs * upper
            high = mine * upper + theirs * (1 - upper)
            self.slab[:, self.cols] = jnp.concatenate([low, high], axis=0).astype(LOW)
            self.place.start()
            self.place.wait()
        super().advance(k - 1)

    def drain(self):
        super().drain()
        self.swap.wait_send()


def forward_kernel(
    steps, per_seq, bits,
    tok, s_key, s_value, s_query, s_gate, s_out, s_gain, s_one, s_two, s_three,
    normed, pre_key, keys, values, pre_query, queries, pre_gate, attended, mixed, residual,
    normed_two, up_one, up_two, glu, prefix, gain_row, full_attn, full_one, full_two, full_three,
    held, held_one, held_two, all_keys, all_values, all_normed, totals, state_out, state_in, carry,
    three_out, three_in, three_slab, send, recv, local,
):
    step = pl.program_id(0)
    width = tok.shape[1]
    sems = Sems(send, recv)
    own = tuple(bit_value(bit) for bit in bits)
    side = bit_value(SIDE).astype(WIDE)
    pieces, waves, start = {}, [], 0
    for wave in ATTEND_PIECES:
        waves.append([])
        for name, order, tiles in wave:
            cols = slice(start, start + 128 * tiles)
            start += 128 * tiles
            pieces[name] = Gather(held, bits, order, sems, cols)
            waves[-1].append(pieces[name])
    feed = []
    for buf, parts in zip((held_one, held_two), FEED_PIECES):
        start = 0
        for name, order, tiles in parts:
            cols = slice(start, start + 128 * tiles)
            start += 128 * tiles
            pieces[name] = Gather(buf, bits, order, sems, cols)
            feed.append(pieces[name])
    start, threes = 0, []
    for n, (name, order, tiles) in enumerate(THREE_PIECES):
        cols = slice(start, start + 128 * tiles)
        start += 128 * tiles
        pieces[name] = ThreeGather(full_three, bits[:-1], order, sems, cols)
        pieces[name].first_swap(
            sems, cols, three_out, three_in, three_slab, full_three.at[own[:-1]], local.at[2 + n]
        )
        threes.append(pieces[name])
    swap_state = sems.copy(state_out, state_in, (SIDE,))
    keep_attn = pltpu.make_async_copy(held, full_attn, local.at[4])
    keep_feed = [
        pltpu.make_async_copy(held_one, full_one, local.at[0]),
        pltpu.make_async_copy(held_two, full_two, local.at[1]),
    ]

    @pl.when(step == 0)
    def _():
        place = [
            pltpu.make_async_copy(s_one, held_one.at[own], local.at[0]),
            pltpu.make_async_copy(s_two, held_two.at[own], local.at[1]),
        ]
        for copy in place:
            copy.start()
        for n, shard in enumerate((s_key, s_value, s_query, s_gate, s_out)):
            held[own + (slice(None), slice(n * width, (n + 1) * width))] = shard[...]
        size = s_gain.shape[1]
        row = lax.broadcasted_iota(jnp.int32, (size, size), 0)
        col = lax.broadcasted_iota(jnp.int32, (size, size), 1)
        spread = jnp.broadcast_to(s_gain[...].astype(WIDE), (size, size))
        column = jnp.sum(jnp.where(row == col, spread, 0.0), axis=1, keepdims=True)
        column = jnp.broadcast_to(column, (size, 128)).astype(LOW)
        held[own + (slice(None), slice(5 * width, 5 * width + 128))] = column
        three_out[...] = s_three[...].astype(WIDE)
        greet(bits)
        for copy in place:
            copy.wait()
        for actions in planned(FORWARD_PLAN, pieces, 0, 1).values():
            for action in actions:
                action()
        for piece in waves[0]:
            piece.finish()

    @pl.when(step == steps)
    def _():
        for wave in waves[1:]:
            for piece in wave:
                piece.finish()
        keep_attn.start()
        column = held[..., 5 * width : 5 * width + 128].reshape(width, 128)
        gain_row[...] = column.astype(WIDE).T[:1]

    for n in range(3):

        @pl.when((step >= n * steps) & (step < (n + 1) * steps))
        def _():
            part = planned(FORWARD_PLAN, pieces, n * steps + 1, (n + 1) * steps + 1)
            run_events(step + 1, part)

    @pl.when(step == 2 * steps)
    def _():
        for piece in feed:
            piece.finish()
        for copy in keep_feed:
            copy.start()

    def weight(n):
        return held[..., n * width : (n + 1) * width].reshape(width, width)

    same = head_square()

    @pl.when(step < steps)
    def _():
        x = tok[...].astype(WIDE)
        rows = (x * rms_scale(x)).astype(LOW)
        normed[...] = rows.T
        here = pl.ds(pl.multiple_of(step * BLOCK, BLOCK), BLOCK)
        all_normed[here, :] = rows
        pre = dot_nn(rows, weight(0))
        pre_key[...] = pre.astype(LOW)
        k = jax.nn.silu(pre).astype(LOW)
        keys[...] = k
        all_keys[here, :] = k
        v = dot_nn(rows, weight(1)).astype(LOW)
        values[...] = v
        all_values[here, :] = v
        seq = step // per_seq

        @pl.when(step % per_seq == 0)
        def _():
            totals[seq] = jnp.zeros((HD, width), WIDE)

        for g in groups(width):
            totals[seq, :, g] += pack_state(dot_tn(k[:, g], v[:, g]), same)

    @pl.when(step == steps - 1)
    def _():
        state_out[...] = totals[...].astype(LOW)
        swap_state.start()

    @pl.when((step >= steps) & (step < 2 * steps))
    def _():
        at = step - steps
        here = pl.ds(pl.multiple_of(at * BLOCK, BLOCK), BLOCK)
        rows = all_normed[here, :]
        pre = dot_nn(rows, weight(2))
        pre_query[...] = pre.astype(LOW)
        queries[...] = jax.nn.silu(pre).astype(LOW)
        gate = dot_nn(rows, weight(3))
        pre_gate[...] = gate.astype(LOW)

        @pl.when(at == 0)
        def _():
            swap_state.wait_recv()

        @pl.when(at % per_seq == 0)
        def _():
            carry[...] = state_in[at // per_seq].astype(WIDE) * side

        marks = head_rows()
        prefix[0] = carry[...].astype(LOW)
        for g in groups(width):
            q, k, v = queries[:, g], all_keys[here, g], all_values[here, g]
            ks, vs = (
                (split_heads(part[:HALF], marks), split_heads(part[HALF:], marks))
                for part in (k, v)
            )
            carried = dot_nn(q, open_state(carry[:, g], same))
            out = causal_apply(causal_pair(q, *ks, True), *vs, True, carried)
            attended[:, g] = out.astype(LOW)
            carry[:, g] += pack_state(dot_tn(k, v), same)
        rows = attended[...].astype(WIDE)
        rows = rows * rms_scale(rows) * gain_row[...] * jax.nn.sigmoid(gate)
        rows = rows.astype(LOW)
        mixed[...] = rows.T
        res = tok[...].astype(WIDE) + dot_nn(rows, weight(4))
        residual[...] = res
        rows = (res * rms_scale(res)).astype(LOW)
        all_normed[here, :] = rows
        normed_two[...] = rows.T

    @pl.when(step >= 2 * steps)
    def _():
        here = pl.ds(pl.multiple_of((step - 2 * steps) * BLOCK, BLOCK), BLOCK)
        rows = all_normed[here, :]
        for c in groups(up_one.shape[1]):
            one = dot_nn(rows, held_one[..., c].reshape(width, GROUP))
            two = dot_nn(rows, held_two[..., c].reshape(width, GROUP))
            up_one[:, c] = one.astype(LOW)
            up_two[:, c] = two.astype(LOW)
            glu[c, :] = (one * two).astype(LOW).T

    @pl.when(step == 3 * steps - 1)
    def _():
        for actions in planned(FORWARD_PLAN, pieces, 3 * steps + 1, 1000).values():
            for action in actions:
                action()
        for piece in threes:
            piece.finish()
        for piece in pieces.values():
            piece.drain()
        swap_state.wait_send()
        keep_attn.wait()
        for copy in keep_feed:
            copy.wait()


def forward(tok, seq_count, shards_attn, gain_row, s_one, s_two, s_three):
    row_count, width = tok.shape
    hidden = s_one.shape[1]
    steps = row_count // BLOCK
    per_seq = steps // seq_count
    bits = index_bits()
    lead = (2,) * len(bits)
    slab = s_one.shape[0]
    deep = s_three.shape[0]
    columns = 5 * width + 128

    def phase(n):
        return lambda i: clip(i - n * steps, 0, steps - 1)

    in_rows = rows_spec(width, order=lambda i: jnp.where(i < steps, i, phase(1)(i)))
    first, second = rows_spec(width, order=phase(0)), rows_spec(width, order=phase(1))
    first_turned = pl.BlockSpec((width, BLOCK), lambda i: (0, phase(0)(i)))
    second_turned = pl.BlockSpec((width, BLOCK), lambda i: (0, phase(1)(i)))
    third = rows_spec(hidden, order=phase(2))
    third_turned = pl.BlockSpec((hidden, BLOCK), lambda i: (0, phase(2)(i)))
    big_low = jax.ShapeDtypeStruct((row_count, hidden), LOW)
    any_spec = pl.BlockSpec(memory_space=pl.ANY)
    vmem = pl.BlockSpec(memory_space=pltpu.VMEM)

    def shape(*dims, dtype=LOW):
        return jax.ShapeDtypeStruct(dims, dtype)

    rows_low, turned_low = shape(row_count, width), shape(width, row_count)
    low = functools.partial(pltpu.VMEM, dtype=LOW)
    out = pl.pallas_call(
        functools.partial(forward_kernel, steps, per_seq, bits),
        grid=(3 * steps,),
        in_specs=[in_rows] + [vmem] * 6 + [any_spec] * 2 + [vmem],
        out_specs=[first_turned] + [first] * 3 + [second] * 4 + [second_turned, second]
        + [second_turned, third, third, third_turned]
        + [
            pl.BlockSpec((1, HD, width), lambda i: (phase(1)(i), 0, 0)),
            pl.BlockSpec((1, width), lambda i: (0, 0)),
        ]
        + [any_spec] * 4,
        out_shape=[turned_low] + [rows_low] * 7 + [turned_low]
        + [
            shape(row_count, width, dtype=WIDE),
            turned_low, big_low, big_low, shape(hidden, row_count),
            shape(steps, HD, width),
            shape(1, width, dtype=WIDE),
            shape(*lead, slab, columns),
            shape(*lead, slab, hidden),
            shape(*lead, slab, hidden),
            shape(*lead[:-1], 2 * deep, width),
        ],
        scratch_shapes=[
            low(lead + (slab, columns)),
            low(lead + (slab, hidden)),
            low(lead + (slab, hidden)),
            low((row_count, width)),
            low((row_count, width)),
            low((row_count, width)),
            pltpu.VMEM((seq_count, HD, width), WIDE),
            low((seq_count, HD, width)),
            low((seq_count, HD, width)),
            pltpu.VMEM((HD, width), WIDE),
            pltpu.VMEM((deep, width), WIDE),
            pltpu.VMEM((deep, width), WIDE),
            low((2 * deep, width)),
            pltpu.SemaphoreType.DMA((FORWARD_COPIES,)),
            pltpu.SemaphoreType.DMA((FORWARD_COPIES,)),
            pltpu.SemaphoreType.DMA((5,)),
        ],
        compiler_params=pltpu.CompilerParams(
            dimension_semantics=("arbitrary",),
            vmem_limit_bytes=62 << 20,
            collective_id=1,
            has_side_effects=True,
        ),
        cost_estimate=pl.CostEstimate(
            flops=28 * row_count * width * width, bytes_accessed=128 << 20, transcendentals=0
        ),
    )(tok, *shards_attn, gain_row, s_one, s_two, s_three)
    return list(out[:16]) + [
        out[16].reshape(-1, columns),
        out[17].reshape(-1, hidden),
        out[18].reshape(-1, hidden),
        out[19].reshape(-1, width),
    ]


def plain_shards(
    tokens,
    lengths,
    w_query,
    w_key,
    w_value,
    w_gate,
    out_gain,
    w_out,
    w_one,
    w_two,
    w_three,
    cotangent,
):
    seq_count, local_length, width = tokens.shape
    row_count = seq_count * local_length
    hidden = w_one.shape[1]
    steps = row_count // BLOCK
    per_seq = local_length // BLOCK
    orders = stream_orders()
    tok = tokens.reshape(row_count, width)
    cot = cotangent.reshape(row_count, width)
    full_key = gather_rows(w_key, orders[0])
    full_value = gather_rows(w_value, orders[1])
    full_query = gather_rows(w_query, orders[2])
    full_gate = gather_rows(w_gate, orders[0])
    gain_columns = jnp.broadcast_to(out_gain[:, None], (out_gain.shape[0], 128))
    full_out = gather_rows(jnp.concatenate([w_out, gain_columns], axis=1), orders[1])
    full_one = gather_rows(w_one, orders[2])
    full_two = gather_rows(w_two, orders[0])
    full_three = gather_rows(w_three, orders[1])
    gain = full_out[:, width].astype(WIDE)[None, :]
    full_out = full_out[:, :width]

    rows = rows_spec(width)
    narrow = ((row_count, width), LOW, rows)
    wide = ((row_count, width), WIDE, rows)
    big = ((row_count, hidden), LOW, rows_spec(hidden))
    state_spec = pl.BlockSpec((1, HD, width), lambda i: (i // per_seq, 0, 0))
    state = ((seq_count, HD, width), WIDE, state_spec)
    square = 2 * row_count * width * width

    normed_low, pre_key, keys, values, totals = call(
        lambda *refs: key_value_kernel(per_seq, *refs),
        steps,
        [(tok, rows), (full_key, whole_spec(full_key)), (full_value, whole_spec(full_value))],
        [narrow, narrow, narrow, narrow, state],
        flops=2 * square,
    )
    incoming = shift_sum(totals, "fsdp", False)
    pre_query, queries, pre_gate = call(
        query_gate_kernel,
        steps,
        [(normed_low, rows), (full_query, whole_spec(full_query)), (full_gate, whole_spec(full_gate))],
        [narrow, narrow, narrow],
        flops=2 * square,
    )
    prefix_spec = pl.BlockSpec((1, HD, width), lambda i: (i, 0, 0))
    attended, mixed, residual, prefix = call(
        lambda *refs: attend_kernel(per_seq, *refs),
        steps,
        [(queries, rows), (keys, rows), (values, rows), (pre_gate, rows), (tok, rows),
         (incoming, state_spec), (gain, whole_spec(gain)), (full_out, whole_spec(full_out))],
        [narrow, narrow, wide, ((steps, HD, width), LOW, prefix_spec)],
        scratch=[pltpu.VMEM((HD, width), WIDE)],
        flops=3 * square,
    )
    (
        layer_out, normed_two, glu, grad_up_one, grad_up_two, upstream_low, grad_residual,
        gated, grad_attended, grad_totals, grad_gain_term,
    ) = call(
        lambda *refs: feed_kernel(per_seq, False, *refs),
        steps,
        [(lengths, pl.BlockSpec(memory_space=pltpu.SMEM)), (residual, rows), (cot, rows),
         (full_one, whole_spec(full_one)), (full_two, whole_spec(full_two)),
         (full_three, whole_spec(full_three)), (full_out, whole_spec(full_out)),
         (gain, whole_spec(gain)), (pre_gate, rows), (attended, rows), (queries, rows)],
        [narrow, narrow, big, big, big, narrow, wide,
         ((row_count, 2 * width), LOW, rows_spec(2 * width)), narrow, state,
         ((1, width), WIDE, pl.BlockSpec((1, width), lambda i: (0, 0)))],
        flops=12 * row_count * width * hidden + square,
    )
    grad_residual_low, grad_pre_gate = gated[:, :width], gated[:, width:]
    outgoing = shift_sum(grad_totals, "fsdp", True)
    grad_one = scatter_rows(dot_tn(normed_two, grad_up_one), orders[1])
    grad_two = scatter_rows(dot_tn(normed_two, grad_up_two), orders[2])
    grad_three = scatter_rows(dot_tn(glu, upstream_low), orders[0])
    gain_term = jnp.broadcast_to(grad_gain_term.reshape(width, 1), (width, 128))
    grad_out = scatter_rows(
        jnp.concatenate([dot_tn(mixed, grad_residual_low), gain_term], axis=1), orders[1]
    )
    grad_gain = grad_out[:, width]
    grad_out = grad_out[:, :width]

    def back(i):
        return (i // per_seq) * per_seq + per_seq - 1 - i % per_seq

    back_rows = rows_spec(width, order=back)
    back_narrow = ((row_count, width), LOW, back_rows)
    grad_pre_query, grad_pre_key, grad_pre_value = call(
        lambda *refs: attend_back_kernel(per_seq, *refs),
        steps,
        [(queries, back_rows), (keys, back_rows), (values, back_rows),
         (grad_attended, back_rows), (pre_query, back_rows), (pre_key, back_rows),
         (prefix, pl.BlockSpec((1, HD, width), lambda i: (back(i), 0, 0))),
         (outgoing, state_spec)],
        [back_narrow, back_narrow, back_narrow],
        scratch=[pltpu.VMEM((HD, width), WIDE)],
        flops=6 * square,
    )
    grad_query = scatter_rows(dot_tn(normed_low, grad_pre_query), orders[0])
    grad_key = scatter_rows(dot_tn(normed_low, grad_pre_key), orders[1])
    grad_value = scatter_rows(dot_tn(normed_low, grad_pre_value), orders[2])
    grad_gate = scatter_rows(dot_tn(normed_low, grad_pre_gate), orders[0])
    (input_grad,) = call(
        input_kernel,
        steps,
        [(grad_pre_query, rows), (grad_pre_key, rows), (grad_pre_value, rows),
         (grad_pre_gate, rows), (full_query, whole_spec(full_query)),
         (full_key, whole_spec(full_key)), (full_value, whole_spec(full_value)),
         (full_gate, whole_spec(full_gate)), (tok, rows), (grad_residual, rows)],
        [wide],
        flops=4 * square,
    )
    return (
        layer_out.reshape(tokens.shape),
        input_grad.reshape(tokens.shape),
        grad_query,
        grad_key,
        grad_value,
        grad_gate,
        grad_gain,
        grad_out,
        grad_one,
        grad_two,
        grad_three,
    )


def feed_step_kernel(
    steps, per_seq, lengths, residual, cotangent, up_one, up_two, all_one, all_two, all_three,
    all_attn, gain, pre_gate, attended, queries,
    layer_out, grad_one, grad_two, upstream_low, grad_residual, gated, grad_attended,
    totals, grad_gain, product, last_back, last_residual, last_upstream,
    w_one, w_two, w_three, w_out, local,
):
    step = pl.program_id(0)
    row_count, width = residual.shape

    hidden = w_one.shape[1]
    loads = {}
    for n, part in enumerate((slice(0, 768), slice(768, 1792), slice(1792, hidden))):
        loads[part.start] = pltpu.make_async_copy(
            all_three.at[part], w_three.at[part], local.at[n]
        )
    later = [
        pltpu.make_async_copy(all_one, w_one, local.at[3]),
        pltpu.make_async_copy(all_two, w_two, local.at[4]),
        pltpu.make_async_copy(all_attn.at[:, 4 * width : 5 * width], w_out, local.at[5]),
    ]

    def norm_part(rows):
        res = last_residual[rows, :]
        grad = last_upstream[rows, :].astype(WIDE)
        grad += norm_back(res, rms_scale(res), last_back[rows, :])
        grad_residual[rows, :] = grad
        gated[rows, :width] = grad.astype(LOW)

    def out_part():
        last_back[...] = dot_nt(gated[:, :width], w_out[...])
        grad_gain[...] = jnp.where(step == 1, 0.0, grad_gain[...])

    def gate_part(rows):
        grad = last_back[rows, :]
        gate = jax.nn.sigmoid(pre_gate[rows, :].astype(WIDE))
        att = attended[rows, :].astype(WIDE)
        scale = rms_scale(att)
        hat = att * scale
        grad = grad * gate
        grad_gain[...] += jnp.sum(grad * hat, axis=0, keepdims=True)
        grad = grad * gain[...]
        gated[rows, width:] = (grad * hat * (1.0 - gate)).astype(LOW)
        grad_attended[rows, :] = norm_back(att, scale, grad).astype(LOW)

    def state_part():
        fresh = (step - 1) % per_seq == 0
        same = head_square()
        for g in groups(width):
            term = pack_state(dot_tn(queries[:, g], grad_attended[:, g]), same)
            totals[0, :, g] = jnp.where(fresh, 0.0, totals[0, :, g]) + term

    def cut(count, n):
        size = row_count // count
        return slice(n * size, (n + 1) * size)

    tail = [functools.partial(norm_part, cut(2, n)) for n in range(2)] + [out_part]
    tail += [functools.partial(gate_part, cut(8, n)) for n in range(8)] + [state_part]

    def begin(todo, loading=False):
        spot = lax.broadcasted_iota(jnp.int32, (row_count, 1), 0) + (step % per_seq) * row_count
        limit = lengths[step // per_seq] - lax.axis_index("fsdp") * per_seq * row_count
        valid = (spot < limit).astype(WIDE)
        up_low = (cotangent[...].astype(WIDE) * valid).astype(LOW)
        upstream_low[...] = up_low
        todo = list(todo)
        for c in groups(hidden):
            if loading and c.start in loads:
                loads[c.start].wait()
            back = dot_nt(up_low, w_three[c, :])
            if todo:
                todo.pop(0)()
            one, two = up_one[:, c].astype(WIDE), up_two[:, c].astype(WIDE)
            product[:, c] = (one * two).astype(LOW)
            grad_one[:, c] = (back * two).astype(LOW)
            grad_two[:, c] = (back * one).astype(LOW)
        for part in todo:
            part()
        res = residual[...]
        layer_out[...] = (valid * (res + dot_nn(product[...], w_three[...]))).astype(LOW)
        if loading:
            for copy in later:
                copy.wait()
        back = dot_nt(grad_one[...], w_one[...]) + dot_nt(grad_two[...], w_two[...])
        last_back[...] = back
        last_residual[...] = res
        last_upstream[...] = up_low

    @pl.when(step == 0)
    def _():
        for copy in list(loads.values()) + later:
            copy.start()
        begin([], loading=True)

    @pl.when((step > 0) & (step < steps))
    def _():
        begin(tail)

    @pl.when(step == steps)
    def _():
        for part in tail:
            part()


def feed(
    seq_count, lengths, residual, cot, up_one, up_two, full_one, full_two, full_three, full_attn,
    gain, pre_gate, attended, queries,
):
    row_count, width = residual.shape
    hidden = full_one.shape[1]
    steps = row_count // BLOCK
    per_seq = steps // seq_count

    def now(i):
        return jnp.minimum(i, steps - 1)

    def last(i):
        return jnp.maximum(i - 1, 0)

    rows = rows_spec(width, order=now)
    done = rows_spec(width, order=last)
    narrow = ((row_count, width), LOW, rows)
    big = ((row_count, hidden), LOW, rows_spec(hidden, order=now))

    state_spec = pl.BlockSpec((1, HD, width), lambda i: (last(i) // per_seq, 0, 0))
    hbm = pl.BlockSpec(memory_space=pl.ANY)
    return call(
        lambda *refs: feed_step_kernel(steps, per_seq, *refs),
        steps + 1,
        [(lengths, pl.BlockSpec(memory_space=pltpu.SMEM)), (residual, rows), (cot, rows),
         (up_one, big[2]), (up_two, big[2]),
         (full_one, hbm), (full_two, hbm), (full_three, hbm), (full_attn, hbm),
         (gain, whole_spec(gain)), (pre_gate, done), (attended, done), (queries, done)],
        [narrow, big, big, narrow,
         ((row_count, width), WIDE, done),
         ((row_count, 2 * width), LOW, rows_spec(2 * width, order=last)),
         ((row_count, width), LOW, done),
         ((seq_count, HD, width), WIDE, state_spec),
         ((1, width), WIDE, pl.BlockSpec((1, width), lambda i: (0, 0)))],
        scratch=[pltpu.VMEM((BLOCK, hidden), LOW), pltpu.VMEM((BLOCK, width), WIDE),
                 pltpu.VMEM((BLOCK, width), WIDE), pltpu.VMEM((BLOCK, width), LOW),
                 pltpu.VMEM((width, hidden), LOW), pltpu.VMEM((width, hidden), LOW),
                 pltpu.VMEM((hidden, width), LOW), pltpu.VMEM((width, width), LOW),
                 pltpu.SemaphoreType.DMA((6,))],
        flops=8 * row_count * width * hidden + 2 * row_count * width * width,
        limit=60,
    )


def fused_shards(
    tokens,
    lengths,
    w_query,
    w_key,
    w_value,
    w_gate,
    out_gain,
    w_out,
    w_one,
    w_two,
    w_three,
    cotangent,
):
    seq_count, local_length, width = tokens.shape
    row_count = seq_count * local_length
    tok = tokens.reshape(row_count, width)
    cot = cotangent.reshape(row_count, width)
    (
        normed_low, pre_key, keys, values, pre_query, queries, pre_gate, attended, mixed,
        residual, normed_two, up_one, up_two, glu, prefix, gain, full_attn, full_one, full_two,
        full_three,
    ) = forward(
        tok, seq_count, (w_key, w_value, w_query, w_gate, w_out), out_gain[None, :], w_one, w_two, w_three
    )

    (
        layer_out, grad_up_one, grad_up_two, upstream_low, grad_residual, gated,
        grad_attended, grad_totals, grad_gain_term,
    ) = feed(
        seq_count, lengths, residual, cot, up_one, up_two, full_one, full_two, full_three,
        full_attn, gain, pre_gate, attended, queries,
    )
    grad_one, grad_two, grad_three, grad_three_pre = feed_back(
        seq_count, normed_two, grad_up_one, grad_up_two, glu, upstream_low, queries, keys, values,
        grad_attended, pre_query, pre_key, prefix, grad_totals,
    )
    grads, input_grad = attend_weights(
        normed_low, mixed, gated, grad_three_pre, grad_gain_term, full_attn, tok, grad_residual
    )
    grad_out, grad_gain = grads[:, :width], grads[:, width]
    grad_gate, grad_query, grad_key, grad_value = (
        grads[:, 128 + n * width : 128 + (n + 1) * width] for n in range(1, 5)
    )
    return (
        layer_out.reshape(tokens.shape),
        input_grad.astype(WIDE).reshape(tokens.shape),
        grad_query,
        grad_key,
        grad_value,
        grad_gate,
        grad_gain,
        grad_out,
        grad_one,
        grad_two,
        grad_three,
    )


def shards(*arrays):
    tokens, w_query, w_three = arrays[0], arrays[2], arrays[10]
    sizes = (lax.axis_size("dp"), lax.axis_size("fsdp"))
    fits = w_query.shape[0] % 16 == 0 and w_three.shape[0] % 8 == 0 and tokens.shape[1] >= 4 * BLOCK
    if sizes == (16, 2) and fits:
        return fused_shards(*arrays)
    return plain_shards(*arrays)


def solution(mesh):
    in_specs = (
        P("dp", "fsdp", None),
        P("dp"),
        P(("dp", "fsdp"), None),
        P(("dp", "fsdp"), None),
        P(("dp", "fsdp"), None),
        P(("dp", "fsdp"), None),
        P(("dp", "fsdp")),
        P(("dp", "fsdp"), None),
        P(("dp", "fsdp"), None),
        P(("dp", "fsdp"), None),
        P(("dp", "fsdp"), None),
        P("dp", "fsdp", None),
    )
    out_specs = (
        P("dp", "fsdp", None),
        P("dp", "fsdp", None),
        P(("dp", "fsdp"), None),
        P(("dp", "fsdp"), None),
        P(("dp", "fsdp"), None),
        P(("dp", "fsdp"), None),
        P(("dp", "fsdp")),
        P(("dp", "fsdp"), None),
        P(("dp", "fsdp"), None),
        P(("dp", "fsdp"), None),
        P(("dp", "fsdp"), None),
    )
    return jax.shard_map(shards, mesh=mesh, in_specs=in_specs, out_specs=out_specs, check_vma=False)
```

```python
import functools

import jax
import jax.numpy as jnp
from jax import lax
from jax.experimental import pallas as pl
from jax.experimental.pallas import tpu as pltpu
from jax.sharding import PartitionSpec as P

HD = 64
H = 16
BLOCK = 256


GROUP = 256
HEADS = GROUP // HD
LOW = jnp.bfloat16
WIDE = jnp.float32

norm_epsilon = 1e-06


def bit_steps():
    steps = []
    for axis in ("dp", "fsdp"):
        size = lax.axis_size(axis)
        bit = 0
        while (1 << bit) < size:
            steps.append((axis, bit, [(i, i ^ (1 << bit)) for i in range(size)]))
            bit += 1
    return steps


def stream_orders():
    steps = bit_steps()
    dp = [s for s in steps if s[0] == "dp"]
    fs = [s for s in steps if s[0] == "fsdp"]
    core, rest = dp[0], fs[:1] + dp[1:3]
    tail = dp[3:] + fs[1:]
    return [[core] + rest[k:] + rest[:k] + tail for k in range(3)]


def own_bit(step):
    axis, bit, _ = step
    return lax.rem(lax.div(lax.axis_index(axis), 1 << bit), 2)


def bit_dims():
    steps = bit_steps()
    dp = sorted([s for s in steps if s[0] == "dp"], key=lambda s: -s[1])
    fs = sorted([s for s in steps if s[0] == "fsdp"], key=lambda s: -s[1])
    return [(s[0], s[1]) for s in dp + fs]


def gather_rows(shard, order):
    dims = bit_dims()
    held = []
    data = shard
    for step in reversed(order):
        axis, bit, perm = step
        other = lax.ppermute(data, axis, perm)
        mine = own_bit(step) == 0
        place = sum(1 for d in held if dims.index(d) < dims.index((axis, bit)))
        held.append((axis, bit))
        data = jnp.stack(
            [jnp.where(mine, data, other), jnp.where(mine, other, data)], axis=place
        )
    return data.reshape((-1,) + shard.shape[1:])


def scatter_rows(full, order):
    dims = bit_dims()
    rows = full.shape[0] >> len(dims)
    data = full.astype(jnp.bfloat16).reshape((2,) * len(dims) + (rows,) + full.shape[1:])
    left = list(dims)
    for at, step in enumerate(order):
        axis, bit, perm = step
        place = left.index((axis, bit))
        left.pop(place)
        own = own_bit(step)
        send = lax.dynamic_index_in_dim(data, 1 - own, place, keepdims=False)
        keep = lax.dynamic_index_in_dim(data, own, place, keepdims=False)
        come = lax.ppermute(send, axis, perm)
        data = keep.astype(jnp.float32) + come.astype(jnp.float32)
        if at < len(order) - 1:
            data = data.astype(jnp.bfloat16)
    return data


def shift_sum(x, axis, reverse):
    size = lax.axis_size(axis)
    total = jnp.zeros_like(x)
    low = x.astype(jnp.bfloat16)
    for s in range(1, size):
        pairs = [(i + s, i) if reverse else (i, i + s) for i in range(size - s)]
        total = total + lax.ppermute(low, axis, pairs).astype(x.dtype)
    return total


def dot_nn(a, b):
    return jnp.dot(a, b, preferred_element_type=WIDE)


def dot_nt(a, b):
    return lax.dot_general(a, b, (((1,), (1,)), ((), ())), preferred_element_type=WIDE)


def dot_tn(a, b):
    return lax.dot_general(a, b, (((0,), (0,)), ((), ())), preferred_element_type=WIDE)


def rms_scale(values):
    return lax.rsqrt(jnp.mean(values * values, axis=-1, keepdims=True) + norm_epsilon)


def norm_back(values, scale, upstream):
    inner_mean = jnp.mean(upstream * values, axis=-1, keepdims=True)
    return scale * (upstream - values * (scale * scale) * inner_mean)


def silu_slope(pre_rows):
    logistic = jax.nn.sigmoid(pre_rows)
    return logistic * (1.0 + pre_rows * (1.0 - logistic))


def head_square():
    row = lax.broadcasted_iota(jnp.int32, (GROUP, GROUP), 0) // HD
    col = lax.broadcasted_iota(jnp.int32, (GROUP, GROUP), 1) // HD
    return (row == col).astype(WIDE)


def head_rows():
    lane = lax.broadcasted_iota(jnp.int32, (1, GROUP), 1) // HD
    return [(lane == h).astype(WIDE).astype(LOW) for h in range(HEADS)]


def split_heads(rows, marks):
    return jnp.concatenate([rows * mark for mark in marks], axis=0)


def pack_state(square, same):
    return jnp.sum((square * same).reshape(HEADS, HD, GROUP), axis=0)


def open_state(packed, same):
    return (jnp.concatenate([packed] * HEADS, axis=0) * same).astype(LOW)


def causal_masks():
    i = lax.broadcasted_iota(jnp.int32, (BLOCK, HEADS * BLOCK), 0)
    j = lax.broadcasted_iota(jnp.int32, (BLOCK, HEADS * BLOCK), 1) % BLOCK
    return (i >= j).astype(WIDE), (j >= i).astype(WIDE)


def groups(width):
    return [slice(g * GROUP, (g + 1) * GROUP) for g in range(width // GROUP)]


def key_value_kernel(per_seq, tok, w_key, w_value, normed, pre_key, keys, values, totals):
    x = tok[...].astype(WIDE)
    rows = (x * rms_scale(x)).astype(LOW)
    normed[...] = rows
    pre = dot_nn(rows, w_key[...])
    pre_key[...] = pre.astype(LOW)
    k = jax.nn.silu(pre).astype(LOW)
    keys[...] = k
    v = dot_nn(rows, w_value[...]).astype(LOW)
    values[...] = v

    @pl.when(pl.program_id(0) % per_seq == 0)
    def _():
        totals[...] = jnp.zeros_like(totals)

    same = head_square()
    for g in groups(k.shape[1]):
        totals[0, :, g] += pack_state(dot_tn(k[:, g], v[:, g]), same)


def query_gate_kernel(normed, w_query, w_gate, pre_query, queries, pre_gate):
    rows = normed[...]
    pre = dot_nn(rows, w_query[...])
    pre_query[...] = pre.astype(LOW)
    queries[...] = jax.nn.silu(pre).astype(LOW)
    pre_gate[...] = dot_nn(rows, w_gate[...]).astype(LOW)


def attend_kernel(
    per_seq, queries, keys, values, pre_gate, tok, incoming, gain, w_out,
    attended, mixed, residual, prefix, carry,
):
    @pl.when(pl.program_id(0) % per_seq == 0)
    def _():
        carry[...] = incoming[0]

    same, marks = head_square(), head_rows()
    causal, _ = causal_masks()
    prefix[0] = carry[...].astype(LOW)
    for g in groups(queries.shape[1]):
        q, k, v = queries[:, g], keys[:, g], values[:, g]
        scores = (dot_nt(q, split_heads(k, marks)) * causal).astype(LOW)
        out = dot_nn(scores, split_heads(v, marks))
        out += dot_nn(q, open_state(carry[:, g], same))
        attended[:, g] = out.astype(LOW)
        carry[:, g] += pack_state(dot_tn(k, v), same)
    rows = attended[...].astype(WIDE)
    gate = jax.nn.sigmoid(pre_gate[...].astype(WIDE))
    rows = (rows * rms_scale(rows) * gain[...] * gate).astype(LOW)
    mixed[...] = rows
    residual[...] = tok[...].astype(WIDE) + dot_nn(rows, w_out[...])


def feed_kernel(
    per_seq, turned, lengths, residual, cotangent, w_one, w_two, w_three, w_out, gain, pre_gate,
    attended, queries,
    layer_out, normed, glu, grad_one, grad_two, upstream_low, grad_residual, gated,
    grad_attended, totals, grad_gain, held=None,
):
    step = pl.program_id(0)
    row_count = residual.shape[0]
    spot = lax.broadcasted_iota(jnp.int32, (row_count, 1), 0) + (step % per_seq) * row_count
    limit = lengths[step // per_seq] - lax.axis_index("fsdp") * per_seq * row_count
    valid = (spot < limit).astype(WIDE)
    res = residual[...]
    scale = rms_scale(res)
    rows = (res * scale).astype(LOW)
    normed[...] = rows.T if turned else rows
    upstream = cotangent[...].astype(WIDE) * valid
    up_low = upstream.astype(LOW)
    upstream_low[...] = up_low
    for c in groups(w_one.shape[1]):
        one = dot_nn(rows, w_one[:, c])
        two = dot_nn(rows, w_two[:, c])
        back = dot_nt(up_low, w_three[c, :])
        product = (one * two).astype(LOW)
        if turned:
            held[:, c] = product
            glu[c, :] = product.T
        else:
            glu[:, c] = product
        grad_one[:, c] = (back * two).astype(LOW)
        grad_two[:, c] = (back * one).astype(LOW)
    layer_out[...] = (valid * (res + dot_nn(held[...] if turned else glu[...], w_three[...]))).astype(LOW)
    back = dot_nt(grad_one[...], w_one[...]) + dot_nt(grad_two[...], w_two[...])
    grad = upstream + norm_back(res, scale, back)
    grad_residual[...] = grad
    grad = grad.astype(LOW)
    width = grad.shape[1]
    gated[:, :width] = grad
    grad = dot_nt(grad, w_out[...])
    gate = jax.nn.sigmoid(pre_gate[...].astype(WIDE))
    att = attended[...].astype(WIDE)
    scale = rms_scale(att)
    hat = att * scale
    grad = grad * gate

    @pl.when(step == 0)
    def _():
        grad_gain[...] = jnp.zeros_like(grad_gain)

    grad_gain[...] += jnp.sum(grad * hat, axis=0, keepdims=True)
    grad = grad * gain[...]
    gated[:, width:] = (grad * hat * (1.0 - gate)).astype(LOW)
    grad_att = norm_back(att, scale, grad).astype(LOW)
    grad_attended[...] = grad_att

    @pl.when(step % per_seq == 0)
    def _():
        totals[...] = jnp.zeros_like(totals)

    same = head_square()
    for g in groups(grad_att.shape[1]):
        totals[0, :, g] += pack_state(dot_tn(queries[:, g], grad_att[:, g]), same)


def attend_back_kernel(
    per_seq, queries, keys, values, grad_attended, pre_query, pre_key, prefix, incoming,
    grad_query, grad_key, grad_value, carry,
):
    @pl.when(pl.program_id(0) % per_seq == 0)
    def _():
        carry[...] = incoming[0]

    same, marks = head_square(), head_rows()
    causal, causal_t = causal_masks()
    for g in groups(queries.shape[1]):
        q, k, v, ga = queries[:, g], keys[:, g], values[:, g], grad_attended[:, g]
        qs, ks, vs, gs = (split_heads(rows, marks) for rows in (q, k, v, ga))
        state = open_state(prefix[0, :, g].astype(WIDE), same)
        grad_state = open_state(carry[:, g], same)
        grad_scores = (dot_nt(ga, vs) * causal).astype(LOW)
        gq = dot_nn(grad_scores, ks) + dot_nt(ga, state)
        grad_scores = (dot_nt(v, gs) * causal_t).astype(LOW)
        gk = dot_nn(grad_scores, qs) + dot_nt(v, grad_state)
        scores = (dot_nt(k, qs) * causal_t).astype(LOW)
        gv = dot_nn(scores, gs) + dot_nn(k, grad_state)
        grad_query[:, g] = (gq * silu_slope(pre_query[:, g].astype(WIDE))).astype(LOW)
        grad_key[:, g] = (gk * silu_slope(pre_key[:, g].astype(WIDE))).astype(LOW)
        grad_value[:, g] = gv.astype(LOW)
        carry[:, g] += pack_state(dot_tn(q, ga), same)


def input_kernel(
    grad_query, grad_key, grad_value, grad_gate, w_query, w_key, w_value, w_gate, tok,
    grad_residual, input_grad,
):
    grad = dot_nt(grad_query[...], w_query[...]) + dot_nt(grad_key[...], w_key[...])
    grad += dot_nt(grad_value[...], w_value[...]) + dot_nt(grad_gate[...], w_gate[...])
    x = tok[...].astype(WIDE)
    input_grad[...] = grad_residual[...] + norm_back(x, rms_scale(x), grad)


def rows_spec(width, block=BLOCK, order=lambda i: i):
    return pl.BlockSpec((block, width), lambda i: (order(i), 0))


def whole_spec(array):
    rank = array.ndim
    return pl.BlockSpec(array.shape, lambda i: (0,) * rank, pipeline_mode=pl.Buffered(1))


def call(kernel, steps, operands, results, scratch=(), flops=0, limit=56):
    moved = sum(a.size * a.dtype.itemsize for a, _ in operands)
    return pl.pallas_call(
        kernel,
        grid=(steps,),
        in_specs=[spec for _, spec in operands],
        out_specs=[spec for _, _, spec in results],
        out_shape=[jax.ShapeDtypeStruct(shape, dtype) for shape, dtype, _ in results],
        scratch_shapes=list(scratch),
        compiler_params=pltpu.CompilerParams(
            dimension_semantics=("arbitrary",), vmem_limit_bytes=limit << 20
        ),
        cost_estimate=pl.CostEstimate(flops=flops, bytes_accessed=moved, transcendentals=0),
    )(*[a for a, _ in operands])


def index_bits():
    bits = []
    for axis in ("dp", "fsdp"):
        count = lax.axis_size(axis).bit_length() - 1
        bits += [(axis, bit) for bit in reversed(range(count))]
    return bits


LINKS = {
    "1": (("dp", 3),),
    "0": (("dp", 2),),
    "z": (("dp", 3), ("dp", 2)),
    "y": (("dp", 1),),
    "x": (("fsdp", 0),),
}
CORE = ("dp", 0)
SIDE = ("fsdp", 0)


def bit_value(bit):
    axis, at = bit
    return lax.rem(lax.div(lax.axis_index(axis), 1 << at), 2)


def flips_of(name):
    group = LINKS[name]
    if len(group) == 1:
        return [group]
    return [group[:1], group[1:], group]


def flip_device(flips):
    place = {}
    for axis, at in flips:
        moved = place.get(axis, lax.axis_index(axis))
        place[axis] = moved + (1 - 2 * bit_value((axis, at))) * (1 << at)
    return place


def greet(bits, far=True):
    partners = [(bit,) for bit in bits] + ([LINKS["z"]] if far else [])
    barrier = pltpu.get_barrier_semaphore()
    for flips in partners:
        pl.semaphore_signal(
            barrier, inc=1, device_id=flip_device(flips), device_id_type=pl.DeviceIdType.MESH
        )
    pl.semaphore_wait(barrier, len(partners))


class Sems:
    def __init__(self, send, recv):
        self.send, self.recv, self.used = send, recv, 0

    def copy(self, src, dst, flips):
        at = self.used
        self.used += 1
        return pltpu.make_async_remote_copy(
            src_ref=src,
            dst_ref=dst,
            send_sem=self.send.at[at],
            recv_sem=self.recv.at[at],
            device_id=flip_device(flips),
            device_id_type=pl.DeviceIdType.MESH,
        )


class Gather:
    def __init__(self, buf, bits, order, sems, columns=slice(None)):
        self.stages, held = [], []

        def cube(flips=()):
            index = []
            for bit in bits:
                if bit in held:
                    index.append(slice(None))
                else:
                    index.append(1 - bit_value(bit) if bit in flips else bit_value(bit))
            return buf.at[tuple(index) + (slice(None), columns)]

        for n, name in enumerate(order):
            ref, flips = cube(), flips_of(name)
            self.stages.append([sems.copy(ref, ref, flip) for flip in flips])
            if n == len(order) - 1:
                self.near = sems.copy(ref, ref, (CORE,))
                far = [cube(flip) for flip in flips]
                self.stages.append([sems.copy(ref, ref, (CORE,)) for ref in far])
            held.extend(LINKS[name])

    def start(self, k):
        for copy in self.stages[k]:
            copy.start()
        if k == len(self.stages) - 2:
            self.near.start()

    def advance(self, k):
        if k:
            for copy in self.stages[k - 1]:
                copy.wait_recv()
        self.start(k)

    def finish(self):
        self.near.wait_recv()
        for copy in self.stages[-1]:
            copy.wait_recv()

    def drain(self):
        for copy in [c for stage in self.stages for c in stage] + [self.near]:
            copy.wait_send()


class Scatter:
    def __init__(
        self, sems, bits, order, acc, send, come, recvs, columns, send_columns, come_columns
    ):
        self.bits, self.order, self.acc, self.columns = bits, order, acc, columns
        self.come, self.recvs, self.come_columns = come, recvs, come_columns
        rows = (slice(None),)
        full = (slice(None),) * len(bits) + rows
        self.core = sems.copy(
            send.at[full + (send_columns,)], come.at[full + (come_columns,)], (CORE,)
        )
        self.copies, self.done = [], []
        for k, name in enumerate(order):
            (bit,) = LINKS[name]
            done = [LINKS[n][0] for n in order[:k]]
            index = tuple(
                1 - bit_value(b) if b == bit else bit_value(b) if b in done else slice(None)
                for b in bits
            )
            free = (slice(None),) * (len(bits) - k - 1)
            source = acc.at[index + rows + (columns,)]
            self.copies.append(sems.copy(source, recvs[k].at[free + rows + (columns,)], (bit,)))
            self.done.append(done)

    def add(self, done, source, columns):
        free = [b for b in self.bits if b not in done]

        def one(k):
            at = [(k // (1 << (len(free) - 1 - n))) % 2 for n in range(len(free))]
            mine = tuple(bit_value(b) if b in done else at[free.index(b)] for b in self.bits)
            here = mine + (slice(None), self.columns)
            self.acc[here] = self.acc[here] + source[tuple(at) + (slice(None), columns)]

        if len(free) <= 2:
            for k in range(1 << len(free)):
                one(k)
        else:
            lax.fori_loop(0, 1 << len(free), lambda k, c: (one(k), c)[1], 0)

    def launch(self):
        self.core.start()

    def advance(self, k):
        if k == 0:
            self.core.wait_recv()
            self.add([], self.come, self.come_columns)
        else:
            self.copies[k - 1].wait_recv()
            self.add(self.done[k - 1] + [LINKS[self.order[k - 1]][0]], self.recvs[k - 1], self.columns)
        self.copies[k].start()

    def result(self):
        self.copies[-1].wait_recv()
        own = tuple(bit_value(b) for b in self.bits)
        here = (slice(None), self.columns)
        return self.acc[own + here].astype(WIDE) + self.recvs[-1][here].astype(WIDE)

    def drain(self, core=True):
        if core:
            self.core.wait_send()
        for copy in self.copies:
            copy.wait_send()


def run_events(step, events):
    for at in sorted(events):

        @pl.when(step == at)
        def _():
            for action in events[at]:
                action()


def planned(table, pieces, low, high):
    events = {}
    for at, todo in table:
        if low <= at < high:
            events[at] = [functools.partial(pieces[name].advance, k) for name, k in todo]
    return events


FORWARD_PLAN = (
    (0, (
        ("a00", 0), ("a02", 0), ("f5", 0), ("f4", 0), ("a01", 0), ("a00", 1), ("f5", 1),
        ("a02", 1), ("a01", 1), ("a20", 0), ("a00", 2), ("a22", 0), ("a21", 0), ("a02", 2),
        ("a12", 0), ("a11", 0), ("a10", 0), ("a01", 2), ("a20", 1), ("a02", 3), ("a21", 1),
        ("a12", 1), ("a00", 3), ("a01", 3), ("a11", 1), ("a10", 1), ("a22", 1), ("a21", 2),
        ("a20", 2), ("a12", 2), ("a02", 4), ("f2", 0), ("f0", 0), ("a11", 2), ("a10", 2),
        ("a00", 4), ("a01", 4), ("a21", 3), ("a20", 3),
    )),
    (1, (("a10", 3), ("f1", 0),)),
    (2, (("a22", 2), ("a11", 3),)),
    (3, (("f3", 0),)),
    (4, (("a22", 3), ("a20", 4), ("f1", 1), ("a12", 3),)),
    (5, (("a21", 4), ("f0", 1), ("f2", 1), ("f3", 1),)),
    (7, (("a10", 4), ("f1", 2), ("a11", 4),)),
    (8, (("a12", 4), ("f4", 1), ("a22", 4), ("f0", 2),)),
    (10, (("f2", 2), ("f1", 3), ("f3", 2), ("f5", 2),)),
    (11, (("f0", 3),)),
    (13, (("f4", 2), ("f2", 3), ("f3", 3),)),
    (14, (("f1", 4),)),
    (16, (("f0", 4), ("f5", 3),)),
    (18, (("f4", 3),)),
    (21, (("f2", 4),)),
    (22, (("f3", 4),)),
    (29, (("f5", 4),)),
    (30, (("f4", 4),)),
)
FEED_BACK_PLAN = (
    (10, (("three0", 0),)),
    (11, (("three1", 0),)),
    (12, (("one0", 0),)),
    (13, (("two0", 0),)),
    (15, (("two1", 0), ("one1", 0),)),
    (16, (("three0", 1),)),
    (17, (("two0", 1), ("three1", 1),)),
    (18, (("two2", 0),)),
    (19, (("one2", 0), ("one0", 1), ("one1", 1), ("three0", 2),)),
    (21, (("one3", 0),)),
    (22, (("one0", 2),)),
    (23, (("two2", 1), ("two0", 2), ("one1", 2), ("two3", 0),)),
    (24, (("three1", 2),)),
    (25, (("one2", 1), ("two0", 3),)),
    (26, (("one3", 1),)),
    (27, (("two1", 1), ("one0", 3), ("two2", 2),)),
    (28, (("one1", 3), ("two3", 1),)),
    (29, (("one2", 2), ("one3", 2),)),
    (30, (("two2", 3), ("three0", 3),)),
    (31, (("two1", 2), ("two3", 2), ("one2", 3),)),
    (32, (("one3", 3), ("three1", 3),)),
    (33, (("two1", 3),)),
    (34, (("two3", 3),)),
)
ATTEND_BACK_PLAN = (
    (4, (("p0", 0),)),
    (6, (("p1", 0),)),
    (7, (("p2", 0), ("p3", 0),)),
    (8, (("p4", 0),)),
    (9, (("p0", 1),)),
    (10, (("p5", 0), ("p3", 1), ("p4", 1), ("p1", 1), ("p6", 0),)),
    (11, (("p2", 1), ("p0", 2),)),
    (12, (("p4", 2), ("p3", 2), ("p1", 2),)),
    (13, (("p5", 1), ("p6", 1), ("p2", 2), ("p3", 3),)),
    (14, (("p0", 3), ("p1", 3),)),
    (15, (("p6", 2), ("p4", 3), ("p5", 2), ("p2", 3),)),
    (16, (("p6", 3),)),
    (17, (("p5", 3),)),
)


HALF = BLOCK // 2


def causal_pair(a, firsts, seconds, later):
    row = lax.broadcasted_iota(jnp.int32, (HALF, HEADS * HALF), 0)
    col = lax.broadcasted_iota(jnp.int32, (HALF, HEADS * HALF), 1) % HALF
    if later:
        mask = (row >= col).astype(WIDE)
        full, part = dot_nt(a, firsts), dot_nt(a[HALF:], seconds)
        full = [(full[:HALF] * mask).astype(LOW), full[HALF:].astype(LOW)]
    else:
        mask = (col >= row).astype(WIDE)
        full, part = dot_nt(a, seconds), dot_nt(a[:HALF], firsts)
        full = [full[:HALF].astype(LOW), (full[HALF:] * mask).astype(LOW)]
    return jnp.concatenate(full, axis=0), (part * mask).astype(LOW)


def causal_apply(scores, firsts, seconds, later, carried):
    full, part = scores
    if later:
        total = dot_nn(full, firsts) + carried
        return jnp.concatenate([total[:HALF], total[HALF:] + dot_nn(part, seconds)], axis=0)
    total = dot_nn(full, seconds) + carried
    return jnp.concatenate([total[:HALF] + dot_nn(part, firsts), total[HALF:]], axis=0)


def attend_back_step(
    same, queries, keys, values, grad_attended, pre_query, pre_key, prefix, grads, carry, middle,
):
    marks = head_rows()
    width = queries.shape[1]
    for g in groups(width):
        if g.start == width // 2:
            middle()
        q, k, v, ga = queries[:, g], keys[:, g], values[:, g], grad_attended[:, g]
        qs, ks, vs, gs = (
            (split_heads(rows[:HALF], marks), split_heads(rows[HALF:], marks))
            for rows in (q, k, v, ga)
        )
        state = open_state(prefix[0, :, g].astype(WIDE), same)
        grad_state = open_state(carry[:, g], same)
        gq = causal_apply(causal_pair(ga, *vs, True), *ks, True, dot_nt(ga, state))
        gk = causal_apply(causal_pair(v, *gs, False), *qs, False, dot_nt(v, grad_state))
        gv = causal_apply(causal_pair(k, *qs, False), *gs, False, dot_nn(k, grad_state))
        gq = gq * silu_slope(pre_query[:, g].astype(WIDE))
        gk = gk * silu_slope(pre_key[:, g].astype(WIDE))
        for n, grad in enumerate((gq, gk, gv)):
            grads[:, n * width + g.start : n * width + g.stop] = grad.astype(LOW)
        carry[:, g] += pack_state(dot_tn(q, ga), same)


def clip(value, low, high):
    return jnp.minimum(jnp.maximum(value, low), high)


CHUNK = 256
PAIRS = (2, 3, 3, 3)
PAIR_ORDERS = (("xy01", "xy01"), ("xy01", "0xy1"), ("xy01", "xy01"), ("yx01", "xy01"))
THREE_ORDERS = ("0y1", "y01")
THREE_AFTER = 0


def feed_back_blocks():
    pairs, three, at = [], None, 0
    for n, count in enumerate(PAIRS):
        if n == THREE_AFTER:
            three = (at, 8)
            at += 8
        pairs.append((at, count))
        at += count
    return pairs, three, at


class ThreeScatter(Scatter):
    def last_swap(self, sems, out, give, take):
        self.out, self.give, self.take = out, give, take
        cols = self.columns
        self.swap = sems.copy(give.at[:, cols], take.at[:, cols], (SIDE,))

    def advance(self, k):
        if k < len(self.order):
            super().advance(k)
            return
        cols = self.columns
        total = self.result()
        deep = total.shape[0] // 2
        low, high = total[:deep], total[deep:]
        upper = bit_value(SIDE).astype(WIDE)
        self.out[:, cols] = low * (1 - upper) + high * upper
        self.give[:, cols] = low * upper + high * (1 - upper)
        self.swap.start()

    def finish(self):
        self.swap.wait_recv()
        self.out[:, self.columns] += self.take[:, self.columns]
        self.swap.wait_send()


def feed_back_kernel(
    per_seq, bits,
    normed_hbm, grad_one, grad_two, glu, upstream_hbm,
    queries, keys, values, grad_attended, pre_query, pre_key, prefix, totals,
    out_one, out_two, out_three, grads,
    normed, upstream, acc, come1, come2, come3, come4, send, come,
    acc3, come31, come32, come33, send3, take3, last_send, last_come,
    state_out, state_in, carry, part, part3, send_sems, recv_sems, local,
):
    step = pl.program_id(0)
    pairs, three_block, base = feed_back_blocks()
    links = [bit for bit in bits if bit != CORE]
    mine, side = bit_value(CORE), bit_value(SIDE)
    other = 1 - mine
    sems = Sems(send_sems, recv_sems)
    hidden, width = out_one.shape[1], out_three.shape[1]
    recvs = (come1, come2, come3, come4)
    pieces, ends, first = {}, [], 0
    for n, count in enumerate(PAIRS):
        for w, (name, out) in enumerate((("one", out_one), ("two", out_two))):
            begin = w * hidden + first * CHUNK
            span = count * CHUNK
            pieces[f"{name}{n}"] = Scatter(
                sems, links, PAIR_ORDERS[n][w], acc, send.at[n % 2, w], come, recvs,
                slice(begin, begin + span), slice(0, span), slice(begin, begin + span),
            )
            ends.append((pieces[f"{name}{n}"], out, first * CHUNK))
        first += count
    half = width // 2
    threes = []
    for n in range(2):
        cols = slice(n * half, (n + 1) * half)
        piece = ThreeScatter(
            sems, links[:-1], THREE_ORDERS[n], acc3, send3, take3, (come31, come32, come33),
            cols, cols, cols,
        )
        piece.last_swap(sems, out_three, last_send, last_come)
        pieces[f"three{n}"] = piece
        threes.append(piece)
    swap_state = sems.copy(state_out, state_in, (SIDE,))
    load = [
        pltpu.make_async_copy(normed_hbm, normed, local.at[0]),
        pltpu.make_async_copy(upstream_hbm, upstream, local.at[1]),
    ]

    @pl.when(step == 0)
    def _():
        for copy in load:
            copy.start()
        greet(bits, far=False)
        state_out[...] = totals[...].astype(LOW)
        swap_state.start()

    for first_use, copy in ((pairs[0][0], load[0]), (three_block[0], load[1])):

        @pl.when(step == first_use)
        def _():
            copy.wait()

    for n in range(2, len(PAIRS)):

        @pl.when(step == pairs[n][0])
        def _():
            pieces[f"one{n - 2}"].core.wait_send()
            pieces[f"two{n - 2}"].core.wait_send()

    later = planned(FEED_BACK_PLAN, pieces, base, base + 16)
    at_start = {base + (at - base) // 2: todo for at, todo in later.items() if (at - base) % 2 == 0}
    at_middle = {base + (at - base) // 2: todo for at, todo in later.items() if (at - base) % 2}

    @pl.when(step < base)
    def _():
        run_events(step, planned(FEED_BACK_PLAN, pieces, 0, base))

    @pl.when(step >= base)
    def _():
        run_events(step, at_start)

    lead = acc.shape[:-1]
    fill = (slice(None),) * len(lead)

    def weight_chunk(w, rhs, chunk, group, first):
        part[...] = dot_nn(normed[...], rhs[...]).astype(LOW).reshape(part.shape)
        at = pl.ds(pl.multiple_of(chunk * CHUNK, CHUNK), CHUNK)
        send[(group % 2, w) + fill + (at,)] = part[:, other].reshape(lead + (CHUNK,))
        at = pl.ds(pl.multiple_of(w * hidden + (first + chunk) * CHUNK, CHUNK), CHUNK)
        acc[fill + (at,)] = part[:, mine].reshape(lead + (CHUNK,))

    first = 0
    for n, (begin, count) in enumerate(pairs):

        @pl.when((step >= begin) & (step < begin + count))
        def _():
            weight_chunk(0, grad_one, step - begin, n, first)
            weight_chunk(1, grad_two, step - begin, n, first)

        @pl.when(step == begin + count - 1)
        def _():
            pieces[f"one{n}"].launch()
            pieces[f"two{n}"].launch()

        first += count

    begin, count = three_block

    @pl.when((step >= begin) & (step < begin + count))
    def _():
        k = step - begin
        at = tuple((k // (1 << (2 - d))) % 2 for d in range(3))
        part3[...] = dot_nn(glu[...], upstream[...]).astype(LOW).reshape(part3.shape)
        send3[at] = part3[other]
        acc3[at] = part3[mine]

    @pl.when(step == begin + count - 1)
    def _():
        for piece in threes:
            piece.launch()

    @pl.when(step >= base)
    def _():
        at = step - base

        @pl.when(at == 0)
        def _():
            swap_state.wait_recv()

        @pl.when(at % per_seq == 0)
        def _():
            carry[...] = state_in[at // per_seq].astype(WIDE) * (1 - side).astype(WIDE)

        attend_back_step(
            head_square(), queries, keys, values, grad_attended, pre_query, pre_key, prefix,
            grads, carry, lambda: run_events(step, at_middle),
        )

    @pl.when(step == pl.num_programs(0) - 1)
    def _():
        for actions in planned(FEED_BACK_PLAN, pieces, base + 16, 1000).values():
            for action in actions:
                action()
        for piece, out, begin in ends:
            span = piece.columns.stop - piece.columns.start
            out[:, begin : begin + span] = piece.result()
        for n in range(len(PAIRS)):
            for name in ("one", "two"):
                pieces[f"{name}{n}"].drain(core=n + 2 >= len(PAIRS))
        for piece in threes:
            piece.finish()
            piece.drain()
        swap_state.wait_send()


def feed_back(
    seq_count, normed, grad_one, grad_two, glu, upstream, queries, keys, values, grad_attended,
    pre_query, pre_key, prefix, totals,
):
    row_count, width = queries.shape
    hidden = grad_one.shape[1]
    steps = row_count // BLOCK
    per_seq = steps // seq_count
    bits = index_bits()
    pairs, three, base = feed_back_blocks()
    deep = hidden // 8
    slab = width // 32

    def pair_at(i):
        done = sum(clip(i - begin, 0, count) for begin, count in pairs)
        return jnp.minimum(done, sum(PAIRS) - 1)

    def back(i):
        at = clip(i - base, 0, steps - 1)
        return (at // per_seq) * per_seq + per_seq - 1 - at % per_seq

    rows = pl.BlockSpec((BLOCK, width), lambda i: (back(i), 0))
    pair = pl.BlockSpec((row_count, CHUNK), lambda i: (0, pair_at(i)))
    vmem = pl.BlockSpec(memory_space=pltpu.VMEM)
    hbm = pl.BlockSpec(memory_space=pl.ANY)
    low = functools.partial(pltpu.VMEM, dtype=LOW)
    span = max(PAIRS) * CHUNK
    copies = 10 * len(PAIRS) + 2 * 5 + 1
    return pl.pallas_call(
        functools.partial(feed_back_kernel, per_seq, bits),
        grid=(base + steps,),
        in_specs=[
            hbm, pair, pair,
            pl.BlockSpec((deep, row_count), lambda i: (clip(i - three[0], 0, 7), 0)),
            hbm,
        ]
        + [rows] * 6
        + [pl.BlockSpec((1, HD, width), lambda i: (back(i), 0, 0)), vmem],
        out_specs=[vmem] * 3 + [pl.BlockSpec((BLOCK, 3 * width), lambda i: (back(i), 0))],
        out_shape=[
            jax.ShapeDtypeStruct((slab, hidden), WIDE),
            jax.ShapeDtypeStruct((slab, hidden), WIDE),
            jax.ShapeDtypeStruct((hidden // 32, width), WIDE),
            jax.ShapeDtypeStruct((row_count, 3 * width), LOW),
        ],
        scratch_shapes=[
            low((width, row_count)),
            low((row_count, width)),
            low((2, 2, 2, 2, slab, 2 * hidden)),
            low((2, 2, 2, slab, 2 * hidden)),
            low((2, 2, slab, 2 * hidden)),
            low((2, slab, 2 * hidden)),
            low((slab, 2 * hidden)),
            low((2, 2, 2, 2, 2, 2, slab, span)),
            low((2, 2, 2, 2, slab, 2 * hidden)),
            low((2, 2, 2, deep // 2, width)),
            low((2, 2, deep // 2, width)),
            low((2, deep // 2, width)),
            low((deep // 2, width)),
            low((2, 2, 2, deep // 2, width)),
            low((2, 2, 2, deep // 2, width)),
            pltpu.VMEM((hidden // 32, width), WIDE),
            pltpu.VMEM((hidden // 32, width), WIDE),
            low((seq_count, HD, width)),
            low((seq_count, HD, width)),
            pltpu.VMEM((HD, width), WIDE),
            low((8, 2, width // 16, CHUNK)),
            low((2, deep // 2, width)),
            pltpu.SemaphoreType.DMA((copies,)),
            pltpu.SemaphoreType.DMA((copies,)),
            pltpu.SemaphoreType.DMA((2,)),
        ],
        compiler_params=pltpu.CompilerParams(
            dimension_semantics=("arbitrary",),
            vmem_limit_bytes=63 << 20,
            collective_id=2,
            has_side_effects=True,
        ),
        cost_estimate=pl.CostEstimate(
            flops=6 * row_count * width * hidden + 12 * row_count * width * width,
            bytes_accessed=128 << 20,
            transcendentals=0,
        ),
    )(
        normed, grad_one, grad_two, glu, upstream, queries, keys, values, grad_attended,
        pre_query, pre_key, prefix, totals,
    )


WIDE_CHUNK = 512
PARTS = (2, 1, 2, 1, 1, 2, 1)
PART_ORDERS = ("y0x1", "0xy1", "x0y1", "0xy1", "y01x", "yx01", "x0y1")


def attend_weights_kernel(
    bits,
    normed_hbm, mixed_hbm, gated, grads, gain_term, rows_three, rows_gate, weights_hbm, tok,
    grad_residual,
    out, input_grad,
    normed, mixed, weights, acc, come1, come2, come3, come4, send, come, part,
    send_sems, recv_sems, local,
):
    step = pl.program_id(0)
    links = [bit for bit in bits if bit != CORE]
    mine = bit_value(CORE)
    other = 1 - mine
    sems = Sems(send_sems, recv_sems)
    width = tok.shape[1]
    per = width // WIDE_CHUNK
    chunks = 5 * per
    lead = acc.shape[:-1]
    fill = (slice(None),) * len(lead)

    def column(chunk):
        return chunk * WIDE_CHUNK + (128 if chunk >= per else 0)

    pieces, first = {}, 0
    launches = {}
    for n, count in enumerate(PARTS):
        cols = slice(column(first), column(first + count))
        first += count
        pieces[f"p{n}"] = Scatter(
            sems, links, PART_ORDERS[n], acc, send, come, (come1, come2, come3, come4), cols,
            cols, cols,
        )
        launches[first - 1] = [pieces[f"p{n}"].launch]
    load = [
        pltpu.make_async_copy(mixed_hbm, mixed, local.at[0]),
        pltpu.make_async_copy(normed_hbm, normed, local.at[1]),
        pltpu.make_async_copy(weights_hbm.at[:, : 4 * width], weights, local.at[2]),
    ]

    @pl.when(step == 0)
    def _():
        for copy in load:
            copy.start()
        greet(bits, far=False)
        load[0].wait()

    @pl.when(step == per)
    def _():
        load[1].wait()

    @pl.when(step == chunks)
    def _():
        load[2].wait()

    run_events(step, planned(ATTEND_BACK_PLAN, pieces, 0, chunks + 8))

    def chunk_phase(begin, end, lhs, rhs, shift):
        @pl.when((step >= begin) & (step < end))
        def _():
            at = pl.ds(pl.multiple_of(step * WIDE_CHUNK + shift, 128), WIDE_CHUNK)
            part[...] = dot_nn(lhs[...], rhs[...]).astype(LOW).reshape(part.shape)
            send[fill + (at,)] = part[:, other].reshape(lead + (WIDE_CHUNK,))
            acc[fill + (at,)] = part[:, mine].reshape(lead + (WIDE_CHUNK,))

    chunk_phase(0, per, mixed, gated, 0)
    chunk_phase(per, 2 * per, normed, gated, 128)
    chunk_phase(2 * per, chunks, normed, grads, 128)

    @pl.when(step == 0)
    def _():
        column = jnp.broadcast_to(gain_term[...], (128, width)).T
        column = column.reshape(8, 2, width // 16, 128)
        upper = mine.astype(WIDE)
        low, high = column[:, 0], column[:, 1]
        at = fill + (slice(width, width + 128),)
        acc[at] = (low * (1 - upper) + high * upper).astype(LOW).reshape(lead + (128,))
        send[at] = (low * upper + high * (1 - upper)).astype(LOW).reshape(lead + (128,))

    run_events(step, launches)

    @pl.when(step >= chunks)
    def _():
        def weight(n):
            return weights[:, n * width : (n + 1) * width]

        def row(n):
            return rows_three[:, n * width : (n + 1) * width]

        grad = dot_nt(row(0), weight(2)) + dot_nt(row(1), weight(0))
        grad += dot_nt(row(2), weight(1)) + dot_nt(rows_gate[...], weight(3))
        x = tok[...].astype(WIDE)
        grad = grad_residual[...] + norm_back(x, rms_scale(x), grad)
        input_grad[...] = grad.astype(input_grad.dtype)

    @pl.when(step == pl.num_programs(0) - 1)
    def _():
        for actions in planned(ATTEND_BACK_PLAN, pieces, chunks + 8, 1000).values():
            for action in actions:
                action()
        for piece in pieces.values():
            out[:, piece.columns] = piece.result()
        for piece in pieces.values():
            piece.drain()


def attend_weights(normed, mixed, gated, grads, gain_term, full_attn, tok, grad_residual):
    row_count, width = tok.shape
    steps = row_count // BLOCK
    bits = index_bits()
    per = width // WIDE_CHUNK
    chunks = 5 * per
    slab = width // 32
    vmem = pl.BlockSpec(memory_space=pltpu.VMEM)
    hbm = pl.BlockSpec(memory_space=pl.ANY)

    def rows(size, column=0):
        return pl.BlockSpec((BLOCK, size), lambda i: (clip(i - chunks, 0, steps - 1), column))

    def chunk(begin, count):
        return pl.BlockSpec(
            (row_count, WIDE_CHUNK), lambda i: (0, clip(i - begin, 0, count - 1))
        )

    low = functools.partial(pltpu.VMEM, dtype=LOW)
    columns = 5 * width + 128
    copies = 5 * len(PARTS)
    return pl.pallas_call(
        functools.partial(attend_weights_kernel, bits),
        grid=(chunks + steps,),
        in_specs=[hbm, hbm, chunk(0, 2 * per), chunk(2 * per, 3 * per), vmem, rows(3 * width),
                  rows(width, 1), hbm, rows(width), rows(width)],
        out_specs=[vmem, rows(width)],
        out_shape=[
            jax.ShapeDtypeStruct((slab, columns), WIDE),
            jax.ShapeDtypeStruct((row_count, width), LOW),
        ],
        scratch_shapes=[
            low((width, row_count)),
            low((width, row_count)),
            low((width, 4 * width)),
            low((2, 2, 2, 2, slab, columns)),
            low((2, 2, 2, slab, columns)),
            low((2, 2, slab, columns)),
            low((2, slab, columns)),
            low((slab, columns)),
            low((2, 2, 2, 2, slab, columns)),
            low((2, 2, 2, 2, slab, columns)),
            low((8, 2, width // 16, WIDE_CHUNK)),
            pltpu.SemaphoreType.DMA((copies,)),
            pltpu.SemaphoreType.DMA((copies,)),
            pltpu.SemaphoreType.DMA((3,)),
        ],
        compiler_params=pltpu.CompilerParams(
            dimension_semantics=("arbitrary",),
            vmem_limit_bytes=62 << 20,
            collective_id=3,
            has_side_effects=True,
        ),
        cost_estimate=pl.CostEstimate(
            flops=18 * row_count * width * width, bytes_accessed=64 << 20, transcendentals=0
        ),
    )(normed, mixed, gated, grads, gain_term, grads, gated, full_attn, tok, grad_residual)


ATTEND_PIECES = (
    (("a00", "10xy", 7), ("a01", "10yx", 6), ("a02", "10yx", 3)),
    (("a10", "10xy", 8), ("a11", "10yx", 5), ("a12", "1y0x", 3)),
    (("a20", "1x0y", 3), ("a21", "10yx", 4), ("a22", "10xy", 2)),
)
FEED_PIECES = (
    (("f0", "10yx", 11), ("f1", "10xy", 11)),
    (("f2", "10xy", 13), ("f3", "1y0x", 9)),
)
THREE_PIECES = (("f4", "10y", 4), ("f5", "y10", 4))
FORWARD_COPIES = 128


class ThreeGather(Gather):
    def first_swap(self, sems, columns, give, take, slab, target, local):
        self.cols, self.give, self.take, self.slab = columns, give, take, slab
        self.swap = sems.copy(give.at[:, columns], take.at[:, columns], (SIDE,))
        self.place = pltpu.make_async_copy(slab.at[:, columns], target.at[:, columns], local)

    def advance(self, k):
        if k == 0:
            self.swap.start()
            return
        if k == 1:
            self.swap.wait_recv()
            upper = bit_value(SIDE).astype(WIDE)
            mine, theirs = self.give[:, self.cols], self.take[:, self.cols]
            low = mine * (1 - upper) + theirs * upper
            high = mine * upper + theirs * (1 - upper)
            self.slab[:, self.cols] = jnp.concatenate([low, high], axis=0).astype(LOW)
            self.place.start()
            self.place.wait()
        super().advance(k - 1)

    def drain(self):
        super().drain()
        self.swap.wait_send()


def forward_kernel(
    steps, per_seq, bits,
    tok, s_key, s_value, s_query, s_gate, s_out, s_gain, s_one, s_two, s_three,
    normed, pre_key, keys, values, pre_query, queries, pre_gate, attended, mixed, residual,
    normed_two, up_one, up_two, prefix, gain_row, full_attn, full_one, full_two, full_three,
    held, held_one, held_two, all_keys, all_values, all_normed, totals, state_out, state_in, carry,
    three_out, three_in, three_slab, send, recv, local,
):
    step = pl.program_id(0)
    width = tok.shape[1]
    sems = Sems(send, recv)
    own = tuple(bit_value(bit) for bit in bits)
    side = bit_value(SIDE).astype(WIDE)
    pieces, waves, start = {}, [], 0
    for wave in ATTEND_PIECES:
        waves.append([])
        for name, order, tiles in wave:
            cols = slice(start, start + 128 * tiles)
            start += 128 * tiles
            pieces[name] = Gather(held, bits, order, sems, cols)
            waves[-1].append(pieces[name])
    feed = []
    for buf, parts in zip((held_one, held_two), FEED_PIECES):
        feed.append([])
        start = 0
        for name, order, tiles in parts:
            cols = slice(start, start + 128 * tiles)
            start += 128 * tiles
            pieces[name] = Gather(buf, bits, order, sems, cols)
            feed[-1].append(pieces[name])
    start, threes = 0, []
    for n, (name, order, tiles) in enumerate(THREE_PIECES):
        cols = slice(start, start + 128 * tiles)
        start += 128 * tiles
        pieces[name] = ThreeGather(full_three, bits[:-1], order, sems, cols)
        pieces[name].first_swap(
            sems, cols, three_out, three_in, three_slab, full_three.at[own[:-1]], local.at[2 + n]
        )
        threes.append(pieces[name])
    swap_state = sems.copy(state_out, state_in, (SIDE,))
    keep_attn = pltpu.make_async_copy(held, full_attn, local.at[4])
    keep_feed = [
        pltpu.make_async_copy(held_one, full_one, local.at[0]),
        pltpu.make_async_copy(held_two, full_two, local.at[1]),
    ]

    @pl.when(step == 0)
    def _():
        place = [
            pltpu.make_async_copy(s_one, held_one.at[own], local.at[0]),
            pltpu.make_async_copy(s_two, held_two.at[own], local.at[1]),
        ]
        for copy in place:
            copy.start()
        for n, shard in enumerate((s_key, s_value, s_query, s_gate, s_out)):
            held[own + (slice(None), slice(n * width, (n + 1) * width))] = shard[...]
        size = s_gain.shape[1]
        row = lax.broadcasted_iota(jnp.int32, (size, size), 0)
        col = lax.broadcasted_iota(jnp.int32, (size, size), 1)
        spread = jnp.broadcast_to(s_gain[...].astype(WIDE), (size, size))
        column = jnp.sum(jnp.where(row == col, spread, 0.0), axis=1, keepdims=True)
        column = jnp.broadcast_to(column, (size, 128)).astype(LOW)
        held[own + (slice(None), slice(5 * width, 5 * width + 128))] = column
        three_out[...] = s_three[...].astype(WIDE)
        greet(bits)
        for copy in place:
            copy.wait()
        for actions in planned(FORWARD_PLAN, pieces, 0, 1).values():
            for action in actions:
                action()
        for piece in waves[0]:
            piece.finish()

    @pl.when(step == steps)
    def _():
        for wave in waves[1:]:
            for piece in wave:
                piece.finish()
        keep_attn.start()
        column = held[..., 5 * width : 5 * width + 128].reshape(width, 128)
        gain_row[...] = column.astype(WIDE).T[:1]

    for n in range(4):

        @pl.when((step >= n * steps) & (step < (n + 1) * steps))
        def _():
            part = planned(FORWARD_PLAN, pieces, n * steps + 1, (n + 1) * steps + 1)
            run_events(step + 1, part)

    for n in range(2):

        @pl.when(step == (2 + n) * steps)
        def _():
            for piece in feed[n]:
                piece.finish()
            keep_feed[n].start()

    def weight(n):
        return held[..., n * width : (n + 1) * width].reshape(width, width)

    same = head_square()

    @pl.when(step < steps)
    def _():
        x = tok[...].astype(WIDE)
        rows = (x * rms_scale(x)).astype(LOW)
        normed[...] = rows.T
        here = pl.ds(pl.multiple_of(step * BLOCK, BLOCK), BLOCK)
        all_normed[here, :] = rows
        pre = dot_nn(rows, weight(0))
        pre_key[...] = pre.astype(LOW)
        k = jax.nn.silu(pre).astype(LOW)
        keys[...] = k
        all_keys[here, :] = k
        v = dot_nn(rows, weight(1)).astype(LOW)
        values[...] = v
        all_values[here, :] = v
        seq = step // per_seq

        @pl.when(step % per_seq == 0)
        def _():
            totals[seq] = jnp.zeros((HD, width), WIDE)

        for g in groups(width):
            totals[seq, :, g] += pack_state(dot_tn(k[:, g], v[:, g]), same)

    @pl.when(step == steps - 1)
    def _():
        state_out[...] = totals[...].astype(LOW)
        swap_state.start()

    @pl.when((step >= steps) & (step < 2 * steps))
    def _():
        at = step - steps
        here = pl.ds(pl.multiple_of(at * BLOCK, BLOCK), BLOCK)
        rows = all_normed[here, :]
        pre = dot_nn(rows, weight(2))
        pre_query[...] = pre.astype(LOW)
        queries[...] = jax.nn.silu(pre).astype(LOW)
        gate = dot_nn(rows, weight(3))
        pre_gate[...] = gate.astype(LOW)

        @pl.when(at == 0)
        def _():
            swap_state.wait_recv()

        @pl.when(at % per_seq == 0)
        def _():
            carry[...] = state_in[at // per_seq].astype(WIDE) * side

        marks = head_rows()
        prefix[0] = carry[...].astype(LOW)
        for g in groups(width):
            q, k, v = queries[:, g], all_keys[here, g], all_values[here, g]
            ks, vs = (
                (split_heads(part[:HALF], marks), split_heads(part[HALF:], marks))
                for part in (k, v)
            )
            carried = dot_nn(q, open_state(carry[:, g], same))
            out = causal_apply(causal_pair(q, *ks, True), *vs, True, carried)
            attended[:, g] = out.astype(LOW)
            carry[:, g] += pack_state(dot_tn(k, v), same)
        rows = attended[...].astype(WIDE)
        rows = rows * rms_scale(rows) * gain_row[...] * jax.nn.sigmoid(gate)
        rows = rows.astype(LOW)
        mixed[...] = rows.T
        res = tok[...].astype(WIDE) + dot_nn(rows, weight(4))
        residual[...] = res
        rows = (res * rms_scale(res)).astype(LOW)
        all_normed[here, :] = rows
        normed_two[...] = rows.T

    for n, (weights, result) in enumerate(((held_one, up_one), (held_two, up_two))):

        @pl.when((step >= (2 + n) * steps) & (step < (3 + n) * steps))
        def _():
            at = step - (2 + n) * steps
            rows = all_normed[pl.ds(pl.multiple_of(at * BLOCK, BLOCK), BLOCK), :]
            for c in groups(result.shape[1]):
                result[:, c] = dot_nn(rows, weights[..., c].reshape(width, GROUP)).astype(LOW)

    @pl.when(step == 4 * steps - 1)
    def _():
        for actions in planned(FORWARD_PLAN, pieces, 4 * steps + 1, 1000).values():
            for action in actions:
                action()
        for piece in threes:
            piece.finish()
        for piece in pieces.values():
            piece.drain()
        swap_state.wait_send()
        keep_attn.wait()
        for copy in keep_feed:
            copy.wait()


def forward(tok, seq_count, shards_attn, gain_row, s_one, s_two, s_three):
    row_count, width = tok.shape
    hidden = s_one.shape[1]
    steps = row_count // BLOCK
    per_seq = steps // seq_count
    bits = index_bits()
    lead = (2,) * len(bits)
    slab = s_one.shape[0]
    deep = s_three.shape[0]
    columns = 5 * width + 128

    def phase(n):
        return lambda i: clip(i - n * steps, 0, steps - 1)

    in_rows = rows_spec(width, order=lambda i: jnp.where(i < steps, i, phase(1)(i)))
    first, second = rows_spec(width, order=phase(0)), rows_spec(width, order=phase(1))
    first_turned = pl.BlockSpec((width, BLOCK), lambda i: (0, phase(0)(i)))
    second_turned = pl.BlockSpec((width, BLOCK), lambda i: (0, phase(1)(i)))
    third, fourth = rows_spec(hidden, order=phase(2)), rows_spec(hidden, order=phase(3))
    big_low = jax.ShapeDtypeStruct((row_count, hidden), LOW)
    any_spec = pl.BlockSpec(memory_space=pl.ANY)
    vmem = pl.BlockSpec(memory_space=pltpu.VMEM)

    def shape(*dims, dtype=LOW):
        return jax.ShapeDtypeStruct(dims, dtype)

    rows_low, turned_low = shape(row_count, width), shape(width, row_count)
    low = functools.partial(pltpu.VMEM, dtype=LOW)
    out = pl.pallas_call(
        functools.partial(forward_kernel, steps, per_seq, bits),
        grid=(4 * steps,),
        in_specs=[in_rows] + [vmem] * 6 + [any_spec] * 2 + [vmem],
        out_specs=[first_turned] + [first] * 3 + [second] * 4 + [second_turned, second]
        + [second_turned, third, fourth]
        + [
            pl.BlockSpec((1, HD, width), lambda i: (phase(1)(i), 0, 0)),
            pl.BlockSpec((1, width), lambda i: (0, 0)),
        ]
        + [any_spec] * 4,
        out_shape=[turned_low] + [rows_low] * 7 + [turned_low]
        + [
            shape(row_count, width, dtype=WIDE),
            turned_low, big_low, big_low,
            shape(steps, HD, width),
            shape(1, width, dtype=WIDE),
            shape(*lead, slab, columns),
            shape(*lead, slab, hidden),
            shape(*lead, slab, hidden),
            shape(*lead[:-1], 2 * deep, width),
        ],
        scratch_shapes=[
            low(lead + (slab, columns)),
            low(lead + (slab, hidden)),
            low(lead + (slab, hidden)),
            low((row_count, width)),
            low((row_count, width)),
            low((row_count, width)),
            pltpu.VMEM((seq_count, HD, width), WIDE),
            low((seq_count, HD, width)),
            low((seq_count, HD, width)),
            pltpu.VMEM((HD, width), WIDE),
            pltpu.VMEM((deep, width), WIDE),
            pltpu.VMEM((deep, width), WIDE),
            low((2 * deep, width)),
            pltpu.SemaphoreType.DMA((FORWARD_COPIES,)),
            pltpu.SemaphoreType.DMA((FORWARD_COPIES,)),
            pltpu.SemaphoreType.DMA((5,)),
        ],
        compiler_params=pltpu.CompilerParams(
            dimension_semantics=("arbitrary",),
            vmem_limit_bytes=62 << 20,
            collective_id=1,
            has_side_effects=True,
        ),
        cost_estimate=pl.CostEstimate(
            flops=28 * row_count * width * width, bytes_accessed=128 << 20, transcendentals=0
        ),
    )(tok, *shards_attn, gain_row, s_one, s_two, s_three)
    return list(out[:15]) + [
        out[15].reshape(-1, columns),
        out[16].reshape(-1, hidden),
        out[17].reshape(-1, hidden),
        out[18].reshape(-1, width),
    ]


def plain_shards(
    tokens,
    lengths,
    w_query,
    w_key,
    w_value,
    w_gate,
    out_gain,
    w_out,
    w_one,
    w_two,
    w_three,
    cotangent,
):
    seq_count, local_length, width = tokens.shape
    row_count = seq_count * local_length
    hidden = w_one.shape[1]
    steps = row_count // BLOCK
    per_seq = local_length // BLOCK
    orders = stream_orders()
    tok = tokens.reshape(row_count, width)
    cot = cotangent.reshape(row_count, width)
    full_key = gather_rows(w_key, orders[0])
    full_value = gather_rows(w_value, orders[1])
    full_query = gather_rows(w_query, orders[2])
    full_gate = gather_rows(w_gate, orders[0])
    gain_columns = jnp.broadcast_to(out_gain[:, None], (out_gain.shape[0], 128))
    full_out = gather_rows(jnp.concatenate([w_out, gain_columns], axis=1), orders[1])
    full_one = gather_rows(w_one, orders[2])
    full_two = gather_rows(w_two, orders[0])
    full_three = gather_rows(w_three, orders[1])
    gain = full_out[:, width].astype(WIDE)[None, :]
    full_out = full_out[:, :width]

    rows = rows_spec(width)
    narrow = ((row_count, width), LOW, rows)
    wide = ((row_count, width), WIDE, rows)
    big = ((row_count, hidden), LOW, rows_spec(hidden))
    state_spec = pl.BlockSpec((1, HD, width), lambda i: (i // per_seq, 0, 0))
    state = ((seq_count, HD, width), WIDE, state_spec)
    square = 2 * row_count * width * width

    normed_low, pre_key, keys, values, totals = call(
        lambda *refs: key_value_kernel(per_seq, *refs),
        steps,
        [(tok, rows), (full_key, whole_spec(full_key)), (full_value, whole_spec(full_value))],
        [narrow, narrow, narrow, narrow, state],
        flops=2 * square,
    )
    incoming = shift_sum(totals, "fsdp", False)
    pre_query, queries, pre_gate = call(
        query_gate_kernel,
        steps,
        [(normed_low, rows), (full_query, whole_spec(full_query)), (full_gate, whole_spec(full_gate))],
        [narrow, narrow, narrow],
        flops=2 * square,
    )
    prefix_spec = pl.BlockSpec((1, HD, width), lambda i: (i, 0, 0))
    attended, mixed, residual, prefix = call(
        lambda *refs: attend_kernel(per_seq, *refs),
        steps,
        [(queries, rows), (keys, rows), (values, rows), (pre_gate, rows), (tok, rows),
         (incoming, state_spec), (gain, whole_spec(gain)), (full_out, whole_spec(full_out))],
        [narrow, narrow, wide, ((steps, HD, width), LOW, prefix_spec)],
        scratch=[pltpu.VMEM((HD, width), WIDE)],
        flops=3 * square,
    )
    (
        layer_out, normed_two, glu, grad_up_one, grad_up_two, upstream_low, grad_residual,
        gated, grad_attended, grad_totals, grad_gain_term,
    ) = call(
        lambda *refs: feed_kernel(per_seq, False, *refs),
        steps,
        [(lengths, pl.BlockSpec(memory_space=pltpu.SMEM)), (residual, rows), (cot, rows),
         (full_one, whole_spec(full_one)), (full_two, whole_spec(full_two)),
         (full_three, whole_spec(full_three)), (full_out, whole_spec(full_out)),
         (gain, whole_spec(gain)), (pre_gate, rows), (attended, rows), (queries, rows)],
        [narrow, narrow, big, big, big, narrow, wide,
         ((row_count, 2 * width), LOW, rows_spec(2 * width)), narrow, state,
         ((1, width), WIDE, pl.BlockSpec((1, width), lambda i: (0, 0)))],
        flops=12 * row_count * width * hidden + square,
    )
    grad_residual_low, grad_pre_gate = gated[:, :width], gated[:, width:]
    outgoing = shift_sum(grad_totals, "fsdp", True)
    grad_one = scatter_rows(dot_tn(normed_two, grad_up_one), orders[1])
    grad_two = scatter_rows(dot_tn(normed_two, grad_up_two), orders[2])
    grad_three = scatter_rows(dot_tn(glu, upstream_low), orders[0])
    gain_term = jnp.broadcast_to(grad_gain_term.reshape(width, 1), (width, 128))
    grad_out = scatter_rows(
        jnp.concatenate([dot_tn(mixed, grad_residual_low), gain_term], axis=1), orders[1]
    )
    grad_gain = grad_out[:, width]
    grad_out = grad_out[:, :width]

    def back(i):
        return (i // per_seq) * per_seq + per_seq - 1 - i % per_seq

    back_rows = rows_spec(width, order=back)
    back_narrow = ((row_count, width), LOW, back_rows)
    grad_pre_query, grad_pre_key, grad_pre_value = call(
        lambda *refs: attend_back_kernel(per_seq, *refs),
        steps,
        [(queries, back_rows), (keys, back_rows), (values, back_rows),
         (grad_attended, back_rows), (pre_query, back_rows), (pre_key, back_rows),
         (prefix, pl.BlockSpec((1, HD, width), lambda i: (back(i), 0, 0))),
         (outgoing, state_spec)],
        [back_narrow, back_narrow, back_narrow],
        scratch=[pltpu.VMEM((HD, width), WIDE)],
        flops=6 * square,
    )
    grad_query = scatter_rows(dot_tn(normed_low, grad_pre_query), orders[0])
    grad_key = scatter_rows(dot_tn(normed_low, grad_pre_key), orders[1])
    grad_value = scatter_rows(dot_tn(normed_low, grad_pre_value), orders[2])
    grad_gate = scatter_rows(dot_tn(normed_low, grad_pre_gate), orders[0])
    (input_grad,) = call(
        input_kernel,
        steps,
        [(grad_pre_query, rows), (grad_pre_key, rows), (grad_pre_value, rows),
         (grad_pre_gate, rows), (full_query, whole_spec(full_query)),
         (full_key, whole_spec(full_key)), (full_value, whole_spec(full_value)),
         (full_gate, whole_spec(full_gate)), (tok, rows), (grad_residual, rows)],
        [wide],
        flops=4 * square,
    )
    return (
        layer_out.reshape(tokens.shape),
        input_grad.reshape(tokens.shape),
        grad_query,
        grad_key,
        grad_value,
        grad_gate,
        grad_gain,
        grad_out,
        grad_one,
        grad_two,
        grad_three,
    )


def feed_step_kernel(
    steps, per_seq, lengths, residual, cotangent, up_one, up_two, all_one, all_two, all_three,
    all_attn, gain, pre_gate, attended, queries,
    layer_out, glu, grad_one, grad_two, upstream_low, grad_residual, gated, grad_attended,
    totals, grad_gain, product, last_back, last_residual, last_upstream,
    w_one, w_two, w_three, w_out, local,
):
    step = pl.program_id(0)
    row_count, width = residual.shape

    hidden = w_one.shape[1]
    loads = {}
    for n, part in enumerate((slice(0, 768), slice(768, 1792), slice(1792, hidden))):
        loads[part.start] = pltpu.make_async_copy(
            all_three.at[part], w_three.at[part], local.at[n]
        )
    later = [
        pltpu.make_async_copy(all_one, w_one, local.at[3]),
        pltpu.make_async_copy(all_two, w_two, local.at[4]),
        pltpu.make_async_copy(all_attn.at[:, 4 * width : 5 * width], w_out, local.at[5]),
    ]

    def norm_part(rows):
        res = last_residual[rows, :]
        grad = last_upstream[rows, :].astype(WIDE)
        grad += norm_back(res, rms_scale(res), last_back[rows, :])
        grad_residual[rows, :] = grad
        gated[rows, :width] = grad.astype(LOW)

    def out_part():
        last_back[...] = dot_nt(gated[:, :width], w_out[...])
        grad_gain[...] = jnp.where(step == 1, 0.0, grad_gain[...])

    def gate_part(rows):
        grad = last_back[rows, :]
        gate = jax.nn.sigmoid(pre_gate[rows, :].astype(WIDE))
        att = attended[rows, :].astype(WIDE)
        scale = rms_scale(att)
        hat = att * scale
        grad = grad * gate
        grad_gain[...] += jnp.sum(grad * hat, axis=0, keepdims=True)
        grad = grad * gain[...]
        gated[rows, width:] = (grad * hat * (1.0 - gate)).astype(LOW)
        grad_attended[rows, :] = norm_back(att, scale, grad).astype(LOW)

    def state_part():
        fresh = (step - 1) % per_seq == 0
        same = head_square()
        for g in groups(width):
            term = pack_state(dot_tn(queries[:, g], grad_attended[:, g]), same)
            totals[0, :, g] = jnp.where(fresh, 0.0, totals[0, :, g]) + term

    def cut(count, n):
        size = row_count // count
        return slice(n * size, (n + 1) * size)

    tail = [functools.partial(norm_part, cut(2, n)) for n in range(2)] + [out_part]
    tail += [functools.partial(gate_part, cut(8, n)) for n in range(8)] + [state_part]

    def begin(todo, loading=False):
        spot = lax.broadcasted_iota(jnp.int32, (row_count, 1), 0) + (step % per_seq) * row_count
        limit = lengths[step // per_seq] - lax.axis_index("fsdp") * per_seq * row_count
        valid = (spot < limit).astype(WIDE)
        up_low = (cotangent[...].astype(WIDE) * valid).astype(LOW)
        upstream_low[...] = up_low
        todo = list(todo)
        for c in groups(hidden):
            if loading and c.start in loads:
                loads[c.start].wait()
            back = dot_nt(up_low, w_three[c, :])
            if todo:
                todo.pop(0)()
            one, two = up_one[:, c].astype(WIDE), up_two[:, c].astype(WIDE)
            both = (one * two).astype(LOW)
            product[:, c] = both
            glu[c, :] = both.T
            grad_one[:, c] = (back * two).astype(LOW)
            grad_two[:, c] = (back * one).astype(LOW)
        for part in todo:
            part()
        res = residual[...]
        layer_out[...] = (valid * (res + dot_nn(product[...], w_three[...]))).astype(LOW)
        if loading:
            for copy in later:
                copy.wait()
        back = dot_nt(grad_one[...], w_one[...]) + dot_nt(grad_two[...], w_two[...])
        last_back[...] = back
        last_residual[...] = res
        last_upstream[...] = up_low

    @pl.when(step == 0)
    def _():
        for copy in list(loads.values()) + later:
            copy.start()
        begin([], loading=True)

    @pl.when((step > 0) & (step < steps))
    def _():
        begin(tail)

    @pl.when(step == steps)
    def _():
        for part in tail:
            part()


def feed(
    seq_count, lengths, residual, cot, up_one, up_two, full_one, full_two, full_three, full_attn,
    gain, pre_gate, attended, queries,
):
    row_count, width = residual.shape
    hidden = full_one.shape[1]
    steps = row_count // BLOCK
    per_seq = steps // seq_count

    def now(i):
        return jnp.minimum(i, steps - 1)

    def last(i):
        return jnp.maximum(i - 1, 0)

    rows = rows_spec(width, order=now)
    done = rows_spec(width, order=last)
    narrow = ((row_count, width), LOW, rows)
    big = ((row_count, hidden), LOW, rows_spec(hidden, order=now))

    turned = (
        (hidden, row_count), LOW, pl.BlockSpec((hidden, BLOCK), lambda i: (0, now(i)))
    )
    state_spec = pl.BlockSpec((1, HD, width), lambda i: (last(i) // per_seq, 0, 0))
    hbm = pl.BlockSpec(memory_space=pl.ANY)
    return call(
        lambda *refs: feed_step_kernel(steps, per_seq, *refs),
        steps + 1,
        [(lengths, pl.BlockSpec(memory_space=pltpu.SMEM)), (residual, rows), (cot, rows),
         (up_one, big[2]), (up_two, big[2]),
         (full_one, hbm), (full_two, hbm), (full_three, hbm), (full_attn, hbm),
         (gain, whole_spec(gain)), (pre_gate, done), (attended, done), (queries, done)],
        [narrow, turned, big, big, narrow,
         ((row_count, width), WIDE, done),
         ((row_count, 2 * width), LOW, rows_spec(2 * width, order=last)),
         ((row_count, width), LOW, done),
         ((seq_count, HD, width), WIDE, state_spec),
         ((1, width), WIDE, pl.BlockSpec((1, width), lambda i: (0, 0)))],
        scratch=[pltpu.VMEM((BLOCK, hidden), LOW), pltpu.VMEM((BLOCK, width), WIDE),
                 pltpu.VMEM((BLOCK, width), WIDE), pltpu.VMEM((BLOCK, width), LOW),
                 pltpu.VMEM((width, hidden), LOW), pltpu.VMEM((width, hidden), LOW),
                 pltpu.VMEM((hidden, width), LOW), pltpu.VMEM((width, width), LOW),
                 pltpu.SemaphoreType.DMA((6,))],
        flops=8 * row_count * width * hidden + 2 * row_count * width * width,
        limit=60,
    )


def fused_shards(
    tokens,
    lengths,
    w_query,
    w_key,
    w_value,
    w_gate,
    out_gain,
    w_out,
    w_one,
    w_two,
    w_three,
    cotangent,
):
    seq_count, local_length, width = tokens.shape
    row_count = seq_count * local_length
    tok = tokens.reshape(row_count, width)
    cot = cotangent.reshape(row_count, width)
    (
        normed_low, pre_key, keys, values, pre_query, queries, pre_gate, attended, mixed,
        residual, normed_two, up_one, up_two, prefix, gain, full_attn, full_one, full_two,
        full_three,
    ) = forward(
        tok, seq_count, (w_key, w_value, w_query, w_gate, w_out), out_gain[None, :], w_one, w_two, w_three
    )

    (
        layer_out, glu, grad_up_one, grad_up_two, upstream_low, grad_residual, gated,
        grad_attended, grad_totals, grad_gain_term,
    ) = feed(
        seq_count, lengths, residual, cot, up_one, up_two, full_one, full_two, full_three,
        full_attn, gain, pre_gate, attended, queries,
    )
    grad_one, grad_two, grad_three, grad_three_pre = feed_back(
        seq_count, normed_two, grad_up_one, grad_up_two, glu, upstream_low, queries, keys, values,
        grad_attended, pre_query, pre_key, prefix, grad_totals,
    )
    grads, input_grad = attend_weights(
        normed_low, mixed, gated, grad_three_pre, grad_gain_term, full_attn, tok, grad_residual
    )
    grad_out, grad_gain = grads[:, :width], grads[:, width]
    grad_gate, grad_query, grad_key, grad_value = (
        grads[:, 128 + n * width : 128 + (n + 1) * width] for n in range(1, 5)
    )
    return (
        layer_out.reshape(tokens.shape),
        input_grad.astype(WIDE).reshape(tokens.shape),
        grad_query,
        grad_key,
        grad_value,
        grad_gate,
        grad_gain,
        grad_out,
        grad_one,
        grad_two,
        grad_three,
    )


def shards(*arrays):
    tokens, w_query, w_three = arrays[0], arrays[2], arrays[10]
    sizes = (lax.axis_size("dp"), lax.axis_size("fsdp"))
    fits = w_query.shape[0] % 16 == 0 and w_three.shape[0] % 8 == 0 and tokens.shape[1] >= 4 * BLOCK
    if sizes == (16, 2) and fits:
        return fused_shards(*arrays)
    return plain_shards(*arrays)


def solution(mesh):
    in_specs = (
        P("dp", "fsdp", None),
        P("dp"),
        P(("dp", "fsdp"), None),
        P(("dp", "fsdp"), None),
        P(("dp", "fsdp"), None),
        P(("dp", "fsdp"), None),
        P(("dp", "fsdp")),
        P(("dp", "fsdp"), None),
        P(("dp", "fsdp"), None),
        P(("dp", "fsdp"), None),
        P(("dp", "fsdp"), None),
        P("dp", "fsdp", None),
    )
    out_specs = (
        P("dp", "fsdp", None),
        P("dp", "fsdp", None),
        P(("dp", "fsdp"), None),
        P(("dp", "fsdp"), None),
        P(("dp", "fsdp"), None),
        P(("dp", "fsdp"), None),
        P(("dp", "fsdp")),
        P(("dp", "fsdp"), None),
        P(("dp", "fsdp"), None),
        P(("dp", "fsdp"), None),
        P(("dp", "fsdp"), None),
    )
    return jax.shard_map(shards, mesh=mesh, in_specs=in_specs, out_specs=out_specs, check_vma=False)
```

```python
import functools

import jax
import jax.numpy as jnp
from jax import lax
from jax.experimental import pallas as pl
from jax.experimental.pallas import tpu as pltpu
from jax.sharding import PartitionSpec as P

HD = 64
H = 16
BLOCK = 256


GROUP = 256
HEADS = GROUP // HD
LOW = jnp.bfloat16
WIDE = jnp.float32

norm_epsilon = 1e-06


def bit_steps():
    steps = []
    for axis in ("dp", "fsdp"):
        size = lax.axis_size(axis)
        bit = 0
        while (1 << bit) < size:
            steps.append((axis, bit, [(i, i ^ (1 << bit)) for i in range(size)]))
            bit += 1
    return steps


def stream_orders():
    steps = bit_steps()
    dp = [s for s in steps if s[0] == "dp"]
    fs = [s for s in steps if s[0] == "fsdp"]
    core, rest = dp[0], fs[:1] + dp[1:3]
    tail = dp[3:] + fs[1:]
    return [[core] + rest[k:] + rest[:k] + tail for k in range(3)]


def own_bit(step):
    axis, bit, _ = step
    return lax.rem(lax.div(lax.axis_index(axis), 1 << bit), 2)


def bit_dims():
    steps = bit_steps()
    dp = sorted([s for s in steps if s[0] == "dp"], key=lambda s: -s[1])
    fs = sorted([s for s in steps if s[0] == "fsdp"], key=lambda s: -s[1])
    return [(s[0], s[1]) for s in dp + fs]


def gather_rows(shard, order):
    dims = bit_dims()
    held = []
    data = shard
    for step in reversed(order):
        axis, bit, perm = step
        other = lax.ppermute(data, axis, perm)
        mine = own_bit(step) == 0
        place = sum(1 for d in held if dims.index(d) < dims.index((axis, bit)))
        held.append((axis, bit))
        data = jnp.stack(
            [jnp.where(mine, data, other), jnp.where(mine, other, data)], axis=place
        )
    return data.reshape((-1,) + shard.shape[1:])


def scatter_rows(full, order):
    dims = bit_dims()
    rows = full.shape[0] >> len(dims)
    data = full.astype(jnp.bfloat16).reshape((2,) * len(dims) + (rows,) + full.shape[1:])
    left = list(dims)
    for at, step in enumerate(order):
        axis, bit, perm = step
        place = left.index((axis, bit))
        left.pop(place)
        own = own_bit(step)
        send = lax.dynamic_index_in_dim(data, 1 - own, place, keepdims=False)
        keep = lax.dynamic_index_in_dim(data, own, place, keepdims=False)
        come = lax.ppermute(send, axis, perm)
        data = keep.astype(jnp.float32) + come.astype(jnp.float32)
        if at < len(order) - 1:
            data = data.astype(jnp.bfloat16)
    return data


def shift_sum(x, axis, reverse):
    size = lax.axis_size(axis)
    total = jnp.zeros_like(x)
    low = x.astype(jnp.bfloat16)
    for s in range(1, size):
        pairs = [(i + s, i) if reverse else (i, i + s) for i in range(size - s)]
        total = total + lax.ppermute(low, axis, pairs).astype(x.dtype)
    return total


def dot_nn(a, b):
    return jnp.dot(a, b, preferred_element_type=WIDE)


def dot_nt(a, b):
    return lax.dot_general(a, b, (((1,), (1,)), ((), ())), preferred_element_type=WIDE)


def dot_tn(a, b):
    return lax.dot_general(a, b, (((0,), (0,)), ((), ())), preferred_element_type=WIDE)


def rms_scale(values):
    return lax.rsqrt(jnp.mean(values * values, axis=-1, keepdims=True) + norm_epsilon)


def norm_back(values, scale, upstream):
    inner_mean = jnp.mean(upstream * values, axis=-1, keepdims=True)
    return scale * (upstream - values * (scale * scale) * inner_mean)


def silu_slope(pre_rows):
    logistic = pl.reciprocal(1.0 + jnp.exp(-pre_rows), approx=True)
    return logistic * (1.0 + pre_rows * (1.0 - logistic))


def head_square():
    row = lax.broadcasted_iota(jnp.int32, (GROUP, GROUP), 0) // HD
    col = lax.broadcasted_iota(jnp.int32, (GROUP, GROUP), 1) // HD
    return (row == col).astype(WIDE)


def head_rows():
    lane = lax.broadcasted_iota(jnp.int32, (1, GROUP), 1) // HD
    return [(lane == h).astype(WIDE).astype(LOW) for h in range(HEADS)]


def split_heads(rows, marks):
    return jnp.concatenate([rows * mark for mark in marks], axis=0)


def pack_state(square, same):
    return jnp.sum((square * same).reshape(HEADS, HD, GROUP), axis=0)


def open_state(packed, same):
    return (jnp.concatenate([packed] * HEADS, axis=0) * same).astype(LOW)


def causal_masks():
    i = lax.broadcasted_iota(jnp.int32, (BLOCK, HEADS * BLOCK), 0)
    j = lax.broadcasted_iota(jnp.int32, (BLOCK, HEADS * BLOCK), 1) % BLOCK
    return (i >= j).astype(WIDE), (j >= i).astype(WIDE)


def groups(width):
    return [slice(g * GROUP, (g + 1) * GROUP) for g in range(width // GROUP)]


def key_value_kernel(per_seq, tok, w_key, w_value, normed, pre_key, keys, values, totals):
    x = tok[...].astype(WIDE)
    rows = (x * rms_scale(x)).astype(LOW)
    normed[...] = rows
    pre = dot_nn(rows, w_key[...])
    pre_key[...] = pre.astype(LOW)
    k = jax.nn.silu(pre).astype(LOW)
    keys[...] = k
    v = dot_nn(rows, w_value[...]).astype(LOW)
    values[...] = v

    @pl.when(pl.program_id(0) % per_seq == 0)
    def _():
        totals[...] = jnp.zeros_like(totals)

    same = head_square()
    for g in groups(k.shape[1]):
        totals[0, :, g] += pack_state(dot_tn(k[:, g], v[:, g]), same)


def query_gate_kernel(normed, w_query, w_gate, pre_query, queries, pre_gate):
    rows = normed[...]
    pre = dot_nn(rows, w_query[...])
    pre_query[...] = pre.astype(LOW)
    queries[...] = jax.nn.silu(pre).astype(LOW)
    pre_gate[...] = dot_nn(rows, w_gate[...]).astype(LOW)


def attend_kernel(
    per_seq, queries, keys, values, pre_gate, tok, incoming, gain, w_out,
    attended, mixed, residual, prefix, carry,
):
    @pl.when(pl.program_id(0) % per_seq == 0)
    def _():
        carry[...] = incoming[0]

    same, marks = head_square(), head_rows()
    causal, _ = causal_masks()
    prefix[0] = carry[...].astype(LOW)
    for g in groups(queries.shape[1]):
        q, k, v = queries[:, g], keys[:, g], values[:, g]
        scores = (dot_nt(q, split_heads(k, marks)) * causal).astype(LOW)
        out = dot_nn(scores, split_heads(v, marks))
        out += dot_nn(q, open_state(carry[:, g], same))
        attended[:, g] = out.astype(LOW)
        carry[:, g] += pack_state(dot_tn(k, v), same)
    rows = attended[...].astype(WIDE)
    gate = jax.nn.sigmoid(pre_gate[...].astype(WIDE))
    rows = (rows * rms_scale(rows) * gain[...] * gate).astype(LOW)
    mixed[...] = rows
    residual[...] = tok[...].astype(WIDE) + dot_nn(rows, w_out[...])


def feed_kernel(
    per_seq, turned, lengths, residual, cotangent, w_one, w_two, w_three, w_out, gain, pre_gate,
    attended, queries,
    layer_out, normed, glu, grad_one, grad_two, upstream_low, grad_residual, gated,
    grad_attended, totals, grad_gain, held=None,
):
    step = pl.program_id(0)
    row_count = residual.shape[0]
    spot = lax.broadcasted_iota(jnp.int32, (row_count, 1), 0) + (step % per_seq) * row_count
    limit = lengths[step // per_seq] - lax.axis_index("fsdp") * per_seq * row_count
    valid = (spot < limit).astype(WIDE)
    res = residual[...]
    scale = rms_scale(res)
    rows = (res * scale).astype(LOW)
    normed[...] = rows.T if turned else rows
    upstream = cotangent[...].astype(WIDE) * valid
    up_low = upstream.astype(LOW)
    upstream_low[...] = up_low
    for c in groups(w_one.shape[1]):
        one = dot_nn(rows, w_one[:, c])
        two = dot_nn(rows, w_two[:, c])
        back = dot_nt(up_low, w_three[c, :])
        product = (one * two).astype(LOW)
        if turned:
            held[:, c] = product
            glu[c, :] = product.T
        else:
            glu[:, c] = product
        grad_one[:, c] = (back * two).astype(LOW)
        grad_two[:, c] = (back * one).astype(LOW)
    layer_out[...] = (valid * (res + dot_nn(held[...] if turned else glu[...], w_three[...]))).astype(LOW)
    back = dot_nt(grad_one[...], w_one[...]) + dot_nt(grad_two[...], w_two[...])
    grad = upstream + norm_back(res, scale, back)
    grad_residual[...] = grad
    grad = grad.astype(LOW)
    width = grad.shape[1]
    gated[:, :width] = grad
    grad = dot_nt(grad, w_out[...])
    gate = jax.nn.sigmoid(pre_gate[...].astype(WIDE))
    att = attended[...].astype(WIDE)
    scale = rms_scale(att)
    hat = att * scale
    grad = grad * gate

    @pl.when(step == 0)
    def _():
        grad_gain[...] = jnp.zeros_like(grad_gain)

    grad_gain[...] += jnp.sum(grad * hat, axis=0, keepdims=True)
    grad = grad * gain[...]
    gated[:, width:] = (grad * hat * (1.0 - gate)).astype(LOW)
    grad_att = norm_back(att, scale, grad).astype(LOW)
    grad_attended[...] = grad_att

    @pl.when(step % per_seq == 0)
    def _():
        totals[...] = jnp.zeros_like(totals)

    same = head_square()
    for g in groups(grad_att.shape[1]):
        totals[0, :, g] += pack_state(dot_tn(queries[:, g], grad_att[:, g]), same)


def attend_back_kernel(
    per_seq, queries, keys, values, grad_attended, pre_query, pre_key, prefix, incoming,
    grad_query, grad_key, grad_value, carry,
):
    @pl.when(pl.program_id(0) % per_seq == 0)
    def _():
        carry[...] = incoming[0]

    same, marks = head_square(), head_rows()
    causal, causal_t = causal_masks()
    for g in groups(queries.shape[1]):
        q, k, v, ga = queries[:, g], keys[:, g], values[:, g], grad_attended[:, g]
        qs, ks, vs, gs = (split_heads(rows, marks) for rows in (q, k, v, ga))
        state = open_state(prefix[0, :, g].astype(WIDE), same)
        grad_state = open_state(carry[:, g], same)
        grad_scores = (dot_nt(ga, vs) * causal).astype(LOW)
        gq = dot_nn(grad_scores, ks) + dot_nt(ga, state)
        grad_scores = (dot_nt(v, gs) * causal_t).astype(LOW)
        gk = dot_nn(grad_scores, qs) + dot_nt(v, grad_state)
        scores = (dot_nt(k, qs) * causal_t).astype(LOW)
        gv = dot_nn(scores, gs) + dot_nn(k, grad_state)
        grad_query[:, g] = (gq * silu_slope(pre_query[:, g].astype(WIDE))).astype(LOW)
        grad_key[:, g] = (gk * silu_slope(pre_key[:, g].astype(WIDE))).astype(LOW)
        grad_value[:, g] = gv.astype(LOW)
        carry[:, g] += pack_state(dot_tn(q, ga), same)


def input_kernel(
    grad_query, grad_key, grad_value, grad_gate, w_query, w_key, w_value, w_gate, tok,
    grad_residual, input_grad,
):
    grad = dot_nt(grad_query[...], w_query[...]) + dot_nt(grad_key[...], w_key[...])
    grad += dot_nt(grad_value[...], w_value[...]) + dot_nt(grad_gate[...], w_gate[...])
    x = tok[...].astype(WIDE)
    input_grad[...] = grad_residual[...] + norm_back(x, rms_scale(x), grad)


def rows_spec(width, block=BLOCK, order=lambda i: i):
    return pl.BlockSpec((block, width), lambda i: (order(i), 0))


def whole_spec(array):
    rank = array.ndim
    return pl.BlockSpec(array.shape, lambda i: (0,) * rank, pipeline_mode=pl.Buffered(1))


def call(kernel, steps, operands, results, scratch=(), flops=0, limit=56):
    moved = sum(a.size * a.dtype.itemsize for a, _ in operands)
    return pl.pallas_call(
        kernel,
        grid=(steps,),
        in_specs=[spec for _, spec in operands],
        out_specs=[spec for _, _, spec in results],
        out_shape=[jax.ShapeDtypeStruct(shape, dtype) for shape, dtype, _ in results],
        scratch_shapes=list(scratch),
        compiler_params=pltpu.CompilerParams(
            dimension_semantics=("arbitrary",), vmem_limit_bytes=limit << 20
        ),
        cost_estimate=pl.CostEstimate(flops=flops, bytes_accessed=moved, transcendentals=0),
    )(*[a for a, _ in operands])


def index_bits():
    bits = []
    for axis in ("dp", "fsdp"):
        count = lax.axis_size(axis).bit_length() - 1
        bits += [(axis, bit) for bit in reversed(range(count))]
    return bits


LINKS = {
    "1": (("dp", 3),),
    "0": (("dp", 2),),
    "z": (("dp", 3), ("dp", 2)),
    "y": (("dp", 1),),
    "x": (("fsdp", 0),),
}
CORE = ("dp", 0)
SIDE = ("fsdp", 0)


def bit_value(bit):
    axis, at = bit
    return lax.rem(lax.div(lax.axis_index(axis), 1 << at), 2)


def flips_of(name):
    group = LINKS[name]
    if len(group) == 1:
        return [group]
    return [group[:1], group[1:], group]


def flip_device(flips):
    place = {}
    for axis, at in flips:
        moved = place.get(axis, lax.axis_index(axis))
        place[axis] = moved + (1 - 2 * bit_value((axis, at))) * (1 << at)
    return place


def greet(bits, far=True):
    partners = [(bit,) for bit in bits] + ([LINKS["z"]] if far else [])
    barrier = pltpu.get_barrier_semaphore()
    for flips in partners:
        pl.semaphore_signal(
            barrier, inc=1, device_id=flip_device(flips), device_id_type=pl.DeviceIdType.MESH
        )
    pl.semaphore_wait(barrier, len(partners))


class Sems:
    def __init__(self, send, recv):
        self.send, self.recv, self.used = send, recv, 0

    def copy(self, src, dst, flips):
        at = self.used
        self.used += 1
        return pltpu.make_async_remote_copy(
            src_ref=src,
            dst_ref=dst,
            send_sem=self.send.at[at],
            recv_sem=self.recv.at[at],
            device_id=flip_device(flips),
            device_id_type=pl.DeviceIdType.MESH,
        )


class Gather:
    def __init__(self, buf, bits, order, sems, columns=slice(None)):
        self.stages, held = [], []

        def cube(flips=()):
            index = []
            for bit in bits:
                if bit in held:
                    index.append(slice(None))
                else:
                    index.append(1 - bit_value(bit) if bit in flips else bit_value(bit))
            return buf.at[tuple(index) + (slice(None), columns)]

        for n, name in enumerate(order):
            ref, flips = cube(), flips_of(name)
            self.stages.append([sems.copy(ref, ref, flip) for flip in flips])
            if n == len(order) - 1:
                self.near = sems.copy(ref, ref, (CORE,))
                far = [cube(flip) for flip in flips]
                self.stages.append([sems.copy(ref, ref, (CORE,)) for ref in far])
            held.extend(LINKS[name])

    def start(self, k):
        for copy in self.stages[k]:
            copy.start()
        if k == len(self.stages) - 2:
            self.near.start()

    def advance(self, k):
        if k:
            for copy in self.stages[k - 1]:
                copy.wait_recv()
        self.start(k)

    def finish(self):
        self.near.wait_recv()
        for copy in self.stages[-1]:
            copy.wait_recv()

    def drain(self):
        for copy in [c for stage in self.stages for c in stage] + [self.near]:
            copy.wait_send()


class Scatter:
    def __init__(
        self, sems, bits, order, acc, send, come, recvs, columns, send_columns, come_columns
    ):
        self.bits, self.order, self.acc, self.columns = bits, order, acc, columns
        self.come, self.recvs, self.come_columns = come, recvs, come_columns
        rows = (slice(None),)
        full = (slice(None),) * len(bits) + rows
        self.core = sems.copy(
            send.at[full + (send_columns,)], come.at[full + (come_columns,)], (CORE,)
        )
        self.copies, self.done = [], []
        for k, name in enumerate(order):
            (bit,) = LINKS[name]
            done = [LINKS[n][0] for n in order[:k]]
            index = tuple(
                1 - bit_value(b) if b == bit else bit_value(b) if b in done else slice(None)
                for b in bits
            )
            free = (slice(None),) * (len(bits) - k - 1)
            source = acc.at[index + rows + (columns,)]
            self.copies.append(sems.copy(source, recvs[k].at[free + rows + (columns,)], (bit,)))
            self.done.append(done)

    def add(self, done, source, columns):
        free = [b for b in self.bits if b not in done]

        def one(k):
            at = [(k // (1 << (len(free) - 1 - n))) % 2 for n in range(len(free))]
            mine = tuple(bit_value(b) if b in done else at[free.index(b)] for b in self.bits)
            here = mine + (slice(None), self.columns)
            self.acc[here] = self.acc[here] + source[tuple(at) + (slice(None), columns)]

        if len(free) <= 2:
            for k in range(1 << len(free)):
                one(k)
        else:
            lax.fori_loop(0, 1 << len(free), lambda k, c: (one(k), c)[1], 0)

    def launch(self):
        self.core.start()

    def advance(self, k):
        if k == 0:
            self.core.wait_recv()
            self.add([], self.come, self.come_columns)
        else:
            self.copies[k - 1].wait_recv()
            self.add(self.done[k - 1] + [LINKS[self.order[k - 1]][0]], self.recvs[k - 1], self.columns)
        self.copies[k].start()

    def result(self):
        self.copies[-1].wait_recv()
        own = tuple(bit_value(b) for b in self.bits)
        here = (slice(None), self.columns)
        return self.acc[own + here].astype(WIDE) + self.recvs[-1][here].astype(WIDE)

    def drain(self, core=True):
        if core:
            self.core.wait_send()
        for copy in self.copies:
            copy.wait_send()


def run_events(step, events):
    for at in sorted(events):

        @pl.when(step == at)
        def _():
            for action in events[at]:
                action()


def planned(table, pieces, low, high):
    events = {}
    for at, todo in table:
        if low <= at < high:
            events[at] = [functools.partial(pieces[name].advance, k) for name, k in todo]
    return events


FORWARD_PLAN = (
    (0, (
        ("a00", 0), ("a02", 0), ("f5", 0), ("f4", 0), ("a01", 0), ("a00", 1), ("f5", 1),
        ("a02", 1), ("a01", 1), ("a20", 0), ("a00", 2), ("a22", 0), ("a21", 0), ("a02", 2),
        ("a12", 0), ("a11", 0), ("a10", 0), ("a01", 2), ("a20", 1), ("a02", 3), ("a21", 1),
        ("a12", 1), ("a00", 3), ("a01", 3), ("a11", 1), ("a10", 1), ("a22", 1), ("a21", 2),
        ("a20", 2), ("a12", 2), ("a02", 4), ("f2", 0), ("f0", 0), ("a11", 2), ("a10", 2),
        ("a00", 4), ("a01", 4), ("a21", 3), ("a20", 3),
    )),
    (1, (("a10", 3), ("f1", 0),)),
    (2, (("a22", 2), ("a11", 3),)),
    (3, (("f3", 0),)),
    (4, (("a22", 3), ("a20", 4), ("f1", 1), ("a12", 3),)),
    (5, (("a21", 4), ("f0", 1), ("f2", 1), ("f3", 1),)),
    (7, (("a10", 4), ("f1", 2), ("a11", 4),)),
    (8, (("a12", 4), ("f4", 1), ("a22", 4), ("f0", 2),)),
    (10, (("f2", 2), ("f1", 3), ("f3", 2), ("f5", 2),)),
    (11, (("f0", 3),)),
    (13, (("f4", 2), ("f2", 3), ("f3", 3),)),
    (14, (("f1", 4),)),
    (16, (("f0", 4), ("f5", 3),)),
    (18, (("f4", 3),)),
    (21, (("f2", 4),)),
    (22, (("f3", 4),)),
    (29, (("f5", 4),)),
    (30, (("f4", 4),)),
)
FEED_BACK_PLAN = (
    (10, (("three0", 0),)),
    (11, (("three1", 0),)),
    (12, (("one0", 0),)),
    (13, (("two0", 0),)),
    (15, (("two1", 0), ("one1", 0),)),
    (16, (("three0", 1),)),
    (17, (("two0", 1), ("three1", 1),)),
    (18, (("two2", 0),)),
    (19, (("one2", 0), ("one0", 1), ("one1", 1), ("three0", 2),)),
    (21, (("one3", 0),)),
    (22, (("one0", 2),)),
    (23, (("two2", 1), ("two0", 2), ("one1", 2), ("two3", 0),)),
    (24, (("three1", 2),)),
    (25, (("one2", 1), ("two0", 3),)),
    (26, (("one3", 1),)),
    (27, (("two1", 1), ("one0", 3), ("two2", 2),)),
    (28, (("one1", 3), ("two3", 1),)),
    (29, (("one2", 2), ("one3", 2),)),
    (30, (("two2", 3), ("three0", 3),)),
    (31, (("two1", 2), ("two3", 2), ("one2", 3),)),
    (32, (("one3", 3), ("three1", 3),)),
    (33, (("two1", 3),)),
    (34, (("two3", 3),)),
)
ATTEND_BACK_PLAN = (
    (4, (("p0", 0),)),
    (6, (("p1", 0),)),
    (7, (("p2", 0), ("p3", 0),)),
    (8, (("p4", 0),)),
    (9, (("p0", 1),)),
    (10, (("p5", 0), ("p3", 1), ("p4", 1), ("p1", 1), ("p6", 0),)),
    (11, (("p2", 1), ("p0", 2),)),
    (12, (("p4", 2), ("p3", 2), ("p1", 2),)),
    (13, (("p5", 1), ("p6", 1), ("p2", 2), ("p3", 3),)),
    (14, (("p0", 3), ("p1", 3),)),
    (15, (("p6", 2), ("p4", 3), ("p5", 2), ("p2", 3),)),
    (16, (("p6", 3),)),
    (17, (("p5", 3),)),
)


HALF = BLOCK // 2


def causal_pair(a, firsts, seconds, later):
    row = lax.broadcasted_iota(jnp.int32, (HALF, HEADS * HALF), 0)
    col = lax.broadcasted_iota(jnp.int32, (HALF, HEADS * HALF), 1) % HALF
    if later:
        mask = (row >= col).astype(WIDE)
        full, part = dot_nt(a, firsts), dot_nt(a[HALF:], seconds)
        full = [(full[:HALF] * mask).astype(LOW), full[HALF:].astype(LOW)]
    else:
        mask = (col >= row).astype(WIDE)
        full, part = dot_nt(a, seconds), dot_nt(a[:HALF], firsts)
        full = [full[:HALF].astype(LOW), (full[HALF:] * mask).astype(LOW)]
    return jnp.concatenate(full, axis=0), (part * mask).astype(LOW)


def causal_apply(scores, firsts, seconds, later, carried):
    full, part = scores
    if later:
        total = dot_nn(full, firsts) + carried
        return jnp.concatenate([total[:HALF], total[HALF:] + dot_nn(part, seconds)], axis=0)
    total = dot_nn(full, seconds) + carried
    return jnp.concatenate([total[:HALF] + dot_nn(part, firsts), total[HALF:]], axis=0)


def attend_back_step(
    same, queries, keys, values, grad_attended, pre_query, pre_key, prefix, grads, carry, middle,
):
    marks = head_rows()
    width = queries.shape[1]
    for g in groups(width):
        if g.start == width // 2:
            middle()
        q, k, v, ga = queries[:, g], keys[:, g], values[:, g], grad_attended[:, g]
        qs, ks, vs, gs = (
            (split_heads(rows[:HALF], marks), split_heads(rows[HALF:], marks))
            for rows in (q, k, v, ga)
        )
        state = open_state(prefix[0, :, g].astype(WIDE), same)
        grad_state = open_state(carry[:, g], same)
        gq = causal_apply(causal_pair(ga, *vs, True), *ks, True, dot_nt(ga, state))
        gk = causal_apply(causal_pair(v, *gs, False), *qs, False, dot_nt(v, grad_state))
        gv = causal_apply(causal_pair(k, *qs, False), *gs, False, dot_nn(k, grad_state))
        gq = gq * silu_slope(pre_query[:, g].astype(WIDE))
        gk = gk * silu_slope(pre_key[:, g].astype(WIDE))
        for n, grad in enumerate((gq, gk, gv)):
            grads[:, n * width + g.start : n * width + g.stop] = grad.astype(LOW)
        carry[:, g] += pack_state(dot_tn(q, ga), same)


def clip(value, low, high):
    return jnp.minimum(jnp.maximum(value, low), high)


CHUNK = 256
PAIRS = (2, 3, 3, 3)
PAIR_ORDERS = (("xy01", "xy01"), ("xy01", "0xy1"), ("xy01", "xy01"), ("yx01", "xy01"))
THREE_ORDERS = ("0y1", "y01")
THREE_AFTER = 0


def feed_back_blocks():
    pairs, three, at = [], None, 0
    for n, count in enumerate(PAIRS):
        if n == THREE_AFTER:
            three = (at, 8)
            at += 8
        pairs.append((at, count))
        at += count
    return pairs, three, at


class ThreeScatter(Scatter):
    def last_swap(self, sems, out, give, take):
        self.out, self.give, self.take = out, give, take
        cols = self.columns
        self.swap = sems.copy(give.at[:, cols], take.at[:, cols], (SIDE,))

    def advance(self, k):
        if k < len(self.order):
            super().advance(k)
            return
        cols = self.columns
        total = self.result()
        deep = total.shape[0] // 2
        low, high = total[:deep], total[deep:]
        upper = bit_value(SIDE).astype(WIDE)
        self.out[:, cols] = low * (1 - upper) + high * upper
        self.give[:, cols] = low * upper + high * (1 - upper)
        self.swap.start()

    def finish(self):
        self.swap.wait_recv()
        self.out[:, self.columns] += self.take[:, self.columns]
        self.swap.wait_send()


def feed_back_kernel(
    per_seq, bits,
    normed_hbm, grad_one, grad_two, glu, upstream_hbm,
    queries, keys, values, grad_attended, pre_query, pre_key, prefix, totals,
    out_one, out_two, out_three, grads,
    normed, upstream, acc, come1, come2, come3, come4, send, come,
    acc3, come31, come32, come33, send3, take3, last_send, last_come,
    state_out, state_in, carry, part, part3, send_sems, recv_sems, local,
):
    step = pl.program_id(0)
    pairs, three_block, base = feed_back_blocks()
    links = [bit for bit in bits if bit != CORE]
    mine, side = bit_value(CORE), bit_value(SIDE)
    other = 1 - mine
    sems = Sems(send_sems, recv_sems)
    hidden, width = out_one.shape[1], out_three.shape[1]
    recvs = (come1, come2, come3, come4)
    pieces, ends, first = {}, [], 0
    for n, count in enumerate(PAIRS):
        for w, (name, out) in enumerate((("one", out_one), ("two", out_two))):
            begin = w * hidden + first * CHUNK
            span = count * CHUNK
            pieces[f"{name}{n}"] = Scatter(
                sems, links, PAIR_ORDERS[n][w], acc, send.at[n % 2, w], come, recvs,
                slice(begin, begin + span), slice(0, span), slice(begin, begin + span),
            )
            ends.append((pieces[f"{name}{n}"], out, first * CHUNK))
        first += count
    half = width // 2
    threes = []
    for n in range(2):
        cols = slice(n * half, (n + 1) * half)
        piece = ThreeScatter(
            sems, links[:-1], THREE_ORDERS[n], acc3, send3, take3, (come31, come32, come33),
            cols, cols, cols,
        )
        piece.last_swap(sems, out_three, last_send, last_come)
        pieces[f"three{n}"] = piece
        threes.append(piece)
    swap_state = sems.copy(state_out, state_in, (SIDE,))
    load = [
        pltpu.make_async_copy(normed_hbm, normed, local.at[0]),
        pltpu.make_async_copy(upstream_hbm, upstream, local.at[1]),
    ]

    @pl.when(step == 0)
    def _():
        for copy in load:
            copy.start()
        greet(bits, far=False)
        state_out[...] = totals[...].astype(LOW)
        swap_state.start()

    for first_use, copy in ((pairs[0][0], load[0]), (three_block[0], load[1])):

        @pl.when(step == first_use)
        def _():
            copy.wait()

    for n in range(2, len(PAIRS)):

        @pl.when(step == pairs[n][0])
        def _():
            pieces[f"one{n - 2}"].core.wait_send()
            pieces[f"two{n - 2}"].core.wait_send()

    later = planned(FEED_BACK_PLAN, pieces, base, base + 16)
    at_start = {base + (at - base) // 2: todo for at, todo in later.items() if (at - base) % 2 == 0}
    at_middle = {base + (at - base) // 2: todo for at, todo in later.items() if (at - base) % 2}

    @pl.when(step < base)
    def _():
        run_events(step, planned(FEED_BACK_PLAN, pieces, 0, base))

    @pl.when(step >= base)
    def _():
        run_events(step, at_start)

    lead = acc.shape[:-1]
    fill = (slice(None),) * len(lead)

    def weight_chunk(w, rhs, chunk, group, first):
        part[...] = dot_nn(normed[...], rhs[...]).astype(LOW).reshape(part.shape)
        at = pl.ds(pl.multiple_of(chunk * CHUNK, CHUNK), CHUNK)
        send[(group % 2, w) + fill + (at,)] = part[:, other].reshape(lead + (CHUNK,))
        at = pl.ds(pl.multiple_of(w * hidden + (first + chunk) * CHUNK, CHUNK), CHUNK)
        acc[fill + (at,)] = part[:, mine].reshape(lead + (CHUNK,))

    first = 0
    for n, (begin, count) in enumerate(pairs):

        @pl.when((step >= begin) & (step < begin + count))
        def _():
            weight_chunk(0, grad_one, step - begin, n, first)
            weight_chunk(1, grad_two, step - begin, n, first)

        @pl.when(step == begin + count - 1)
        def _():
            pieces[f"one{n}"].launch()
            pieces[f"two{n}"].launch()

        first += count

    begin, count = three_block

    @pl.when((step >= begin) & (step < begin + count))
    def _():
        k = step - begin
        at = tuple((k // (1 << (2 - d))) % 2 for d in range(3))
        part3[...] = dot_nn(glu[...], upstream[...]).astype(LOW).reshape(part3.shape)
        send3[at] = part3[other]
        acc3[at] = part3[mine]

    @pl.when(step == begin + count - 1)
    def _():
        for piece in threes:
            piece.launch()

    @pl.when(step >= base)
    def _():
        at = step - base

        @pl.when(at == 0)
        def _():
            swap_state.wait_recv()

        @pl.when(at % per_seq == 0)
        def _():
            carry[...] = state_in[at // per_seq].astype(WIDE) * (1 - side).astype(WIDE)

        attend_back_step(
            head_square(), queries, keys, values, grad_attended, pre_query, pre_key, prefix,
            grads, carry, lambda: run_events(step, at_middle),
        )

    @pl.when(step == pl.num_programs(0) - 1)
    def _():
        for actions in planned(FEED_BACK_PLAN, pieces, base + 16, 1000).values():
            for action in actions:
                action()
        for piece, out, begin in ends:
            span = piece.columns.stop - piece.columns.start
            out[:, begin : begin + span] = piece.result()
        for n in range(len(PAIRS)):
            for name in ("one", "two"):
                pieces[f"{name}{n}"].drain(core=n + 2 >= len(PAIRS))
        for piece in threes:
            piece.finish()
            piece.drain()
        swap_state.wait_send()


def feed_back(
    seq_count, normed, grad_one, grad_two, glu, upstream, queries, keys, values, grad_attended,
    pre_query, pre_key, prefix, totals,
):
    row_count, width = queries.shape
    hidden = grad_one.shape[1]
    steps = row_count // BLOCK
    per_seq = steps // seq_count
    bits = index_bits()
    pairs, three, base = feed_back_blocks()
    deep = hidden // 8
    slab = width // 32

    def pair_at(i):
        done = sum(clip(i - begin, 0, count) for begin, count in pairs)
        return jnp.minimum(done, sum(PAIRS) - 1)

    def back(i):
        at = clip(i - base, 0, steps - 1)
        return (at // per_seq) * per_seq + per_seq - 1 - at % per_seq

    rows = pl.BlockSpec((BLOCK, width), lambda i: (back(i), 0))
    pair = pl.BlockSpec((row_count, CHUNK), lambda i: (0, pair_at(i)))
    vmem = pl.BlockSpec(memory_space=pltpu.VMEM)
    hbm = pl.BlockSpec(memory_space=pl.ANY)
    low = functools.partial(pltpu.VMEM, dtype=LOW)
    span = max(PAIRS) * CHUNK
    copies = 10 * len(PAIRS) + 2 * 5 + 1
    return pl.pallas_call(
        functools.partial(feed_back_kernel, per_seq, bits),
        grid=(base + steps,),
        in_specs=[
            hbm, pair, pair,
            pl.BlockSpec((deep, row_count), lambda i: (clip(i - three[0], 0, 7), 0)),
            hbm,
        ]
        + [rows] * 6
        + [pl.BlockSpec((1, HD, width), lambda i: (back(i), 0, 0)), vmem],
        out_specs=[vmem] * 3 + [pl.BlockSpec((BLOCK, 3 * width), lambda i: (back(i), 0))],
        out_shape=[
            jax.ShapeDtypeStruct((slab, hidden), WIDE),
            jax.ShapeDtypeStruct((slab, hidden), WIDE),
            jax.ShapeDtypeStruct((hidden // 32, width), WIDE),
            jax.ShapeDtypeStruct((row_count, 3 * width), LOW),
        ],
        scratch_shapes=[
            low((width, row_count)),
            low((row_count, width)),
            low((2, 2, 2, 2, slab, 2 * hidden)),
            low((2, 2, 2, slab, 2 * hidden)),
            low((2, 2, slab, 2 * hidden)),
            low((2, slab, 2 * hidden)),
            low((slab, 2 * hidden)),
            low((2, 2, 2, 2, 2, 2, slab, span)),
            low((2, 2, 2, 2, slab, 2 * hidden)),
            low((2, 2, 2, deep // 2, width)),
            low((2, 2, deep // 2, width)),
            low((2, deep // 2, width)),
            low((deep // 2, width)),
            low((2, 2, 2, deep // 2, width)),
            low((2, 2, 2, deep // 2, width)),
            pltpu.VMEM((hidden // 32, width), WIDE),
            pltpu.VMEM((hidden // 32, width), WIDE),
            low((seq_count, HD, width)),
            low((seq_count, HD, width)),
            pltpu.VMEM((HD, width), WIDE),
            low((8, 2, width // 16, CHUNK)),
            low((2, deep // 2, width)),
            pltpu.SemaphoreType.DMA((copies,)),
            pltpu.SemaphoreType.DMA((copies,)),
            pltpu.SemaphoreType.DMA((2,)),
        ],
        compiler_params=pltpu.CompilerParams(
            dimension_semantics=("arbitrary",),
            vmem_limit_bytes=63 << 20,
            collective_id=2,
            has_side_effects=True,
        ),
        cost_estimate=pl.CostEstimate(
            flops=6 * row_count * width * hidden + 12 * row_count * width * width,
            bytes_accessed=128 << 20,
            transcendentals=0,
        ),
    )(
        normed, grad_one, grad_two, glu, upstream, queries, keys, values, grad_attended,
        pre_query, pre_key, prefix, totals,
    )


WIDE_CHUNK = 512
PARTS = (2, 1, 2, 1, 1, 2, 1)
PART_ORDERS = ("y0x1", "0xy1", "x0y1", "0xy1", "y01x", "yx01", "x0y1")


def attend_weights_kernel(
    bits,
    normed_hbm, mixed_hbm, gated, grads, gain_term, rows_three, rows_gate, weights_hbm, tok,
    grad_residual,
    out, input_grad,
    normed, mixed, weights, acc, come1, come2, come3, come4, send, come, part,
    send_sems, recv_sems, local,
):
    step = pl.program_id(0)
    links = [bit for bit in bits if bit != CORE]
    mine = bit_value(CORE)
    other = 1 - mine
    sems = Sems(send_sems, recv_sems)
    width = tok.shape[1]
    per = width // WIDE_CHUNK
    chunks = 5 * per
    lead = acc.shape[:-1]
    fill = (slice(None),) * len(lead)

    def column(chunk):
        return chunk * WIDE_CHUNK + (128 if chunk >= per else 0)

    pieces, first = {}, 0
    launches = {}
    for n, count in enumerate(PARTS):
        cols = slice(column(first), column(first + count))
        first += count
        pieces[f"p{n}"] = Scatter(
            sems, links, PART_ORDERS[n], acc, send, come, (come1, come2, come3, come4), cols,
            cols, cols,
        )
        launches[first - 1] = [pieces[f"p{n}"].launch]
    load = [
        pltpu.make_async_copy(mixed_hbm, mixed, local.at[0]),
        pltpu.make_async_copy(normed_hbm, normed, local.at[1]),
        pltpu.make_async_copy(weights_hbm.at[:, : 4 * width], weights, local.at[2]),
    ]

    @pl.when(step == 0)
    def _():
        for copy in load:
            copy.start()
        greet(bits, far=False)
        load[0].wait()

    @pl.when(step == per)
    def _():
        load[1].wait()

    @pl.when(step == chunks)
    def _():
        load[2].wait()

    run_events(step, planned(ATTEND_BACK_PLAN, pieces, 0, chunks + 8))

    def chunk_phase(begin, end, lhs, rhs, shift):
        @pl.when((step >= begin) & (step < end))
        def _():
            at = pl.ds(pl.multiple_of(step * WIDE_CHUNK + shift, 128), WIDE_CHUNK)
            part[...] = dot_nn(lhs[...], rhs[...]).astype(LOW).reshape(part.shape)
            send[fill + (at,)] = part[:, other].reshape(lead + (WIDE_CHUNK,))
            acc[fill + (at,)] = part[:, mine].reshape(lead + (WIDE_CHUNK,))

    chunk_phase(0, per, mixed, gated, 0)
    chunk_phase(per, 2 * per, normed, gated, 128)
    chunk_phase(2 * per, chunks, normed, grads, 128)

    @pl.when(step == 0)
    def _():
        column = jnp.broadcast_to(gain_term[...], (128, width)).T
        column = column.reshape(8, 2, width // 16, 128)
        upper = mine.astype(WIDE)
        low, high = column[:, 0], column[:, 1]
        at = fill + (slice(width, width + 128),)
        acc[at] = (low * (1 - upper) + high * upper).astype(LOW).reshape(lead + (128,))
        send[at] = (low * upper + high * (1 - upper)).astype(LOW).reshape(lead + (128,))

    run_events(step, launches)

    @pl.when(step >= chunks)
    def _():
        def weight(n):
            return weights[:, n * width : (n + 1) * width]

        def row(n):
            return rows_three[:, n * width : (n + 1) * width]

        grad = dot_nt(row(0), weight(2)) + dot_nt(row(1), weight(0))
        grad += dot_nt(row(2), weight(1)) + dot_nt(rows_gate[...], weight(3))
        x = tok[...].astype(WIDE)
        grad = grad_residual[...] + norm_back(x, rms_scale(x), grad)
        input_grad[...] = grad.astype(input_grad.dtype)

    @pl.when(step == pl.num_programs(0) - 1)
    def _():
        for actions in planned(ATTEND_BACK_PLAN, pieces, chunks + 8, 1000).values():
            for action in actions:
                action()
        for piece in pieces.values():
            out[:, piece.columns] = piece.result()
        for piece in pieces.values():
            piece.drain()


def attend_weights(normed, mixed, gated, grads, gain_term, full_attn, tok, grad_residual):
    row_count, width = tok.shape
    steps = row_count // BLOCK
    bits = index_bits()
    per = width // WIDE_CHUNK
    chunks = 5 * per
    slab = width // 32
    vmem = pl.BlockSpec(memory_space=pltpu.VMEM)
    hbm = pl.BlockSpec(memory_space=pl.ANY)

    def rows(size, column=0):
        return pl.BlockSpec((BLOCK, size), lambda i: (clip(i - chunks, 0, steps - 1), column))

    def chunk(begin, count):
        return pl.BlockSpec(
            (row_count, WIDE_CHUNK), lambda i: (0, clip(i - begin, 0, count - 1))
        )

    low = functools.partial(pltpu.VMEM, dtype=LOW)
    columns = 5 * width + 128
    copies = 5 * len(PARTS)
    return pl.pallas_call(
        functools.partial(attend_weights_kernel, bits),
        grid=(chunks + steps,),
        in_specs=[hbm, hbm, chunk(0, 2 * per), chunk(2 * per, 3 * per), vmem, rows(3 * width),
                  rows(width, 1), hbm, rows(width), rows(width)],
        out_specs=[vmem, rows(width)],
        out_shape=[
            jax.ShapeDtypeStruct((slab, columns), WIDE),
            jax.ShapeDtypeStruct((row_count, width), LOW),
        ],
        scratch_shapes=[
            low((width, row_count)),
            low((width, row_count)),
            low((width, 4 * width)),
            low((2, 2, 2, 2, slab, columns)),
            low((2, 2, 2, slab, columns)),
            low((2, 2, slab, columns)),
            low((2, slab, columns)),
            low((slab, columns)),
            low((2, 2, 2, 2, slab, columns)),
            low((2, 2, 2, 2, slab, columns)),
            low((8, 2, width // 16, WIDE_CHUNK)),
            pltpu.SemaphoreType.DMA((copies,)),
            pltpu.SemaphoreType.DMA((copies,)),
            pltpu.SemaphoreType.DMA((3,)),
        ],
        compiler_params=pltpu.CompilerParams(
            dimension_semantics=("arbitrary",),
            vmem_limit_bytes=62 << 20,
            collective_id=3,
            has_side_effects=True,
        ),
        cost_estimate=pl.CostEstimate(
            flops=18 * row_count * width * width, bytes_accessed=64 << 20, transcendentals=0
        ),
    )(normed, mixed, gated, grads, gain_term, grads, gated, full_attn, tok, grad_residual)


ATTEND_PIECES = (
    (("a00", "10xy", 7), ("a01", "10yx", 6), ("a02", "10yx", 3)),
    (("a10", "10xy", 8), ("a11", "10yx", 5), ("a12", "1y0x", 3)),
    (("a20", "1x0y", 3), ("a21", "10yx", 4), ("a22", "10xy", 2)),
)
FEED_PIECES = (
    (("f0", "10yx", 11), ("f1", "10xy", 11)),
    (("f2", "10xy", 13), ("f3", "1y0x", 9)),
)
THREE_PIECES = (("f4", "10y", 4), ("f5", "y10", 4))
FORWARD_COPIES = 128


class ThreeGather(Gather):
    def first_swap(self, sems, columns, give, take, slab, target, local):
        self.cols, self.give, self.take, self.slab = columns, give, take, slab
        self.swap = sems.copy(give.at[:, columns], take.at[:, columns], (SIDE,))
        self.place = pltpu.make_async_copy(slab.at[:, columns], target.at[:, columns], local)

    def advance(self, k):
        if k == 0:
            self.swap.start()
            return
        if k == 1:
            self.swap.wait_recv()
            upper = bit_value(SIDE).astype(WIDE)
            mine, theirs = self.give[:, self.cols], self.take[:, self.cols]
            low = mine * (1 - upper) + theirs * upper
            high = mine * upper + theirs * (1 - upper)
            self.slab[:, self.cols] = jnp.concatenate([low, high], axis=0).astype(LOW)
            self.place.start()
            self.place.wait()
        super().advance(k - 1)

    def drain(self):
        super().drain()
        self.swap.wait_send()


def forward_kernel(
    steps, per_seq, bits,
    tok, s_key, s_value, s_query, s_gate, s_out, s_gain, s_one, s_two, s_three,
    normed, pre_key, keys, values, pre_query, queries, pre_gate, attended, mixed, residual,
    normed_two, up_one, up_two, prefix, gain_row, full_attn, full_one, full_two, full_three,
    held, held_one, held_two, all_keys, all_values, all_normed, totals, state_out, state_in, carry,
    three_out, three_in, three_slab, send, recv, local,
):
    step = pl.program_id(0)
    width = tok.shape[1]
    sems = Sems(send, recv)
    own = tuple(bit_value(bit) for bit in bits)
    side = bit_value(SIDE).astype(WIDE)
    pieces, waves, start = {}, [], 0
    for wave in ATTEND_PIECES:
        waves.append([])
        for name, order, tiles in wave:
            cols = slice(start, start + 128 * tiles)
            start += 128 * tiles
            pieces[name] = Gather(held, bits, order, sems, cols)
            waves[-1].append(pieces[name])
    feed = []
    for buf, parts in zip((held_one, held_two), FEED_PIECES):
        feed.append([])
        start = 0
        for name, order, tiles in parts:
            cols = slice(start, start + 128 * tiles)
            start += 128 * tiles
            pieces[name] = Gather(buf, bits, order, sems, cols)
            feed[-1].append(pieces[name])
    start, threes = 0, []
    for n, (name, order, tiles) in enumerate(THREE_PIECES):
        cols = slice(start, start + 128 * tiles)
        start += 128 * tiles
        pieces[name] = ThreeGather(full_three, bits[:-1], order, sems, cols)
        pieces[name].first_swap(
            sems, cols, three_out, three_in, three_slab, full_three.at[own[:-1]], local.at[2 + n]
        )
        threes.append(pieces[name])
    swap_state = sems.copy(state_out, state_in, (SIDE,))
    keep_attn = pltpu.make_async_copy(held, full_attn, local.at[4])
    keep_feed = [
        pltpu.make_async_copy(held_one, full_one, local.at[0]),
        pltpu.make_async_copy(held_two, full_two, local.at[1]),
    ]

    @pl.when(step == 0)
    def _():
        place = [
            pltpu.make_async_copy(s_one, held_one.at[own], local.at[0]),
            pltpu.make_async_copy(s_two, held_two.at[own], local.at[1]),
        ]
        for copy in place:
            copy.start()
        for n, shard in enumerate((s_key, s_value, s_query, s_gate, s_out)):
            held[own + (slice(None), slice(n * width, (n + 1) * width))] = shard[...]
        size = s_gain.shape[1]
        row = lax.broadcasted_iota(jnp.int32, (size, size), 0)
        col = lax.broadcasted_iota(jnp.int32, (size, size), 1)
        spread = jnp.broadcast_to(s_gain[...].astype(WIDE), (size, size))
        column = jnp.sum(jnp.where(row == col, spread, 0.0), axis=1, keepdims=True)
        column = jnp.broadcast_to(column, (size, 128)).astype(LOW)
        held[own + (slice(None), slice(5 * width, 5 * width + 128))] = column
        three_out[...] = s_three[...].astype(WIDE)
        greet(bits)
        for copy in place:
            copy.wait()
        for actions in planned(FORWARD_PLAN, pieces, 0, 1).values():
            for action in actions:
                action()
        for piece in waves[0]:
            piece.finish()

    @pl.when(step == steps)
    def _():
        for wave in waves[1:]:
            for piece in wave:
                piece.finish()
        keep_attn.start()
        column = held[..., 5 * width : 5 * width + 128].reshape(width, 128)
        gain_row[...] = column.astype(WIDE).T[:1]

    for n in range(4):

        @pl.when((step >= n * steps) & (step < (n + 1) * steps))
        def _():
            part = planned(FORWARD_PLAN, pieces, n * steps + 1, (n + 1) * steps + 1)
            run_events(step + 1, part)

    for n in range(2):

        @pl.when(step == (2 + n) * steps)
        def _():
            for piece in feed[n]:
                piece.finish()
            keep_feed[n].start()

    def weight(n):
        return held[..., n * width : (n + 1) * width].reshape(width, width)

    same = head_square()

    @pl.when(step < steps)
    def _():
        x = tok[...].astype(WIDE)
        rows = (x * rms_scale(x)).astype(LOW)
        normed[...] = rows.T
        here = pl.ds(pl.multiple_of(step * BLOCK, BLOCK), BLOCK)
        all_normed[here, :] = rows
        pre = dot_nn(rows, weight(0))
        pre_key[...] = pre.astype(LOW)
        k = jax.nn.silu(pre).astype(LOW)
        keys[...] = k
        all_keys[here, :] = k
        v = dot_nn(rows, weight(1)).astype(LOW)
        values[...] = v
        all_values[here, :] = v
        seq = step // per_seq

        @pl.when(step % per_seq == 0)
        def _():
            totals[seq] = jnp.zeros((HD, width), WIDE)

        for g in groups(width):
            totals[seq, :, g] += pack_state(dot_tn(k[:, g], v[:, g]), same)

    @pl.when(step == steps - 1)
    def _():
        state_out[...] = totals[...].astype(LOW)
        swap_state.start()

    @pl.when((step >= steps) & (step < 2 * steps))
    def _():
        at = step - steps
        here = pl.ds(pl.multiple_of(at * BLOCK, BLOCK), BLOCK)
        rows = all_normed[here, :]
        pre = dot_nn(rows, weight(2))
        pre_query[...] = pre.astype(LOW)
        queries[...] = jax.nn.silu(pre).astype(LOW)
        gate = dot_nn(rows, weight(3))
        pre_gate[...] = gate.astype(LOW)

        @pl.when(at == 0)
        def _():
            swap_state.wait_recv()

        @pl.when(at % per_seq == 0)
        def _():
            carry[...] = state_in[at // per_seq].astype(WIDE) * side

        marks = head_rows()
        prefix[0] = carry[...].astype(LOW)
        for g in groups(width):
            q, k, v = queries[:, g], all_keys[here, g], all_values[here, g]
            ks, vs = (
                (split_heads(part[:HALF], marks), split_heads(part[HALF:], marks))
                for part in (k, v)
            )
            carried = dot_nn(q, open_state(carry[:, g], same))
            out = causal_apply(causal_pair(q, *ks, True), *vs, True, carried)
            attended[:, g] = out.astype(LOW)
            carry[:, g] += pack_state(dot_tn(k, v), same)
        rows = attended[...].astype(WIDE)
        rows = rows * rms_scale(rows) * gain_row[...] * jax.nn.sigmoid(gate)
        rows = rows.astype(LOW)
        mixed[...] = rows.T
        res = tok[...].astype(WIDE) + dot_nn(rows, weight(4))
        residual[...] = res
        rows = (res * rms_scale(res)).astype(LOW)
        all_normed[here, :] = rows
        normed_two[...] = rows.T

    for n, (weights, result) in enumerate(((held_one, up_one), (held_two, up_two))):

        @pl.when((step >= (2 + n) * steps) & (step < (3 + n) * steps))
        def _():
            at = step - (2 + n) * steps
            rows = all_normed[pl.ds(pl.multiple_of(at * BLOCK, BLOCK), BLOCK), :]
            for c in groups(result.shape[1]):
                result[:, c] = dot_nn(rows, weights[..., c].reshape(width, GROUP)).astype(LOW)

    @pl.when(step == 4 * steps - 1)
    def _():
        for actions in planned(FORWARD_PLAN, pieces, 4 * steps + 1, 1000).values():
            for action in actions:
                action()
        for piece in threes:
            piece.finish()
        for piece in pieces.values():
            piece.drain()
        swap_state.wait_send()
        keep_attn.wait()
        for copy in keep_feed:
            copy.wait()


def forward(tok, seq_count, shards_attn, gain_row, s_one, s_two, s_three):
    row_count, width = tok.shape
    hidden = s_one.shape[1]
    steps = row_count // BLOCK
    per_seq = steps // seq_count
    bits = index_bits()
    lead = (2,) * len(bits)
    slab = s_one.shape[0]
    deep = s_three.shape[0]
    columns = 5 * width + 128

    def phase(n):
        return lambda i: clip(i - n * steps, 0, steps - 1)

    in_rows = rows_spec(width, order=lambda i: jnp.where(i < steps, i, phase(1)(i)))
    first, second = rows_spec(width, order=phase(0)), rows_spec(width, order=phase(1))
    first_turned = pl.BlockSpec((width, BLOCK), lambda i: (0, phase(0)(i)))
    second_turned = pl.BlockSpec((width, BLOCK), lambda i: (0, phase(1)(i)))
    third, fourth = rows_spec(hidden, order=phase(2)), rows_spec(hidden, order=phase(3))
    big_low = jax.ShapeDtypeStruct((row_count, hidden), LOW)
    any_spec = pl.BlockSpec(memory_space=pl.ANY)
    vmem = pl.BlockSpec(memory_space=pltpu.VMEM)

    def shape(*dims, dtype=LOW):
        return jax.ShapeDtypeStruct(dims, dtype)

    rows_low, turned_low = shape(row_count, width), shape(width, row_count)
    low = functools.partial(pltpu.VMEM, dtype=LOW)
    out = pl.pallas_call(
        functools.partial(forward_kernel, steps, per_seq, bits),
        grid=(4 * steps,),
        in_specs=[in_rows] + [vmem] * 6 + [any_spec] * 2 + [vmem],
        out_specs=[first_turned] + [first] * 3 + [second] * 4 + [second_turned, second]
        + [second_turned, third, fourth]
        + [
            pl.BlockSpec((1, HD, width), lambda i: (phase(1)(i), 0, 0)),
            pl.BlockSpec((1, width), lambda i: (0, 0)),
        ]
        + [any_spec] * 4,
        out_shape=[turned_low] + [rows_low] * 7 + [turned_low]
        + [
            shape(row_count, width, dtype=WIDE),
            turned_low, big_low, big_low,
            shape(steps, HD, width),
            shape(1, width, dtype=WIDE),
            shape(*lead, slab, columns),
            shape(*lead, slab, hidden),
            shape(*lead, slab, hidden),
            shape(*lead[:-1], 2 * deep, width),
        ],
        scratch_shapes=[
            low(lead + (slab, columns)),
            low(lead + (slab, hidden)),
            low(lead + (slab, hidden)),
            low((row_count, width)),
            low((row_count, width)),
            low((row_count, width)),
            pltpu.VMEM((seq_count, HD, width), WIDE),
            low((seq_count, HD, width)),
            low((seq_count, HD, width)),
            pltpu.VMEM((HD, width), WIDE),
            pltpu.VMEM((deep, width), WIDE),
            pltpu.VMEM((deep, width), WIDE),
            low((2 * deep, width)),
            pltpu.SemaphoreType.DMA((FORWARD_COPIES,)),
            pltpu.SemaphoreType.DMA((FORWARD_COPIES,)),
            pltpu.SemaphoreType.DMA((5,)),
        ],
        compiler_params=pltpu.CompilerParams(
            dimension_semantics=("arbitrary",),
            vmem_limit_bytes=62 << 20,
            collective_id=1,
            has_side_effects=True,
        ),
        cost_estimate=pl.CostEstimate(
            flops=28 * row_count * width * width, bytes_accessed=128 << 20, transcendentals=0
        ),
    )(tok, *shards_attn, gain_row, s_one, s_two, s_three)
    return list(out[:15]) + [
        out[15].reshape(-1, columns),
        out[16].reshape(-1, hidden),
        out[17].reshape(-1, hidden),
        out[18].reshape(-1, width),
    ]


def plain_shards(
    tokens,
    lengths,
    w_query,
    w_key,
    w_value,
    w_gate,
    out_gain,
    w_out,
    w_one,
    w_two,
    w_three,
    cotangent,
):
    seq_count, local_length, width = tokens.shape
    row_count = seq_count * local_length
    hidden = w_one.shape[1]
    steps = row_count // BLOCK
    per_seq = local_length // BLOCK
    orders = stream_orders()
    tok = tokens.reshape(row_count, width)
    cot = cotangent.reshape(row_count, width)
    full_key = gather_rows(w_key, orders[0])
    full_value = gather_rows(w_value, orders[1])
    full_query = gather_rows(w_query, orders[2])
    full_gate = gather_rows(w_gate, orders[0])
    gain_columns = jnp.broadcast_to(out_gain[:, None], (out_gain.shape[0], 128))
    full_out = gather_rows(jnp.concatenate([w_out, gain_columns], axis=1), orders[1])
    full_one = gather_rows(w_one, orders[2])
    full_two = gather_rows(w_two, orders[0])
    full_three = gather_rows(w_three, orders[1])
    gain = full_out[:, width].astype(WIDE)[None, :]
    full_out = full_out[:, :width]

    rows = rows_spec(width)
    narrow = ((row_count, width), LOW, rows)
    wide = ((row_count, width), WIDE, rows)
    big = ((row_count, hidden), LOW, rows_spec(hidden))
    state_spec = pl.BlockSpec((1, HD, width), lambda i: (i // per_seq, 0, 0))
    state = ((seq_count, HD, width), WIDE, state_spec)
    square = 2 * row_count * width * width

    normed_low, pre_key, keys, values, totals = call(
        lambda *refs: key_value_kernel(per_seq, *refs),
        steps,
        [(tok, rows), (full_key, whole_spec(full_key)), (full_value, whole_spec(full_value))],
        [narrow, narrow, narrow, narrow, state],
        flops=2 * square,
    )
    incoming = shift_sum(totals, "fsdp", False)
    pre_query, queries, pre_gate = call(
        query_gate_kernel,
        steps,
        [(normed_low, rows), (full_query, whole_spec(full_query)), (full_gate, whole_spec(full_gate))],
        [narrow, narrow, narrow],
        flops=2 * square,
    )
    prefix_spec = pl.BlockSpec((1, HD, width), lambda i: (i, 0, 0))
    attended, mixed, residual, prefix = call(
        lambda *refs: attend_kernel(per_seq, *refs),
        steps,
        [(queries, rows), (keys, rows), (values, rows), (pre_gate, rows), (tok, rows),
         (incoming, state_spec), (gain, whole_spec(gain)), (full_out, whole_spec(full_out))],
        [narrow, narrow, wide, ((steps, HD, width), LOW, prefix_spec)],
        scratch=[pltpu.VMEM((HD, width), WIDE)],
        flops=3 * square,
    )
    (
        layer_out, normed_two, glu, grad_up_one, grad_up_two, upstream_low, grad_residual,
        gated, grad_attended, grad_totals, grad_gain_term,
    ) = call(
        lambda *refs: feed_kernel(per_seq, False, *refs),
        steps,
        [(lengths, pl.BlockSpec(memory_space=pltpu.SMEM)), (residual, rows), (cot, rows),
         (full_one, whole_spec(full_one)), (full_two, whole_spec(full_two)),
         (full_three, whole_spec(full_three)), (full_out, whole_spec(full_out)),
         (gain, whole_spec(gain)), (pre_gate, rows), (attended, rows), (queries, rows)],
        [narrow, narrow, big, big, big, narrow, wide,
         ((row_count, 2 * width), LOW, rows_spec(2 * width)), narrow, state,
         ((1, width), WIDE, pl.BlockSpec((1, width), lambda i: (0, 0)))],
        flops=12 * row_count * width * hidden + square,
    )
    grad_residual_low, grad_pre_gate = gated[:, :width], gated[:, width:]
    outgoing = shift_sum(grad_totals, "fsdp", True)
    grad_one = scatter_rows(dot_tn(normed_two, grad_up_one), orders[1])
    grad_two = scatter_rows(dot_tn(normed_two, grad_up_two), orders[2])
    grad_three = scatter_rows(dot_tn(glu, upstream_low), orders[0])
    gain_term = jnp.broadcast_to(grad_gain_term.reshape(width, 1), (width, 128))
    grad_out = scatter_rows(
        jnp.concatenate([dot_tn(mixed, grad_residual_low), gain_term], axis=1), orders[1]
    )
    grad_gain = grad_out[:, width]
    grad_out = grad_out[:, :width]

    def back(i):
        return (i // per_seq) * per_seq + per_seq - 1 - i % per_seq

    back_rows = rows_spec(width, order=back)
    back_narrow = ((row_count, width), LOW, back_rows)
    grad_pre_query, grad_pre_key, grad_pre_value = call(
        lambda *refs: attend_back_kernel(per_seq, *refs),
        steps,
        [(queries, back_rows), (keys, back_rows), (values, back_rows),
         (grad_attended, back_rows), (pre_query, back_rows), (pre_key, back_rows),
         (prefix, pl.BlockSpec((1, HD, width), lambda i: (back(i), 0, 0))),
         (outgoing, state_spec)],
        [back_narrow, back_narrow, back_narrow],
        scratch=[pltpu.VMEM((HD, width), WIDE)],
        flops=6 * square,
    )
    grad_query = scatter_rows(dot_tn(normed_low, grad_pre_query), orders[0])
    grad_key = scatter_rows(dot_tn(normed_low, grad_pre_key), orders[1])
    grad_value = scatter_rows(dot_tn(normed_low, grad_pre_value), orders[2])
    grad_gate = scatter_rows(dot_tn(normed_low, grad_pre_gate), orders[0])
    (input_grad,) = call(
        input_kernel,
        steps,
        [(grad_pre_query, rows), (grad_pre_key, rows), (grad_pre_value, rows),
         (grad_pre_gate, rows), (full_query, whole_spec(full_query)),
         (full_key, whole_spec(full_key)), (full_value, whole_spec(full_value)),
         (full_gate, whole_spec(full_gate)), (tok, rows), (grad_residual, rows)],
        [wide],
        flops=4 * square,
    )
    return (
        layer_out.reshape(tokens.shape),
        input_grad.reshape(tokens.shape),
        grad_query,
        grad_key,
        grad_value,
        grad_gate,
        grad_gain,
        grad_out,
        grad_one,
        grad_two,
        grad_three,
    )


def feed_step_kernel(
    steps, per_seq, lengths, residual, cotangent, up_one, up_two, all_one, all_two, all_three,
    all_attn, gain, pre_gate, attended, queries,
    layer_out, glu, grad_one, grad_two, upstream_low, grad_residual, gated, grad_attended,
    totals, grad_gain, product, last_back, last_residual, last_upstream,
    w_one, w_two, w_three, w_out, local,
):
    step = pl.program_id(0)
    row_count, width = residual.shape

    hidden = w_one.shape[1]
    loads = {}
    for n, part in enumerate((slice(0, 768), slice(768, 1792), slice(1792, hidden))):
        loads[part.start] = pltpu.make_async_copy(
            all_three.at[part], w_three.at[part], local.at[n]
        )
    later = [
        pltpu.make_async_copy(all_one, w_one, local.at[3]),
        pltpu.make_async_copy(all_two, w_two, local.at[4]),
        pltpu.make_async_copy(all_attn.at[:, 4 * width : 5 * width], w_out, local.at[5]),
    ]

    def norm_part(rows):
        res = last_residual[rows, :]
        grad = last_upstream[rows, :].astype(WIDE)
        grad += norm_back(res, rms_scale(res), last_back[rows, :])
        grad_residual[rows, :] = grad
        gated[rows, :width] = grad.astype(LOW)

    def out_part():
        last_back[...] = dot_nt(gated[:, :width], w_out[...])
        grad_gain[...] = jnp.where(step == 1, 0.0, grad_gain[...])

    def gate_part(rows):
        grad = last_back[rows, :]
        gate = jax.nn.sigmoid(pre_gate[rows, :].astype(WIDE))
        att = attended[rows, :].astype(WIDE)
        scale = rms_scale(att)
        hat = att * scale
        grad = grad * gate
        grad_gain[...] += jnp.sum(grad * hat, axis=0, keepdims=True)
        grad = grad * gain[...]
        gated[rows, width:] = (grad * hat * (1.0 - gate)).astype(LOW)
        grad_attended[rows, :] = norm_back(att, scale, grad).astype(LOW)

    def state_part():
        fresh = (step - 1) % per_seq == 0
        same = head_square()
        for g in groups(width):
            term = pack_state(dot_tn(queries[:, g], grad_attended[:, g]), same)
            totals[0, :, g] = jnp.where(fresh, 0.0, totals[0, :, g]) + term

    def cut(count, n):
        size = row_count // count
        return slice(n * size, (n + 1) * size)

    tail = [functools.partial(norm_part, cut(2, n)) for n in range(2)] + [out_part]
    tail += [functools.partial(gate_part, cut(8, n)) for n in range(8)] + [state_part]

    def begin(todo, loading=False):
        spot = lax.broadcasted_iota(jnp.int32, (row_count, 1), 0) + (step % per_seq) * row_count
        limit = lengths[step // per_seq] - lax.axis_index("fsdp") * per_seq * row_count
        valid = (spot < limit).astype(WIDE)
        up_low = (cotangent[...].astype(WIDE) * valid).astype(LOW)
        upstream_low[...] = up_low
        todo = list(todo)
        for c in groups(hidden):
            if loading and c.start in loads:
                loads[c.start].wait()
            back = dot_nt(up_low, w_three[c, :])
            if todo:
                todo.pop(0)()
            one, two = up_one[:, c].astype(WIDE), up_two[:, c].astype(WIDE)
            both = (one * two).astype(LOW)
            product[:, c] = both
            glu[c, :] = both.T
            grad_one[:, c] = (back * two).astype(LOW)
            grad_two[:, c] = (back * one).astype(LOW)
        for part in todo:
            part()
        res = residual[...]
        layer_out[...] = (valid * (res + dot_nn(product[...], w_three[...]))).astype(LOW)
        if loading:
            for copy in later:
                copy.wait()
        back = dot_nt(grad_one[...], w_one[...]) + dot_nt(grad_two[...], w_two[...])
        last_back[...] = back
        last_residual[...] = res
        last_upstream[...] = up_low

    @pl.when(step == 0)
    def _():
        for copy in list(loads.values()) + later:
            copy.start()
        begin([], loading=True)

    @pl.when((step > 0) & (step < steps))
    def _():
        begin(tail)

    @pl.when(step == steps)
    def _():
        for part in tail:
            part()


def feed(
    seq_count, lengths, residual, cot, up_one, up_two, full_one, full_two, full_three, full_attn,
    gain, pre_gate, attended, queries,
):
    row_count, width = residual.shape
    hidden = full_one.shape[1]
    steps = row_count // BLOCK
    per_seq = steps // seq_count

    def now(i):
        return jnp.minimum(i, steps - 1)

    def last(i):
        return jnp.maximum(i - 1, 0)

    rows = rows_spec(width, order=now)
    done = rows_spec(width, order=last)
    narrow = ((row_count, width), LOW, rows)
    big = ((row_count, hidden), LOW, rows_spec(hidden, order=now))

    turned = (
        (hidden, row_count), LOW, pl.BlockSpec((hidden, BLOCK), lambda i: (0, now(i)))
    )
    state_spec = pl.BlockSpec((1, HD, width), lambda i: (last(i) // per_seq, 0, 0))
    hbm = pl.BlockSpec(memory_space=pl.ANY)
    return call(
        lambda *refs: feed_step_kernel(steps, per_seq, *refs),
        steps + 1,
        [(lengths, pl.BlockSpec(memory_space=pltpu.SMEM)), (residual, rows), (cot, rows),
         (up_one, big[2]), (up_two, big[2]),
         (full_one, hbm), (full_two, hbm), (full_three, hbm), (full_attn, hbm),
         (gain, whole_spec(gain)), (pre_gate, done), (attended, done), (queries, done)],
        [narrow, turned, big, big, narrow,
         ((row_count, width), WIDE, done),
         ((row_count, 2 * width), LOW, rows_spec(2 * width, order=last)),
         ((row_count, width), LOW, done),
         ((seq_count, HD, width), WIDE, state_spec),
         ((1, width), WIDE, pl.BlockSpec((1, width), lambda i: (0, 0)))],
        scratch=[pltpu.VMEM((BLOCK, hidden), LOW), pltpu.VMEM((BLOCK, width), WIDE),
                 pltpu.VMEM((BLOCK, width), WIDE), pltpu.VMEM((BLOCK, width), LOW),
                 pltpu.VMEM((width, hidden), LOW), pltpu.VMEM((width, hidden), LOW),
                 pltpu.VMEM((hidden, width), LOW), pltpu.VMEM((width, width), LOW),
                 pltpu.SemaphoreType.DMA((6,))],
        flops=8 * row_count * width * hidden + 2 * row_count * width * width,
        limit=60,
    )


def fused_shards(
    tokens,
    lengths,
    w_query,
    w_key,
    w_value,
    w_gate,
    out_gain,
    w_out,
    w_one,
    w_two,
    w_three,
    cotangent,
):
    seq_count, local_length, width = tokens.shape
    row_count = seq_count * local_length
    tok = tokens.reshape(row_count, width)
    cot = cotangent.reshape(row_count, width)
    (
        normed_low, pre_key, keys, values, pre_query, queries, pre_gate, attended, mixed,
        residual, normed_two, up_one, up_two, prefix, gain, full_attn, full_one, full_two,
        full_three,
    ) = forward(
        tok, seq_count, (w_key, w_value, w_query, w_gate, w_out), out_gain[None, :], w_one, w_two, w_three
    )

    (
        layer_out, glu, grad_up_one, grad_up_two, upstream_low, grad_residual, gated,
        grad_attended, grad_totals, grad_gain_term,
    ) = feed(
        seq_count, lengths, residual, cot, up_one, up_two, full_one, full_two, full_three,
        full_attn, gain, pre_gate, attended, queries,
    )
    grad_one, grad_two, grad_three, grad_three_pre = feed_back(
        seq_count, normed_two, grad_up_one, grad_up_two, glu, upstream_low, queries, keys, values,
        grad_attended, pre_query, pre_key, prefix, grad_totals,
    )
    grads, input_grad = attend_weights(
        normed_low, mixed, gated, grad_three_pre, grad_gain_term, full_attn, tok, grad_residual
    )
    grad_out, grad_gain = grads[:, :width], grads[:, width]
    grad_gate, grad_query, grad_key, grad_value = (
        grads[:, 128 + n * width : 128 + (n + 1) * width] for n in range(1, 5)
    )
    return (
        layer_out.reshape(tokens.shape),
        input_grad.astype(WIDE).reshape(tokens.shape),
        grad_query,
        grad_key,
        grad_value,
        grad_gate,
        grad_gain,
        grad_out,
        grad_one,
        grad_two,
        grad_three,
    )


def shards(*arrays):
    tokens, w_query, w_three = arrays[0], arrays[2], arrays[10]
    sizes = (lax.axis_size("dp"), lax.axis_size("fsdp"))
    fits = w_query.shape[0] % 16 == 0 and w_three.shape[0] % 8 == 0 and tokens.shape[1] >= 4 * BLOCK
    if sizes == (16, 2) and fits:
        return fused_shards(*arrays)
    return plain_shards(*arrays)


def solution(mesh):
    in_specs = (
        P("dp", "fsdp", None),
        P("dp"),
        P(("dp", "fsdp"), None),
        P(("dp", "fsdp"), None),
        P(("dp", "fsdp"), None),
        P(("dp", "fsdp"), None),
        P(("dp", "fsdp")),
        P(("dp", "fsdp"), None),
        P(("dp", "fsdp"), None),
        P(("dp", "fsdp"), None),
        P(("dp", "fsdp"), None),
        P("dp", "fsdp", None),
    )
    out_specs = (
        P("dp", "fsdp", None),
        P("dp", "fsdp", None),
        P(("dp", "fsdp"), None),
        P(("dp", "fsdp"), None),
        P(("dp", "fsdp"), None),
        P(("dp", "fsdp"), None),
        P(("dp", "fsdp")),
        P(("dp", "fsdp"), None),
        P(("dp", "fsdp"), None),
        P(("dp", "fsdp"), None),
        P(("dp", "fsdp"), None),
    )
    return jax.shard_map(shards, mesh=mesh, in_specs=in_specs, out_specs=out_specs, check_vma=False)
```
